32 devices in a mesh: dp: 16 (over z, y, core), tensor: 2 (over x).
Axes of the slice: x: 2, y: 2, z: 4, core: 2. Of those that a mesh axis runs over, the one named last changes fastest.
Arguments:
- hidden: bfloat16 [8192, 2048], P('dp'), may hold values from -6 to 6
- segment_ids: int32 [8192], P('dp'), may hold values from 0 to 19, never falling along the last dimension, each value on 1 to 800 neighbouring positions
- cotangent: bfloat16 [8192, 2048], P('dp'), may hold values from -6 to 6
- w_zx: bfloat16 [2, 2048, 4096], P(None, 'dp', 'tensor'), may hold values from -0.125 to 0.125
- w_dt: bfloat16 [2048, 64], P('dp', 'tensor'), may hold values from -0.125 to 0.125
- w_bc: bfloat16 [2048, 256], P('dp'), may hold values from -0.125 to 0.125
- w_out: bfloat16 [4096, 2048], P('tensor', 'dp'), may hold values from -0.09375 to 0.09375
- conv_x: float32 [4, 4096], P(None, 'tensor'), may hold values from -3 to 3
- conv_bias_x: float32 [4096], P('tensor'), may hold values from -3 to 3
- conv_bc: float32 [4, 256], replicated, may hold values from -3 to 3
- conv_bias_bc: float32 [256], replicated, may hold values from -3 to 3
- dt_bias: float32 [64], P('tensor'), may hold values from -9 to -3
- a_log: float32 [64], P('tensor'), may hold values from -1 to 2
- d_skip: float32 [64], P('tensor'), may hold values from 0.5 to 1.5
- pre_gain: float32 [2048], replicated, may hold values from 0.1 to 1.9
- gate_gain: float32 [4096], P('tensor'), may hold values from 0.1 to 1.9
Outputs:
- output: bfloat16 [8192, 2048], P('dp')
- grad_hidden: bfloat16 [8192, 2048], P('dp')
- grad_w_zx: float32 [2, 2048, 4096], P(None, 'dp', 'tensor')
- grad_w_dt: float32 [2048, 64], P('dp', 'tensor')
- grad_w_bc: float32 [2048, 256], P('dp', 'tensor')
- grad_w_out: float32 [4096, 2048], P('tensor', 'dp')
- grad_conv_x: float32 [4, 4096], P(None, 'tensor')
- grad_conv_bias_x: float32 [4096], P('tensor')
- grad_conv_bc: float32 [4, 256], replicated
- grad_conv_bias_bc: float32 [256], replicated
- grad_dt_bias: float32 [64], P('tensor')
- grad_a_log: float32 [64], P('tensor')
- grad_d_skip: float32 [64], P('tensor')
- grad_pre_gain: float32 [2048], replicated
- grad_gate_gain: float32 [4096], P('tensor')
The draws below stay inside these ranges and needn't reach their ends.
Inputs may be any that keep to these rules, and one draw needn't show every extreme that they name: `segment_ids`: never falling along the tokens; each document has 1 to 800 tokens, and one has exactly 800.
All inputs are finite; a program needn't handle non-finite values.
Results may differ from the reference program's by a relative error of at most 0.0096.
Values may be sent and summed in bfloat16 or wider, within the bound.
No kernel may reach another device: no remote copies, remote signals or barrier semaphores. Data moves between devices by JAX's collectives and lax.ppermute only.
A program may use at most 192 MiB of HBM per device.

```python
import math
import jax
import jax.numpy as jnp
import numpy as np
from jax import lax

D = 2048
HEADS = 64
STATE = 128
CONV = 4
SPAN = 256
DOC_MAX = 800
TOK_DEV = 512
INNER = 4096
TOKENS = 8192
DOCS = 20
N_DP = 16


def shard_levels(own_key, dims, split, smallest, largest):
    loudness = 1.0
    for axis_at, parts in split:
        steps = jax.random.uniform(jax.random.fold_in(jax.random.fold_in(own_key, 6), axis_at), (parts,), jnp.float32, smallest / len(split), largest / len(split))
        loudness = loudness * jnp.repeat(jnp.exp(steps), dims[axis_at] // parts).reshape((-1,) + (1,) * (len(dims) - 1 - axis_at))
    return loudness


def length_profile(number_of, total, limit, slope):
    weights = [(1 << 20) // math.isqrt(grade ** slope) + 1 for grade in range(2, number_of + 1)]
    surplus, given = total - limit - (number_of - 1), [1] * (number_of - 1)
    while surplus > 0:
        movable = [i for i in range(number_of - 1) if given[i] < limit]
        pool, budget = sum([weights[i] for i in movable]), surplus
        for i in movable:
            more = min(limit - given[i], max(1, budget * weights[i] // pool), surplus)
            given[i] = given[i] + more
            surplus = surplus - more
    return np.array([limit] + given)


def ragged(key, count, total, most, slope):
    if count == 2:
        one = jax.random.randint(key, (), max(1, total - most), min(most, total - 1) + 1)
        return jnp.stack([one, total - one])
    lengths = jnp.asarray(length_profile(count, total, most, slope), jnp.int32)
    pairs = (count - 1) // 2
    donor, taker = lengths[1:1 + 2 * pairs:2], lengths[2:2 + 2 * pairs:2]
    margin = jnp.minimum(donor - 1, most - taker)
    passed = jax.random.randint(jax.random.fold_in(key, 1), (pairs,), 0, 1 << 20) % (margin + 1)
    lengths = lengths.at[1:1 + 2 * pairs:2].set(donor - passed).at[2:2 + 2 * pairs:2].set(taker + passed)
    return lengths[jax.random.permutation(jax.random.fold_in(key, 2), count)]


def gaussian(rng, extent, scale, most, pieces=(), dtype=jnp.bfloat16):
    drawn = jax.random.normal(rng, extent, jnp.float32) * scale
    if len(pieces) > 0:
        drawn = shard_levels(rng, extent, pieces, -0.22, 0.18) * drawn
    return jnp.clip(drawn, min=-most, max=most).astype(dtype)


def setup_inputs(seed: int = 0) -> dict:
    seeds = jax.random.split(jax.random.key(seed), 17)
    hidden = gaussian(seeds[0], (TOKENS, D), 1.0, 6.0, ((0, 16),))
    segment_ids = jnp.searchsorted(jnp.cumsum(ragged(seeds[1], DOCS, TOKENS, DOC_MAX, 0)), jnp.arange(TOKENS), side="right").astype(jnp.int32)
    cotangent = gaussian(seeds[2], (TOKENS, D), 1.0, 6.0, ((0, 16),))
    w_zx = gaussian(seeds[3], (2, D, INNER), D ** -0.5, 0.125, ((1, 16), (2, 2)))
    w_dt = gaussian(seeds[4], (D, HEADS), D ** -0.5, 0.125, ((0, 16), (1, 2)))
    w_bc = gaussian(seeds[5], (D, 2 * STATE), D ** -0.5, 0.125, ((0, 16),))
    w_out = gaussian(seeds[6], (INNER, D), INNER ** -0.5, 0.09375, ((0, 2), (1, 16)))
    conv_x = gaussian(seeds[7], (CONV, INNER), CONV ** -0.5, 3.0, ((1, 2),), jnp.float32)
    conv_bias_x = gaussian(seeds[8], (INNER,), 0.5, 3.0, ((0, 2),), jnp.float32)
    conv_bc = gaussian(seeds[9], (CONV, 2 * STATE), CONV ** -0.5, 3.0, (), jnp.float32)
    conv_bias_bc = gaussian(seeds[10], (2 * STATE,), 0.5, 3.0, (), jnp.float32)
    dt_bias = jnp.clip(-9.0 + 6.0 * jax.random.uniform(seeds[11], (HEADS,), jnp.float32) ** shard_levels(seeds[11], (HEADS,), ((0, 2),), -0.2, 0.2), -9.0, -3.0)
    a_log = jnp.clip(-1.0 + 3.0 * jax.random.uniform(seeds[12], (HEADS,), jnp.float32) ** shard_levels(seeds[12], (HEADS,), ((0, 2),), -0.2, 0.2), -1.0, 2.0)
    d_skip = jnp.clip(0.5 + 1.0 * jax.random.uniform(seeds[13], (HEADS,), jnp.float32) ** shard_levels(seeds[13], (HEADS,), ((0, 2),), -0.2, 0.2), 0.5, 1.5)
    pre_gain = jnp.clip(1.0 + 0.18 * jax.random.normal(seeds[14], (D,), jnp.float32), 0.1, 1.9)
    gate_gain = jnp.clip(1.0 + 0.18 * jax.random.normal(seeds[15], (INNER,), jnp.float32), 0.1, 1.9)
    return {"hidden": hidden, "segment_ids": segment_ids, "cotangent": cotangent, "w_zx": w_zx, "w_dt": w_dt, "w_bc": w_bc, "w_out": w_out, "conv_x": conv_x, "conv_bias_x": conv_bias_x, "conv_bc": conv_bc, "conv_bias_bc": conv_bias_bc, "dt_bias": dt_bias, "a_log": a_log, "d_skip": d_skip, "pre_gain": pre_gain, "gate_gain": gate_gain}


epsilon = 1e-05
highest = lax.Precision.HIGHEST

@jax.custom_vjp
def low(v):
    return lax.optimization_barrier(v.astype(jnp.bfloat16)).astype(jnp.float32)

@jax.custom_vjp
def low_back(v):
    return v

def low_keep(v):
    return (low(v), None)

def low_pass(kept, grad):
    return (grad,)

def back_keep(v):
    return (v, None)

def back_low(kept, grad):
    return (low(grad),)
low.defvjp(low_keep, low_pass)
low_back.defvjp(back_keep, back_low)

def causal_conv(values, weights, bias, segs):
    width = weights.shape[0]
    length = values.shape[1]
    padded = jnp.pad(values, ((0, 0), (width - 1, 0), (0, 0)))
    pad_segs = jnp.pad(segs, ((0, 0), (width - 1, 0)), constant_values=-1)
    total = jnp.zeros(values.shape, jnp.float32) + bias
    for offset in range(width):
        same = (pad_segs[:, offset:offset + length] == segs).astype(jnp.float32)
        total = total + weights[offset] * padded[:, offset:offset + length] * same[..., None]
    return total

def state_scan(x_act, b_act, c_act, steps, rates, segs):
    groups, length, heads, hsize = x_act.shape
    count = length // SPAN

    def blocks(value):
        return jnp.moveaxis(value.reshape((groups, count, SPAN) + value.shape[2:]), 1, 0)
    causal = jnp.arange(SPAN)[:, None] >= jnp.arange(SPAN)[None, :]

    def one_block(carry, item):
        state, last_seg = carry
        x_blk, b_blk, c_blk, d_blk, s_blk = item
        cums = jnp.cumsum(d_blk * rates, axis=1)
        inner = jnp.einsum('gin,gjn->gij', c_blk, b_blk, precision=highest)
        keep = ((s_blk[:, :, None] == s_blk[:, None, :]) & causal[None])[..., None]
        gaps = cums[:, :, None, :] - cums[:, None, :, :]
        decay = jnp.where(keep, jnp.exp(jnp.where(keep, gaps, 0.0)), 0.0)
        mixing = inner[..., None] * decay * d_blk[:, None, :, :]
        intra = jnp.einsum('gijh,gjhp->gihp', mixing, x_blk, precision=highest)
        enter = jnp.exp(cums) * (s_blk == last_seg[:, None]).astype(jnp.float32)[..., None]
        carried = jnp.einsum('gin,ghnp->gihp', c_blk, state, precision=highest) * enter[..., None]
        tail = jnp.exp(cums[:, -1:, :] - cums) * (s_blk == s_blk[:, -1:]).astype(jnp.float32)[..., None] * d_blk
        fresh = jnp.einsum('gjn,gjhp->ghnp', b_blk, x_blk * tail[..., None], precision=highest)
        passing = jnp.exp(cums[:, -1, :]) * (s_blk[:, -1] == last_seg).astype(jnp.float32)[:, None]
        state = state * passing[:, :, None, None] + fresh
        return ((state, s_blk[:, -1]), intra + carried)
    start = (jnp.zeros((groups, heads, b_act.shape[-1], hsize), jnp.float32), jnp.full((groups,), -1, jnp.int32))
    items = (blocks(x_act), blocks(b_act), blocks(c_act), blocks(steps), blocks(segs))
    final, outs = lax.scan(jax.checkpoint(one_block), start, items)
    return jnp.moveaxis(outs, 0, 1).reshape(x_act.shape)

def gate_mix(x_act, bc_act, gate, dt_raw, dt_bias, a_log, d_skip, segs):
    groups, length, inner = x_act.shape
    heads = dt_raw.shape[-1]
    x_heads = x_act.reshape(groups, length, heads, inner // heads)
    half = bc_act.shape[-1] // 2
    steps = jax.nn.softplus(dt_raw + dt_bias)
    rates = -jnp.exp(a_log)
    mixed = state_scan(x_heads, bc_act[..., :half], bc_act[..., half:], steps, rates, segs)
    mixed = mixed + d_skip[:, None] * x_heads
    return mixed.reshape(groups, length, inner) * jax.nn.silu(gate)

def mixer_block(inputs, segs, w_zx, w_dt, w_bc, w_out, conv_x, conv_bias_x, conv_bc, conv_bias_bc, dt_bias, a_log, d_skip, pre_gain, gate_gain):
    scales = lax.rsqrt(lax.optimization_barrier(jnp.mean(inputs * inputs, -1, keepdims=True)) + epsilon)
    normed = low(inputs * scales * pre_gain)
    proj_zx = low_back(jnp.einsum('gtd,kdi->kgti', normed, w_zx, precision=highest))
    proj_bc = low_back(jnp.einsum('gtd,dn->gtn', normed, w_bc, precision=highest))
    proj_dt = low_back(jnp.einsum('gtd,dh->gth', normed, w_dt, precision=highest))
    x_act = low(jax.nn.silu(causal_conv(proj_zx[1], conv_x, conv_bias_x, segs)))
    bc_act = low(jax.nn.silu(causal_conv(proj_bc, conv_bc, conv_bias_bc, segs)))
    gated = gate_mix(x_act, bc_act, proj_zx[0], proj_dt, dt_bias, a_log, d_skip, segs)
    gate_scale = lax.rsqrt(lax.optimization_barrier(jnp.mean(gated * gated, -1, keepdims=True)) + epsilon)
    normal = low(gated * gate_scale * gate_gain)
    return inputs + jnp.einsum('gti,id->gtd', normal, w_out, precision=highest)

def reference(hidden, segment_ids, cotangent, w_zx, w_dt, w_bc, w_out, conv_x, conv_bias_x, conv_bc, conv_bias_bc, dt_bias, a_log, d_skip, pre_gain, gate_gain):
    weights = tuple((value.astype(jnp.float32) for value in (w_zx, w_dt, w_bc, w_out, conv_x, conv_bias_x, conv_bc, conv_bias_bc, dt_bias, a_log, d_skip, pre_gain, gate_gain)))
    group = math.gcd(N_DP, max(1, 4096 // TOK_DEV))
    rounds = N_DP // group

    def shaped(value):
        return value.reshape((rounds, group, TOK_DEV) + value.shape[1:])

    def one_round(totals, item):
        inputs, segs, cots = item

        def forward(values, *params):
            return mixer_block(values, segs, *params)
        result, pull = jax.vjp(forward, inputs.astype(jnp.float32), *weights)
        grads = pull(cots.astype(jnp.float32))
        totals = tuple((left + right for left, right in zip(totals, grads[1:])))
        return (totals, (result.astype(jnp.bfloat16), grads[0].astype(jnp.bfloat16)))
    zeros = tuple((jnp.zeros_like(value) for value in weights))
    totals, (results, grad_in) = lax.scan(one_round, zeros, (shaped(hidden), shaped(segment_ids), shaped(cotangent)))
    output = results.reshape(TOKENS, D)
    grad_hidden = grad_in.reshape(TOKENS, D)
    return (output, grad_hidden, totals[0], totals[1], totals[2], totals[3], totals[4], totals[5], totals[6], totals[7], totals[8], totals[9], totals[10], totals[11], totals[12])
```

```python
import functools

import jax
import jax.numpy as jnp
import numpy as np
from jax import lax
from jax.experimental import pallas as pl
from jax.experimental.pallas import tpu as pltpu
from jax.sharding import PartitionSpec as P

EPS = 1e-05
Q = 128
NEG = -1e30
F32 = jnp.float32
BF16 = jnp.bfloat16
HIGH = lax.Precision.HIGHEST
VMEM_LIMIT = 56 * 1024 * 1024


def dot(a, b, dims, precision=None):
    return lax.dot_general(a, b, (dims, ((), ())), precision=precision, preferred_element_type=F32)


def params():
    return pltpu.CompilerParams(vmem_limit_bytes=VMEM_LIMIT)


def ring_order(chips):
    if chips == 8:
        return [0, 2, 4, 6, 7, 5, 3, 1]
    half = chips // 2
    return list(range(half)) + list(range(chips - 1, half - 1, -1))


class Ring:
    def __init__(self, n_dp):
        self.n = n_dp // 2
        self.order = ring_order(self.n)
        place = [0] * self.n
        for position, chip in enumerate(self.order):
            place[chip] = position
        me = lax.axis_index("dp")
        self.core = me % 2
        self.pos = jnp.asarray(place, jnp.int32)[me // 2]
        self.right = self.perm(1)
        self.left = self.perm(-1)
        self.full = self.n // 2 - 1

    def perm(self, step):
        pairs = []
        for p in range(self.n):
            for c in range(2):
                pairs.append((self.order[p] * 2 + c, self.order[(p + step) % self.n] * 2 + c))
        return pairs

    def chip(self, step):
        return jnp.asarray(self.order, jnp.int32)[(self.pos + step) % self.n]

    def go_right(self, v):
        return lax.ppermute(v, "dp", self.right)

    def go_left(self, v):
        return lax.ppermute(v, "dp", self.left)

    def swap(self, v):
        return lax.ppermute(v, "dp", [(i, i ^ 1) for i in range(2 * self.n)])

    def chip_sum(self, v):
        dist = 2
        while dist < 2 * self.n:
            v = v + lax.ppermute(v, "dp", [(i, i ^ dist) for i in range(2 * self.n)])
            dist *= 2
        return v


def half_rows(rows):
    return (rows // 2 + 15) // 16 * 16


def ring_gather(ring, unit):
    h = half_rows(unit.shape[0])
    r, l = [unit], [unit]
    for _ in range(ring.full):
        r.append(ring.go_right(r[-1]))
        l.append(ring.go_left(l[-1]))
    top = ring.go_right(r[-1][:h])
    bottom = ring.go_left(l[-1][h:])
    return [unit] + r[1:] + l[1:] + [top, bottom]


def gather_steps(ring):
    return [0] + [-k for k in range(1, ring.full + 1)] + list(range(1, ring.full + 1)) + [ring.n // 2]


def ring_scatter(ring, block, rows):
    h = half_rows(rows)
    far = block(ring.n // 2)
    r = ring.go_right(far[:h].astype(BF16))
    l = ring.go_left(far[h:].astype(BF16))
    for j in range(ring.full, 0, -1):
        br, bl = block(j), block(-j)
        if j == ring.full:
            br = jnp.concatenate([br[:h] + r.astype(F32), br[h:]])
            bl = jnp.concatenate([bl[:h], bl[h:] + l.astype(F32)])
        else:
            br = br + r.astype(F32)
            bl = bl + l.astype(F32)
        r = ring.go_right(br.astype(BF16))
        l = ring.go_left(bl.astype(BF16))
    return block(0) + r.astype(F32) + l.astype(F32)


def proj_kernel(n_blocks, dd, offs, *refs):
    blocks, act, out = refs[:n_blocks], refs[n_blocks], refs[n_blocks + 1]
    pieces, cols = [], []
    for b in range(n_blocks - 2):
        pieces.append(blocks[b][...])
    pieces.append(jnp.concatenate([blocks[-2][...], blocks[-1][...]], axis=0))
    for b in range(n_blocks - 1):
        off = pl.multiple_of(offs[b], dd)
        cols.append(act[:, pl.ds(off, dd)])
    out[...] = dot(
        jnp.concatenate(pieces, axis=1), jnp.concatenate(cols, axis=1), (((1,), (1,)))
    )


def proj(blocks, act, offs):
    rows, dd = blocks[0].shape
    tokens, width = act.shape
    tile = 256
    n = len(blocks)
    specs = [pl.BlockSpec(b.shape, lambda i, o: (0, 0)) for b in blocks]
    return pl.pallas_call(
        functools.partial(proj_kernel, n, dd),
        out_shape=jax.ShapeDtypeStruct((rows, tokens), F32),
        grid_spec=pltpu.PrefetchScalarGridSpec(
            num_scalar_prefetch=1,
            grid=(tokens // tile,),
            in_specs=specs + [pl.BlockSpec((tile, width), lambda i, o: (i, 0))],
            out_specs=pl.BlockSpec((rows, tile), lambda i, o: (0, i)),
        ),
        compiler_params=params(),
        cost_estimate=pl.CostEstimate(
            flops=2 * rows * tokens * width,
            bytes_accessed=2 * rows * width + 2 * tokens * width + 4 * rows * tokens,
            transcendentals=0,
        ),
    )(offs, *blocks, act)


def back_kernel(sizes, dd, offs, *refs):
    out = refs[-1]
    at = 0
    groups = []
    for n_blocks in sizes:
        blocks = refs[at : at + n_blocks]
        vt = refs[at + n_blocks]
        at += n_blocks + 1
        groups.append((blocks, vt[...].T))
    for b in range(sizes[0] - 1):
        off = pl.multiple_of(offs[b], dd)
        total = None
        for blocks, v in groups:
            w = blocks[b][...]
            if b == len(blocks) - 2:
                w = jnp.concatenate([w, blocks[b + 1][...]], axis=0)
            part = dot(v, w, (((1,), (0,))))
            total = part if total is None else total + part
        out[:, pl.ds(off, dd)] = total.astype(out.dtype)


def back(groups, offs, width):
    dd = groups[0][0][0].shape[1]
    tokens = groups[0][1].shape[1]
    tile = 256
    args, specs = [], []
    flops = 0
    for blocks, vt in groups:
        args += list(blocks) + [vt]
        specs += [pl.BlockSpec(b.shape, lambda i, o: (0, 0)) for b in blocks]
        specs += [pl.BlockSpec((vt.shape[0], tile), lambda i, o: (0, i))]
        flops += 2 * vt.shape[0] * tokens * width
    return pl.pallas_call(
        functools.partial(back_kernel, [len(g[0]) for g in groups], dd),
        out_shape=jax.ShapeDtypeStruct((tokens, width), BF16),
        grid_spec=pltpu.PrefetchScalarGridSpec(
            num_scalar_prefetch=1,
            grid=(tokens // tile,),
            in_specs=specs,
            out_specs=pl.BlockSpec((tile, width), lambda i, o: (i, 0)),
        ),
        compiler_params=params(),
        cost_estimate=pl.CostEstimate(
            flops=flops, bytes_accessed=flops // 1024 + 2 * tokens * width, transcendentals=0
        ),
    )(offs, *args)


HEAD = 64
STATE = 128


def head_terms(raw, hp_ref):
    pre = raw + hp_ref[:, 0:1]
    small = jnp.exp(-jnp.abs(pre))
    one = 1.0 + small
    away = one - 1.0
    log1p = jnp.where(away == 0.0, small, jnp.log(one) * (small / jnp.where(away == 0.0, 1.0, away)))
    dt = jnp.maximum(pre, 0.0) + log1p
    logistic = jnp.where(pre >= 0.0, 1.0, small) / one
    rows = lax.broadcasted_iota(jnp.int32, (Q, Q), 0)
    lanes = lax.broadcasted_iota(jnp.int32, (Q, Q), 1)
    upto = (rows <= lanes).astype(F32)
    logs = dt * hp_ref[:, 1:2]
    cums = dot(logs, upto, (((1,), (0,))), HIGH)
    return dt, logistic, cums


def to_columns(cums):
    n = cums.shape[0]
    square = jnp.concatenate([cums, jnp.zeros((Q - n, Q), F32)], axis=0)
    return square.T


def pair_bias(segr_ref, segc_ref):
    rows = lax.broadcasted_iota(jnp.int32, (Q, Q), 0)
    lanes = lax.broadcasted_iota(jnp.int32, (Q, Q), 1)
    keep = (segc_ref[...] == segr_ref[...]) & (rows <= lanes)
    return jnp.where(keep, 0.0, NEG)


def fwd_kernel(
    heads, xr_ref, mask_ref, segr_ref, segc_ref, par_ref, hp_ref,
    y_ref, xa_ref, u_ref, s_ref, prev, state, parb, xt,
):
    first = (pl.program_id(0) == 0) & (pl.program_id(1) == 0)
    chans = heads * HEAD
    wide = chans + 2 * STATE

    @pl.when(first)
    def _():
        for k in range(6):
            parb[k] = jnp.broadcast_to(par_ref[:, k : k + 1], (wide, Q))

    @pl.when(pl.program_id(1) == 0)
    def _():
        prev[...] = jnp.zeros_like(prev)
        state[...] = jnp.zeros_like(state)

    lane = lax.broadcasted_iota(jnp.int32, (HEAD, Q), 1)
    m1, m2, m3 = mask_ref[0:1, :], mask_ref[1:2, :], mask_ref[2:3, :]

    def conv(r0):
        rows = slice(r0, r0 + HEAD)
        cur = xr_ref[rows, :]
        old = prev[rows, :]
        u = parb[4, rows, :] + parb[3, rows, :] * cur
        u = u + parb[2, rows, :] * (m1 * pltpu.roll(jnp.where(lane >= Q - 1, old, cur), 1, 1))
        u = u + parb[1, rows, :] * (m2 * pltpu.roll(jnp.where(lane >= Q - 2, old, cur), 2, 1))
        u = u + parb[0, rows, :] * (m3 * pltpu.roll(jnp.where(lane >= Q - 3, old, cur), 3, 1))
        prev[rows, :] = cur
        u_ref[rows, :] = u
        xa = (u * (0.5 * jnp.tanh(0.5 * u) + 0.5)).astype(BF16)
        xa_ref[rows, :] = xa
        return xa

    for r0 in range(chans, wide, HEAD):
        conv(r0)
    bt = xa_ref[chans : chans + STATE, :]
    ct = xa_ref[chans + STATE : wide, :]
    mix = dot(bt.T, ct, (((1,), (0,))))
    dt, _, cums = head_terms(xr_ref[wide:, :], hp_ref)
    cols = to_columns(cums)
    bias = pair_bias(segr_ref, segc_ref)
    enter = jnp.exp(cums) * mask_ref[3:4, :]
    last = jnp.broadcast_to(cums[:, Q - 1 : Q], cums.shape)
    tail = jnp.exp(last - cums) * mask_ref[4:5, :]
    passing = jnp.exp(last) * mask_ref[5:6, :]
    s_in = state[...].astype(BF16)
    s_ref[...] = s_in
    carried = dot(s_in, ct, (((1,), (0,))))
    for h in range(heads):
        rows = slice(h * HEAD, (h + 1) * HEAD)
        xa = conv(h * HEAD).astype(F32)
        decay = jnp.exp(cums[h : h + 1, :] - cols[:, h : h + 1] + bias)
        mixing = (mix * decay).astype(BF16)
        xd = xa * dt[h : h + 1, :]
        xt[rows, :] = (xd * tail[h : h + 1, :]).astype(BF16)
        y = dot(xd.astype(BF16), mixing, (((1,), (0,))))
        y = y + enter[h : h + 1, :] * carried[rows, :] + parb[5, rows, :] * xa
        y_ref[rows, :] = y
    fresh = dot(xt[...], bt, (((1,), (1,))))
    for h in range(heads):
        rows = slice(h * HEAD, (h + 1) * HEAD)
        state[rows, :] = state[rows, :] * passing[h : h + 1, :] + fresh[rows, :]


def scan_forward(xr, masks, segr, segc, par, hp, heads, seqs):
    rows, tokens = xr.shape
    chans = heads * HEAD
    wide = chans + 2 * STATE
    count = tokens // seqs // Q
    at = lambda s, k: (0, s * count + k)
    whole = lambda s, k: (0, 0)
    return pl.pallas_call(
        functools.partial(fwd_kernel, heads),
        grid=(seqs, count),
        out_shape=(
            jax.ShapeDtypeStruct((chans, tokens), F32),
            jax.ShapeDtypeStruct((wide, tokens), BF16),
            jax.ShapeDtypeStruct((wide, tokens), F32),
            jax.ShapeDtypeStruct((chans, tokens), BF16),
        ),
        in_specs=[
            pl.BlockSpec((rows, Q), at),
            pl.BlockSpec((8, Q), at),
            pl.BlockSpec((1, Q), at),
            pl.BlockSpec((Q, 1), lambda s, k: (s * count + k, 0)),
            pl.BlockSpec(par.shape, whole),
            pl.BlockSpec(hp.shape, whole),
        ],
        out_specs=(
            pl.BlockSpec((chans, Q), at),
            pl.BlockSpec((wide, Q), at),
            pl.BlockSpec((wide, Q), at),
            pl.BlockSpec((chans, STATE), at),
        ),
        scratch_shapes=[
            pltpu.VMEM((wide, Q), F32),
            pltpu.VMEM((chans, STATE), F32),
            pltpu.VMEM((6, wide, Q), F32),
            pltpu.VMEM((chans, Q), BF16),
        ],
        compiler_params=params(),
        cost_estimate=pl.CostEstimate(
            flops=20_000_000_000, bytes_accessed=18 * wide * tokens, transcendentals=0
        ),
    )(xr, masks, segr, segc, par, hp)


def bwd_kernel(
    heads, xr_ref, mask_ref, segr_ref, segc_ref, par_ref, hp_ref, xa_ref, u_ref, s_ref, dy_ref, y_ref,
    dx_ref, dbc_ref, ddt_ref, cg_ref, hg_ref,
    dstate, parb, after, nmask, xt, dye,
):
    first = (pl.program_id(0) == 0) & (pl.program_id(1) == 0)
    chans = heads * HEAD
    wide = chans + 2 * STATE

    @pl.when(first)
    def _():
        for k in range(6):
            parb[k] = jnp.broadcast_to(par_ref[:, k : k + 1], (wide, Q))
        cg_ref[...] = jnp.zeros_like(cg_ref)
        hg_ref[...] = jnp.zeros_like(hg_ref)

    @pl.when(pl.program_id(1) == 0)
    def _():
        dstate[...] = jnp.zeros_like(dstate)
        after[...] = jnp.zeros_like(after)
        nmask[...] = jnp.zeros_like(nmask)

    lane = lax.broadcasted_iota(jnp.int32, (HEAD, Q), 1)
    lane8 = lax.broadcasted_iota(jnp.int32, (8, Q), 1)
    sub8 = lax.broadcasted_iota(jnp.int32, (8, Q), 0)
    masks = mask_ref[...]
    shifted_masks = jnp.where(lane8 <= sub8, nmask[...], masks)
    nmask[...] = masks

    def conv_back(r0, dxa, out, out0):
        rows = slice(r0, r0 + HEAD)
        u = u_ref[rows, :]
        sig = 0.5 * jnp.tanh(0.5 * u) + 0.5
        dc = dxa * (sig * (1.0 + u * (1.0 - sig)))
        xr = xr_ref[rows, :]
        old = after[rows, :]
        after[rows, :] = dc
        dx = parb[3, rows, :] * dc
        cg_ref[4, rows, :] += dc
        cg_ref[3, rows, :] += xr * dc
        for k in (1, 2, 3):
            e = jnp.where(lane < k, old, dc) * shifted_masks[k - 1 : k, :]
            e = pltpu.roll(e, Q - k, 1)
            dx = dx + parb[3 - k, rows, :] * e
            cg_ref[3 - k, rows, :] += xr * e
        out[out0 : out0 + HEAD, :] = dx.astype(out.dtype)

    bt = xa_ref[chans : chans + STATE, :]
    ct = xa_ref[chans + STATE : wide, :]
    mix = dot(bt.T, ct, (((1,), (0,))))
    dt, logistic, cums = head_terms(xr_ref[wide:, :], hp_ref)
    cols = to_columns(cums)
    bias = pair_bias(segr_ref, segc_ref)
    enter = jnp.exp(cums) * masks[3:4, :]
    last = jnp.broadcast_to(cums[:, Q - 1 : Q], cums.shape)
    tail = jnp.exp(last - cums) * masks[4:5, :]
    passing = jnp.exp(last) * masks[5:6, :]
    ds = dstate[...].astype(BF16)
    spread = dot(ds, bt, (((1,), (0,))))
    dmix = jnp.zeros((Q, Q), F32)
    s_in = s_ref[...]
    direct, cross, skip, outward, through, inward = [], [], [], [], [], []
    for h in range(heads):
        rows = slice(h * HEAD, (h + 1) * HEAD)
        xa = xa_ref[rows, :].astype(F32)
        dyb = dy_ref[rows, :]
        dy = dyb.astype(F32)
        decay = jnp.exp(cums[h : h + 1, :] - cols[:, h : h + 1] + bias)
        mixing = (mix * decay).astype(BF16)
        xd = xa * dt[h : h + 1, :]
        xdb = xd.astype(BF16)
        xt[rows, :] = (xd * tail[h : h + 1, :]).astype(BF16)
        dye[rows, :] = (dy * enter[h : h + 1, :]).astype(BF16)
        dmix = dmix + dot(xdb, dyb, (((0,), (0,)))) * decay
        near = dot(dyb, mixing, (((1,), (1,))))
        far = tail[h : h + 1, :] * spread[rows, :]
        pull = near + far
        direct.append(jnp.sum(xa * pull, axis=0, keepdims=True))
        cross.append(jnp.sum(xdb.astype(F32) * near, axis=0, keepdims=True))
        outward.append(jnp.sum(xd * far, axis=0, keepdims=True))
        through.append(jnp.sum(dstate[rows, :] * s_in[rows, :].astype(F32), axis=0, keepdims=True))
        skip.append(jnp.sum(xa * dy, axis=0, keepdims=True))
        inward.append(jnp.sum(y_ref[rows, :] * dy, axis=0, keepdims=True))
        dxa = dt[h : h + 1, :] * pull + parb[5, rows, :] * dy
        conv_back(h * HEAD, dxa, dx_ref, h * HEAD)
    pad = ddt_ref.shape[0] - heads
    if pad:
        zero = [jnp.zeros((pad, Q), F32)]
        direct, cross, skip = direct + zero, cross + zero, skip + zero
        outward, through, inward = outward + zero, through + zero, inward + zero
    direct, cross, skip, outward, through, inward = (
        jnp.concatenate(v, axis=0) for v in (direct, cross, skip, outward, through, inward)
    )
    dlog = inward - hp_ref[:, 2:3] * skip - cross
    rows = lax.broadcasted_iota(jnp.int32, (Q, Q), 0)
    lanes = lax.broadcasted_iota(jnp.int32, (Q, Q), 1)
    dl = dot(dlog, (rows >= lanes).astype(F32), (((1,), (0,))), HIGH)
    dl = dl + dot(outward, (rows < lanes).astype(F32), (((1,), (0,))), HIGH)
    dl = dl + passing * jnp.sum(through, axis=1, keepdims=True)
    ddt = (direct + hp_ref[:, 1:2] * dl) * logistic
    ddt_ref[...] = ddt
    hg_ref[0] += ddt
    hg_ref[1] += dt * dl
    hg_ref[2] += skip
    dmixb = dmix.astype(BF16)
    xtv, dyev = xt[...], dye[...]
    dbt = dot(ct, dmixb, (((1,), (1,)))) + dot(ds, xtv, (((0,), (0,))))
    dct = dot(bt, dmixb, (((1,), (0,)))) + dot(s_ref[...], dyev, (((0,), (0,))))
    dbca = jnp.concatenate([dbt, dct], axis=0)
    for r0 in range(0, 2 * STATE, HEAD):
        conv_back(chans + r0, dbca[r0 : r0 + HEAD, :], dbc_ref, r0)
    fresh = dot(dyev, ct, (((1,), (1,))))
    for h in range(heads):
        rows = slice(h * HEAD, (h + 1) * HEAD)
        dstate[rows, :] = dstate[rows, :] * passing[h : h + 1, :] + fresh[rows, :]


def scan_backward(xr, masks, segr, segc, par, hp, xa, u, s_in, dy, y, heads, seqs):
    rows, tokens = xr.shape
    chans = heads * HEAD
    wide = chans + 2 * STATE
    count = tokens // seqs // Q
    padded = rows - wide
    at = lambda s, k: (0, s * count + count - 1 - k)
    whole = lambda s, k: (0, 0)
    whole3 = lambda s, k: (0, 0, 0)
    return pl.pallas_call(
        functools.partial(bwd_kernel, heads),
        grid=(seqs, count),
        out_shape=(
            jax.ShapeDtypeStruct((chans, tokens), BF16),
            jax.ShapeDtypeStruct((2 * STATE, tokens), F32),
            jax.ShapeDtypeStruct((padded, tokens), F32),
            jax.ShapeDtypeStruct((5, wide, Q), F32),
            jax.ShapeDtypeStruct((3, padded, Q), F32),
        ),
        in_specs=[
            pl.BlockSpec((rows, Q), at),
            pl.BlockSpec((8, Q), at),
            pl.BlockSpec((1, Q), at),
            pl.BlockSpec((Q, 1), lambda s, k: (s * count + count - 1 - k, 0)),
            pl.BlockSpec(par.shape, whole),
            pl.BlockSpec(hp.shape, whole),
            pl.BlockSpec((wide, Q), at),
            pl.BlockSpec((wide, Q), at),
            pl.BlockSpec((chans, STATE), at),
            pl.BlockSpec((chans, Q), at),
            pl.BlockSpec((chans, Q), at),
        ],
        out_specs=(
            pl.BlockSpec((chans, Q), at),
            pl.BlockSpec((2 * STATE, Q), at),
            pl.BlockSpec((padded, Q), at),
            pl.BlockSpec((5, wide, Q), whole3),
            pl.BlockSpec((3, padded, Q), whole3),
        ),
        scratch_shapes=[
            pltpu.VMEM((chans, STATE), F32),
            pltpu.VMEM((6, wide, Q), F32),
            pltpu.VMEM((wide, Q), F32),
            pltpu.VMEM((8, Q), F32),
            pltpu.VMEM((chans, Q), BF16),
            pltpu.VMEM((chans, Q), BF16),
        ],
        compiler_params=params(),
        cost_estimate=pl.CostEstimate(
            flops=40_000_000_000, bytes_accessed=18 * wide * tokens, transcendentals=0
        ),
    )(xr, masks, segr, segc, par, hp, xa, u, s_in, dy, y)


def block_masks(segs, seqs):
    s = segs.reshape(seqs, -1)
    length = s.shape[1]
    rows = []
    for k in (1, 2, 3):
        old = jnp.pad(s, ((0, 0), (k, 0)), constant_values=-1)[:, :length]
        rows.append(old == s)
    b = s.reshape(seqs, length // Q, Q)
    ends = b[:, :, -1:]
    before = jnp.concatenate([jnp.full((seqs, 1, 1), -1, s.dtype), ends[:, :-1]], axis=1)
    rows += [b == before, b == ends, jnp.broadcast_to(ends == before, b.shape)]
    rows = [r.reshape(1, -1).astype(F32) for r in rows]
    return jnp.concatenate(rows + [jnp.zeros((2, segs.shape[0]), F32)], axis=0)


def local(
    hidden, segment_ids, cotangent, w_zx, w_dt, w_bc, w_out, conv_x, conv_bias_x, conv_bc, conv_bias_bc,
    dt_bias, a_log, d_skip, pre_gain, gate_gain,
):
    n_dp, n_t = lax.axis_size("dp"), lax.axis_size("tensor")
    t_index = lax.axis_index("tensor")
    ring = Ring(n_dp)
    core = ring.core
    mine, width = hidden.shape
    rows_dp = w_zx.shape[1]
    inner_here = w_zx.shape[2]
    chans = inner_here // 2
    heads = w_dt.shape[1] // 2
    padded = max(16, heads)
    wide = chans + 2 * STATE
    inner_all = inner_here * n_t

    def tensor_sum(v):
        if n_t == 2:
            return v + lax.ppermute(v, "tensor", [(0, 1), (1, 0)])
        return lax.psum(v, "tensor")

    def pick(v, which, axis=0):
        size = v.shape[axis] // 2
        return lax.dynamic_slice_in_dim(v, which * size, size, axis)

    def in_order(own, other, axis):
        return jnp.where(
            core == 0, jnp.concatenate([own, other], axis), jnp.concatenate([other, own], axis)
        )

    w_xt, w_zt = w_zx[1].T, w_zx[0].T
    w_dtt = jnp.pad(w_dt.T.reshape(2, heads, rows_dp), ((0, 0), (0, padded - heads), (0, 0)))
    w_dtt = w_dtt.reshape(2 * padded, rows_dp)
    w_bct = w_bc.T

    def unit_x(which):
        return jnp.concatenate([pick(w_xt, which), w_bct, pick(w_dtt, which)], axis=0)

    ux = in_order(unit_x(core), ring.swap(unit_x(1 - core)), 1)
    uz = in_order(pick(w_zt, core), ring.swap(pick(w_zt, 1 - core)), 1)
    uo = in_order(pick(w_out, core), ring.swap(pick(w_out, 1 - core)), 1)
    dd = ux.shape[1]
    offs = jnp.stack([ring.chip(s) for s in gather_steps(ring)]).astype(jnp.int32) * dd

    gx = ring_gather(ring, ux)
    gz = ring_gather(ring, uz)
    go = ring_gather(ring, uo)

    inputs = hidden.astype(F32)
    scales = lax.rsqrt(jnp.mean(inputs * inputs, -1, keepdims=True) + EPS)
    normed_own = (inputs * scales * pre_gain).astype(BF16)
    normed = jnp.concatenate([normed_own, ring.swap(normed_own)], axis=0)
    cots = jnp.concatenate([cotangent, ring.swap(cotangent)], axis=0)
    segs = jnp.concatenate([segment_ids, ring.swap(segment_ids)])
    masks = block_masks(segs, 2)
    segr, segc = segs[None, :], segs[:, None]

    def own_chans(v):
        return pick(v, core, v.ndim - 1)

    taps = jnp.concatenate([own_chans(conv_x), conv_bc], axis=1)
    biases = jnp.concatenate([own_chans(conv_bias_x), conv_bias_bc])
    skips = jnp.repeat(own_chans(d_skip), HEAD)
    par = jnp.concatenate(
        [taps, biases[None], jnp.pad(skips, (0, 2 * STATE))[None], jnp.zeros((2, wide), F32)], axis=0
    ).T
    a_own = -jnp.exp(own_chans(a_log))
    hp = jnp.stack([own_chans(dt_bias), a_own, own_chans(d_skip)], axis=1)
    hp = jnp.pad(hp, ((0, padded - heads), (0, 5)))

    xr = proj(gx, normed, offs)
    y, xa, u, s_in = scan_forward(xr, masks, segr, segc, par, hp, heads, 2)
    z = proj(gz, normed, offs)
    sig = jax.nn.sigmoid(z)
    silu = z * sig
    g = y * silu

    def group_sum(v):
        return tensor_sum(v + ring.swap(jnp.concatenate([v[:, mine:], v[:, :mine]], axis=1)))

    total_sq = group_sum(jnp.sum(g * g, 0, keepdims=True))
    s = lax.rsqrt(total_sq / inner_all + EPS)
    gain = own_chans(gate_gain)[:, None]
    gs = g * s
    ynt = (gs * gain).astype(BF16)

    def term(vt, act):
        def block(step):
            cut = lax.dynamic_slice_in_dim(act, ring.chip(step) * dd, dd, 1)
            return dot(vt, cut, (((1,), (0,))))

        return block

    sum_out = ring_scatter(ring, term(ynt, cots), chans)

    def own_rows(partial):
        return (partial[:mine].astype(F32) + ring.swap(partial[mine:]).astype(F32)).astype(BF16)

    def over_tensor(v):
        if n_t == 2:
            return v.astype(F32) + lax.ppermute(v, "tensor", [(0, 1), (1, 0)]).astype(F32)
        return lax.psum(v.astype(F32), "tensor")

    out_part = back([(go, ynt)], offs, width)
    output = (inputs + over_tensor(own_rows(out_part))).astype(BF16)

    dyn = proj(go, cots, offs)
    grad_gate = jnp.sum(dyn * gs, 1)
    wide_dyn = dyn * gain
    q_total = group_sum(jnp.sum(wide_dyn * g, 0, keepdims=True))
    dg = wide_dyn * s - g * (s * s * s * q_total / inner_all)
    dzt = (dg * y * (sig * (1.0 + z * (1.0 - sig)))).astype(BF16)
    dyt = (dg * silu).astype(BF16)

    sum_z = ring_scatter(ring, term(dzt, normed), chans)

    dxt, dbc, ddt, cg, hg = scan_backward(
        xr, masks, segr, segc, par, hp, xa, u, s_in, dyt, y, heads, 2
    )
    sum_x = ring_scatter(ring, term(dxt, normed), chans)

    quarter = 2 * STATE // (2 * n_t)
    dbc_low = dbc.astype(BF16)
    dbc_own = over_tensor(
        (dbc_low[:, :mine].astype(F32) + ring.swap(dbc_low[:, mine:]).astype(F32)).astype(BF16)
    ).astype(BF16)

    def bc_rows(v, start):
        return lax.dynamic_slice_in_dim(v, start, quarter, 0)

    ours = bc_rows(dbc_own, (t_index * 2 + core) * quarter)
    theirs = ring.swap(bc_rows(dbc_own, (t_index * 2 + 1 - core) * quarter))
    dbc_quarter = jnp.concatenate([ours, theirs], axis=1)
    ddt_low = ddt.astype(BF16)
    small = jnp.concatenate([dbc_quarter, ddt_low], axis=0)
    sum_small = ring_scatter(ring, term(small, normed), quarter + padded)

    row = lax.broadcasted_iota(jnp.int32, (2 * STATE, 1), 0)
    both = jnp.concatenate([dbc_own, ring.swap(dbc_own)], axis=1)
    here = row // quarter == t_index * 2 + core
    dbc_here = jnp.where(here, both, jnp.zeros_like(both))
    dxe = jnp.concatenate([dxt, dbc_here, ddt_low], axis=0)
    dn_own = own_rows(back([(gz, dzt), (gx, dxe)], offs, width))
    dn = over_tensor(dn_own)
    weighted = dn * pre_gain
    change = weighted * scales - inputs * scales**3 * (
        jnp.sum(weighted * inputs, -1, keepdims=True) / width
    )
    grad_hidden = (change + cotangent.astype(F32)).astype(BF16)
    pre_part = jnp.sum(dn_own.astype(F32) * inputs * scales, 0)

    cg = jnp.sum(cg, 2)
    hg = jnp.sum(hg, 2)[:, :heads]
    hg = hg * jnp.stack([jnp.ones_like(a_own), a_own, jnp.ones_like(a_own)])
    split = jnp.concatenate([cg[:, :chans].reshape(-1), grad_gate, hg.reshape(-1)])
    shared = jnp.concatenate([cg[:, chans:].reshape(-1), pre_part])
    both_sums = ring.chip_sum(jnp.concatenate([split, shared]))
    split, shared = both_sums[: split.shape[0]], both_sums[split.shape[0] :]
    split_other = ring.swap(split)
    shared = tensor_sum(shared + ring.swap(shared))

    def parts(v):
        a = v[: 5 * chans].reshape(5, chans)
        b = v[5 * chans : 6 * chans]
        c = v[6 * chans :].reshape(3, heads)
        return a, b, c

    (a0, b0, c0), (a1, b1, c1) = parts(split), parts(split_other)
    cg_x = in_order(a0, a1, 1)
    grad_gate = in_order(b0, b1, 0)
    hg = in_order(c0, c1, 1)
    cg_bc = shared[: 5 * 2 * STATE].reshape(5, 2 * STATE)
    grad_pre = shared[5 * 2 * STATE :]

    def finish(total):
        keep = pick(total, core, 1)
        return keep, ring.swap(pick(total, 1 - core, 1))

    kx, ox = finish(sum_x)
    kz, oz = finish(sum_z)
    ko, oo = finish(sum_out)
    grad_zx = jnp.stack([in_order(kz, oz, 0).T, in_order(kx, ox, 0).T])
    grad_out = in_order(ko, oo, 0)
    ks, os = finish(sum_small)
    grad_bc = in_order(ks[:quarter], os[:quarter], 0).T
    grad_dt = in_order(ks[quarter : quarter + heads], os[quarter : quarter + heads], 0).T
    return (
        output, grad_hidden, grad_zx, grad_dt, grad_bc, grad_out, cg_x[:4], cg_x[4], cg_bc[:4], cg_bc[4],
        hg[0], hg[1], hg[2], grad_pre, grad_gate,
    )


def solution(mesh):
    in_specs = (
        P("dp", None), P("dp"), P("dp", None), P(None, "dp", "tensor"), P("dp", "tensor"), P("dp", None),
        P("tensor", "dp"), P(None, "tensor"), P("tensor"), P(), P(), P("tensor"), P("tensor"), P("tensor"),
        P(), P("tensor"),
    )
    out_specs = (
        P("dp", None), P("dp", None), P(None, "dp", "tensor"), P("dp", "tensor"), P("dp", "tensor"),
        P("tensor", "dp"), P(None, "tensor"), P("tensor"), P(), P(), P("tensor"), P("tensor"), P("tensor"),
        P(), P("tensor"),
    )
    return jax.shard_map(local, mesh=mesh, in_specs=in_specs, out_specs=out_specs, check_vma=False)
```

```python
import functools

import jax
import jax.numpy as jnp
from jax import lax
from jax.experimental import pallas as pl
from jax.experimental.pallas import tpu as pltpu
from jax.sharding import PartitionSpec as P

EPS = 1e-05
Q = 128
NEG = -1e30
F32 = jnp.float32
BF16 = jnp.bfloat16
HIGH = lax.Precision.HIGHEST
MIB = 1024 * 1024
HEAD = 64
STATE = 128


BRIEF = pl.CostEstimate(flops=1, bytes_accessed=1, transcendentals=0)


def dot(a, b, dims, precision=None):
    return lax.dot_general(a, b, (dims, ((), ())), precision=precision, preferred_element_type=F32)


def params(mib):
    return pltpu.CompilerParams(vmem_limit_bytes=mib * MIB)


def after(value, *others):
    return lax.optimization_barrier((value, others))[0]


def ring_order(chips):
    if chips == 8:
        return [0, 2, 4, 6, 7, 5, 3, 1]
    half = chips // 2
    return list(range(half)) + list(range(chips - 1, half - 1, -1))


class Ring:
    def __init__(self, n_dp):
        self.n = n_dp // 2
        self.order = ring_order(self.n)
        place = [0] * self.n
        for position, chip in enumerate(self.order):
            place[chip] = position
        me = lax.axis_index("dp")
        self.core = me % 2
        self.mine = me // 2
        self.pos = jnp.asarray(place, jnp.int32)[self.mine]
        self.right = self.perm(1)
        self.left = self.perm(-1)
        self.full = self.n // 2 - 1

    def perm(self, step):
        pairs = []
        for p in range(self.n):
            for c in range(2):
                pairs.append((self.order[p] * 2 + c, self.order[(p + step) % self.n] * 2 + c))
        return pairs

    def table(self):
        table = [[self.order[(p + s) % self.n] for s in range(self.n)] for p in range(self.n)]
        row = lax.dynamic_index_in_dim(jnp.asarray(table, jnp.int32), self.pos, 0, keepdims=False)
        return jnp.concatenate([row, self.core.reshape(1).astype(jnp.int32)])

    def offsets(self, dd):
        steps = [0] + [-k for k in range(1, self.full + 1)] + list(range(1, self.full + 1)) + [self.n // 2]
        table = [[self.order[(p + s) % self.n] * dd for s in steps] for p in range(self.n)]
        return lax.dynamic_index_in_dim(jnp.asarray(table, jnp.int32), self.pos, 0, keepdims=False)

    def go_right(self, v):
        return lax.ppermute(v, "dp", self.right)

    def go_left(self, v):
        return lax.ppermute(v, "dp", self.left)

    def swap(self, v):
        return lax.ppermute(v, "dp", [(i, i ^ 1) for i in range(2 * self.n)])

    def ahead(self, k):
        pairs = []
        for chip in range(self.n):
            for c in range(2):
                pairs.append((chip * 2 + c, (chip + k) % self.n * 2 + c))
        return pairs


class Gather:
    def __init__(self, ring, unit, far, cut=None):
        self.ring, self.far, self.cut = ring, far, cut
        self.r, self.l = [unit], [unit]
        self.last = []

    def step(self):
        self.r.append(self.ring.go_right(self.r[-1]))
        self.l.append(self.ring.go_left(self.l[-1]))
        return self.newest()

    def newest(self):
        return self.r[-1], self.l[-1]

    def finish(self):
        while len(self.r) <= self.ring.full:
            self.step()
        r, l, cut = self.r[-1], self.l[-1], self.cut
        if self.far == "both":
            self.last = [self.ring.go_right(r[:cut]), self.ring.go_left(l[cut:])]
        elif self.far == "right":
            self.last = [self.ring.go_right(r)]
        else:
            self.last = [self.ring.go_left(l)]
        return self.last

    def blocks(self):
        return self.r + self.l[1:] + self.last


def both_parts(vt, own, other):
    half = own.shape[0]
    return dot(vt[:, :half], own[...], (((1,), (0,)))) + dot(vt[:, half:], other[...], (((1,), (0,))))


def term_kernel(plan, table, vt, *refs):
    i, half = pl.program_id(0), pl.num_programs(0) // 2
    n = len(plan)
    acts, refs = refs[: 2 * n], refs[2 * n :]
    came, outs = refs[: sum(p != "" for p in plan)], refs[sum(p != "" for p in plan) :]
    k = 0
    for b in range(n):
        total = both_parts(vt, acts[2 * b], acts[2 * b + 1])
        if plan[b]:
            part = came[k][...].astype(F32)
            k += 1
            if plan[b] == "top":
                part = jnp.where(i < half, part, 0.0)
            elif plan[b] == "bottom":
                part = jnp.where(i >= half, part, 0.0)
            total = total + part
        outs[b][...] = total.astype(BF16)


def far_kernel(table, vt, own, other, top, bottom):
    i, half = pl.program_id(0), pl.num_programs(0) // 2
    total = both_parts(vt, own, other).astype(BF16)

    @pl.when(i < half)
    def _():
        top[...] = total

    @pl.when(i >= half)
    def _():
        bottom[...] = total


def last_kernel(table, vt, own, other, r, l, keep, give):
    total = both_parts(vt, own, other) + r[...].astype(F32) + l[...].astype(F32)
    dd = keep.shape[1]
    core = table[table.shape[0] - 1]
    low, high = total[:, :dd], total[:, dd:]
    keep[...] = jnp.where(core == 0, low, high)
    give[...] = jnp.where(core == 0, high, low)


class Scatter:
    def __init__(self, ring, table, vt, acts, dd, far):
        self.ring, self.table, self.vt, self.acts, self.dd, self.far = ring, table, vt, acts, dd, far
        self.rows = vt.shape[0]
        self.tile = self.rows // 2
        self.left_to_do = ring.full
        opposite = ring.n // 2
        if far == "both":
            self.out = self.call(far_kernel, (), [opposite], [], ["top", "bottom"])
        else:
            self.out = self.call(functools.partial(term_kernel, [""]), (), [opposite], [], ["all"])
        self.send()

    def spec(self, kind, lanes):
        half = self.rows // self.tile // 2
        if kind == "top":
            return pl.BlockSpec((self.tile, lanes), lambda i, a: (jnp.minimum(i, half - 1), 0))
        if kind == "bottom":
            return pl.BlockSpec((self.tile, lanes), lambda i, a: (jnp.maximum(i - half, 0), 0))
        return pl.BlockSpec((self.tile, lanes), lambda i, a: (i, 0))

    def call(self, kernel, others, steps, came, kinds, lanes=None, dtype=BF16):
        table = after(self.table, *others) if others else self.table
        tokens = self.vt.shape[1]
        lanes = lanes or self.dd
        half = self.rows // 2
        columns = []
        for step in steps:
            place = step % self.ring.n
            columns += [pl.BlockSpec((tokens // 2, self.dd), lambda i, a, place=place: (0, a[place]))] * 2
        shape = lambda kind: jax.ShapeDtypeStruct((half if kind in ("top", "bottom") else self.rows, lanes), dtype)
        return pl.pallas_call(
            kernel,
            out_shape=tuple(shape(k) for k in kinds),
            grid_spec=pltpu.PrefetchScalarGridSpec(
                num_scalar_prefetch=1,
                grid=(self.rows // self.tile,),
                in_specs=[pl.BlockSpec((self.tile, tokens), lambda i, a: (i, 0))]
                + columns
                + [self.spec(kind, self.dd) for kind, _ in came],
                out_specs=tuple(self.spec(k, lanes) for k in kinds),
            ),
            compiler_params=params(20),
            cost_estimate=BRIEF,
        )(table, self.vt, *(self.acts * len(steps)), *[v for _, v in came])

    def send(self):
        self.r = self.l = None
        if self.far != "left" or len(self.out) == 2:
            self.r = self.ring.go_right(self.out[0])
        if self.far != "right" or len(self.out) == 2:
            self.l = self.ring.go_left(self.out[-1])

    def step(self, *others):
        if not self.left_to_do:
            return self.out
        j, ring = self.left_to_do, self.ring
        split = j == ring.full and self.far == "both"
        plan, came = [], []
        for kind, v in (("top", self.r), ("bottom", self.l)):
            kind = kind if split else "all"
            plan.append("" if v is None else kind)
            if v is not None:
                came.append((kind, v))
        self.out = self.call(functools.partial(term_kernel, plan), others, [j, -j], came, ["all", "all"])
        self.left_to_do -= 1
        self.send()
        return self.out

    def finish(self, *others):
        while self.left_to_do:
            self.step()
        return self.call(
            last_kernel, others, [0], [("all", self.r), ("all", self.l)], ["all", "all"], self.dd // 2, F32
        )


def prep_x_kernel(place, own, other, small_own, small_other, out):
    core = place[0]
    dd = own.shape[1]
    chans = own.shape[2] // 2
    padded = out.shape[0] - chans - STATE
    for b in range(2):
        lanes = slice(b * dd, (b + 1) * dd)
        near = core == b
        src = jnp.where(near, own[0], other[0])
        src = jnp.where(core == 0, src[:, :chans], src[:, chans:])
        out[:chans, lanes] = src.T
        small = jnp.where(near, small_own[...], small_other[...])
        states = jnp.where(core == 0, small[:, :STATE], small[:, STATE : 2 * STATE])
        out[chans : chans + STATE, lanes] = states.T
        steps = jnp.where(core == 0, small[:, 2 * STATE : 3 * STATE], small[:, 3 * STATE :])
        out[chans + STATE :, lanes] = steps.T[:padded]


def prep_x(place, own, other, small_own, small_other, padded):
    _, dd, inner = own.shape
    rows = inner // 2 + STATE + padded
    return pl.pallas_call(
        prep_x_kernel,
        out_shape=jax.ShapeDtypeStruct((rows, 2 * dd), BF16),
        grid_spec=pltpu.PrefetchScalarGridSpec(
            num_scalar_prefetch=1,
            grid=(1,),
            in_specs=[pl.BlockSpec((1, dd, inner), lambda i, p: (1, 0, 0))] * 2
            + [pl.BlockSpec((dd, 4 * STATE), lambda i, p: (0, 0))] * 2,
            out_specs=pl.BlockSpec((rows, 2 * dd), lambda i, p: (0, 0)),
        ),
        compiler_params=params(12),
        cost_estimate=BRIEF,
    )(place, own, other, small_own, small_other)


def prep_zo_kernel(place, own, other, out_own, out_other, z, o):
    core = place[0]
    dd = own.shape[1]
    chans = own.shape[2] // 2
    for b in range(2):
        lanes = slice(b * dd, (b + 1) * dd)
        near = core == b
        src = jnp.where(near, own[0], other[0])
        src = jnp.where(core == 0, src[:, :chans], src[:, chans:])
        z[:, lanes] = src.T
        src = jnp.where(near, out_own[...], out_other[...])
        o[:, lanes] = jnp.where(core == 0, src[:chans], src[chans:])


def prep_zo(place, own, other, out_own, out_other):
    _, dd, inner = own.shape
    shape = (inner // 2, 2 * dd)
    return pl.pallas_call(
        prep_zo_kernel,
        out_shape=(jax.ShapeDtypeStruct(shape, BF16),) * 2,
        grid_spec=pltpu.PrefetchScalarGridSpec(
            num_scalar_prefetch=1,
            grid=(1,),
            in_specs=[pl.BlockSpec((1, dd, inner), lambda i, p: (0, 0, 0))] * 2
            + [pl.BlockSpec((inner, dd), lambda i, p: (0, 0))] * 2,
            out_specs=(pl.BlockSpec(shape, lambda i, p: (0, 0)),) * 2,
        ),
        compiler_params=params(12),
        cost_estimate=BRIEF,
    )(place, own, other, out_own, out_other)


class Weight:
    def __init__(self, blocks, first, rows, cut=None):
        self.args, self.specs, self.plan = [], [], []
        self.rows, self.dd = rows, blocks[0].shape[1]

        def view(array, start, size):
            index = start // size
            self.args.append(array)
            self.specs.append(pl.BlockSpec((size, self.dd), lambda i, o, index=index: (index, 0)))

        whole = blocks if cut is None else blocks[:-2]
        for block in whole:
            view(block, first, rows)
            self.plan.append(1)
        if cut is not None:
            pieces = 0
            if first < cut:
                view(blocks[-2], first, min(rows, cut - first))
                pieces += 1
            if first + rows > cut:
                start = max(first, cut)
                view(blocks[-1], start - cut, first + rows - start)
                pieces += 1
            self.plan.append(pieces)

    def read(self, refs):
        at, out = 0, []
        for pieces in self.plan:
            part = [r[...] for r in refs[at : at + pieces]]
            out.append(part[0] if pieces == 1 else jnp.concatenate(part, axis=0))
            at += pieces
        return out


def projected(weight, refs, act, offs):
    total = None
    for b, w in enumerate(weight.read(refs)):
        off = pl.multiple_of(offs[b], weight.dd)
        part = dot(w, act[:, pl.ds(off, weight.dd)], (((1,), (1,))))
        total = part if total is None else total + part
    return total


def projection(body, weight, acts, offs, extra, extra_specs, out_shape, out_specs, mib=40):
    tile, width = acts[0].shape
    tokens = 2 * tile
    n = len(weight.args)

    def kernel(offs, *refs):
        for k in range(2):

            @pl.when(pl.program_id(0) == k)
            def _():
                acc = projected(weight, refs[:n], refs[n + k], offs)
                body(acc, refs[n + 2 : n + 2 + len(extra)], refs[n + 2 + len(extra) :])

    return pl.pallas_call(
        kernel,
        out_shape=out_shape,
        grid_spec=pltpu.PrefetchScalarGridSpec(
            num_scalar_prefetch=1,
            grid=(tokens // tile,),
            in_specs=weight.specs + [pl.BlockSpec((tile, width), lambda i, o: (0, 0))] * 2 + extra_specs,
            out_specs=out_specs,
        ),
        compiler_params=params(mib),
        cost_estimate=BRIEF,
    )(offs, *weight.args, *acts, *extra)


def plain_projection(weight, acts, offs):
    tile = acts[0].shape[0]

    def body(acc, extra, outs):
        outs[0][...] = acc

    return projection(
        body, weight, acts, offs, (), [],
        jax.ShapeDtypeStruct((weight.rows, 2 * tile), F32),
        pl.BlockSpec((weight.rows, tile), lambda i, o: (0, i)),
    )


def two_projections(first, second, acts, offs):
    tile, width = acts[0].shape
    n, m = len(first.args), len(second.args)

    def kernel(offs, *refs):
        parts = [jnp.concatenate(p, axis=0) for p in zip(first.read(refs[:n]), second.read(refs[n : n + m]))]
        for k in range(2):
            total = None
            for b, w in enumerate(parts):
                off = pl.multiple_of(offs[b], first.dd)
                part = dot(w, refs[n + m + k][:, pl.ds(off, first.dd)], (((1,), (1,))))
                total = part if total is None else total + part
            refs[-2][:, k * tile : (k + 1) * tile] = total[: first.rows]
            refs[-1][:, k * tile : (k + 1) * tile] = total[first.rows :]

    whole = lambda i, o: (0, 0)
    return pl.pallas_call(
        kernel,
        out_shape=tuple(jax.ShapeDtypeStruct((w.rows, 2 * tile), F32) for w in (first, second)),
        grid_spec=pltpu.PrefetchScalarGridSpec(
            num_scalar_prefetch=1,
            grid=(1,),
            in_specs=first.specs + second.specs + [pl.BlockSpec((tile, width), whole)] * 2,
            out_specs=tuple(pl.BlockSpec((w.rows, 2 * tile), whole) for w in (first, second)),
        ),
        compiler_params=params(40),
        cost_estimate=BRIEF,
    )(offs, *first.args, *second.args, *acts)


def sigmoid(v):
    return 0.5 * jnp.tanh(0.5 * v) + 0.5


def gate_projection(weight, acts, offs, y):
    rows, tokens = y.shape
    tile = tokens // 2

    def body(z, extra, outs):
        outs[0][...] = z
        g = extra[0][...] * (z * sigmoid(z))
        outs[1][...] = jnp.sum(g * g, axis=0, keepdims=True)

    wide = pl.BlockSpec((rows, tile), lambda i, o: (0, i))
    line = pl.BlockSpec((1, tile), lambda i, o: (0, i))
    return projection(
        body, weight, acts, offs, (y,), [wide],
        (jax.ShapeDtypeStruct((rows, tokens), F32), jax.ShapeDtypeStruct((1, tokens), F32)),
        (wide, line),
    )


def back_projection(weight, acts, offs, y, z, gain):
    rows, tokens = y.shape
    tile = tokens // 2

    def body(dyn, extra, outs):
        y, z, gain = extra
        outs[0][...] = dyn
        zv = z[...]
        g = y[...] * (zv * sigmoid(zv))
        outs[1][...] = jnp.sum(dyn * gain[...] * g, axis=0, keepdims=True)

    wide = pl.BlockSpec((rows, tile), lambda i, o: (0, i))
    line = pl.BlockSpec((1, tile), lambda i, o: (0, i))
    return projection(
        body, weight, acts, offs, (y, z, gain),
        [wide, wide, pl.BlockSpec((rows, 1), lambda i, o: (0, 0))],
        (jax.ShapeDtypeStruct((rows, tokens), F32), jax.ShapeDtypeStruct((1, tokens), F32)),
        (wide, line),
    )


def back(groups, offs, width, base=None, hiddens=None):
    dd = groups[0][0].dd
    tokens = groups[0][1].shape[1]
    half = tokens // 2
    args, specs = [], []
    flops = 0
    for weight, vt in groups:
        args += weight.args + [vt]
        specs += weight.specs + [pl.BlockSpec((vt.shape[0], tokens), lambda i, o: (0, 0))]
        flops += 2 * vt.shape[0] * tokens * width
    out_spec = pl.BlockSpec((half, width), lambda i, o: (0, 0))
    if base is not None:
        args += list(base)
        specs += [out_spec, out_spec]
    shapes = [jax.ShapeDtypeStruct((half, width), BF16)] * 2
    out_specs = [out_spec, out_spec]
    if hiddens is not None:
        args += list(hiddens)
        specs += [out_spec, out_spec]
        shapes.append(jax.ShapeDtypeStruct((1, width), F32))
        out_specs.append(pl.BlockSpec((1, width), lambda i, o: (0, 0)))

    def kernel(offs, *refs):
        outs = refs[len(args) :]
        at, terms = 0, []
        for weight, _ in groups:
            n = len(weight.args)
            terms.append((refs[at + n][...].T, weight.read(refs[at : at + n])))
            at += n + 1
        scales = []
        if hiddens is not None:
            for h in refs[len(args) - 2 : len(args)]:
                v = h[...].astype(F32)
                scales.append(lax.rsqrt(jnp.mean(v * v, axis=1, keepdims=True) + EPS))
        for b in range(len(terms[0][1])):
            off = pl.multiple_of(offs[b], dd)
            along = None
            total = None
            for v, blocks in terms:
                part = dot(v, blocks[b], (((1,), (0,))))
                total = part if total is None else total + part
            for k in range(2):
                part = total[k * half : (k + 1) * half]
                if base is not None:
                    part = part + refs[at + k][:, pl.ds(off, dd)].astype(F32)
                outs[k][:, pl.ds(off, dd)] = part.astype(BF16)
                if hiddens is not None:
                    h = refs[len(args) - 2 + k][:, pl.ds(off, dd)].astype(F32)
                    line = jnp.sum(part * (h * scales[k]), axis=0, keepdims=True)
                    along = line if along is None else along + line
            if hiddens is not None:
                outs[2][:, pl.ds(off, dd)] = along

    return pl.pallas_call(
        kernel,
        out_shape=tuple(shapes),
        grid_spec=pltpu.PrefetchScalarGridSpec(
            num_scalar_prefetch=1, grid=(1,), in_specs=specs, out_specs=tuple(out_specs)
        ),
        compiler_params=params(40),
        cost_estimate=BRIEF,
    )(offs, *args)


def messages_kernel(n, table, rows_ref, own, other, common, *refs):
    outs, terms = refs[:n], refs[n]
    rows = rows_ref.shape[0]
    dd = outs[0].shape[1]
    terms[...] = both_parts(rows_ref, own, other)
    me = table[0]
    for k in range(n):
        off = pl.multiple_of(lax.rem(me + k, n) * dd, dd)
        outs[k][:rows, :] = terms[:, pl.ds(off, dd)].astype(BF16)
        outs[k][rows:, :] = common[...].astype(BF16)


def messages(ring, table, rows, acts, common):
    dd = common.shape[1]
    m, tokens = rows.shape
    width = acts[0].shape[1]
    whole = lambda i, t: (0, 0)
    shape = (m + common.shape[0], dd)
    return pl.pallas_call(
        functools.partial(messages_kernel, ring.n),
        out_shape=(jax.ShapeDtypeStruct(shape, BF16),) * ring.n,
        grid_spec=pltpu.PrefetchScalarGridSpec(
            num_scalar_prefetch=1,
            grid=(1,),
            in_specs=[pl.BlockSpec((m, tokens), whole)]
            + [pl.BlockSpec((tokens // 2, width), whole)] * 2
            + [pl.BlockSpec(common.shape, whole)],
            out_specs=(pl.BlockSpec(shape, whole),) * ring.n,
            scratch_shapes=[pltpu.VMEM((m, width), F32)],
        ),
        compiler_params=params(20),
        cost_estimate=BRIEF,
    )(table, rows, *acts, common)


def norm_back_kernel(own, came, hidden, cot, gain, out):
    h = hidden[...].astype(F32)
    width = h.shape[1]
    r = lax.rsqrt(jnp.mean(h * h, axis=1, keepdims=True) + EPS)
    weighted = (own[...].astype(F32) + came[...].astype(F32)) * gain[...]
    along = jnp.sum(weighted * h, axis=1, keepdims=True) * (1.0 / width)
    out[...] = (weighted * r - h * (r * r * r * along) + cot[...].astype(F32)).astype(BF16)


def norm_back(own, came, hidden, cot, gain):
    rows, width = own.shape
    tile = 128
    block = pl.BlockSpec((tile, width), lambda i: (i, 0))
    return pl.pallas_call(
        norm_back_kernel,
        grid=(rows // tile,),
        out_shape=jax.ShapeDtypeStruct((rows, width), BF16),
        in_specs=[block] * 4 + [pl.BlockSpec((1, width), lambda i: (0, 0))],
        out_specs=block,
        compiler_params=params(16),
        cost_estimate=BRIEF,
    )(own, came, hidden, cot, gain)


def turn_kernel(place, *refs):
    out = refs[-1]
    chans = refs[0].shape[0]
    first = place[0] == 0
    for k in range(2):
        own, other = refs[2 * k][...], refs[2 * k + 1][...]
        out[k, :, :chans] = jnp.where(first, own, other).T
        out[k, :, chans:] = jnp.where(first, other, own).T


def turn(place, *parts):
    chans, dd = parts[0].shape
    return pl.pallas_call(
        turn_kernel,
        out_shape=jax.ShapeDtypeStruct((2, dd, 2 * chans), F32),
        grid_spec=pltpu.PrefetchScalarGridSpec(
            num_scalar_prefetch=1,
            grid=(1,),
            in_specs=[pl.BlockSpec((chans, dd), lambda i, p: (0, 0))] * 4,
            out_specs=pl.BlockSpec((2, dd, 2 * chans), lambda i, p: (0, 0, 0)),
        ),
        compiler_params=params(16),
        cost_estimate=BRIEF,
    )(place, *parts)


def gate_back_kernel(total, dyn, y, z, s, q, gain, dz, dy, dgain):
    zv, yv, sv = z[...], y[...], s[...]
    sig = sigmoid(zv)
    silu = zv * sig
    g = yv * silu
    scaled = dyn[...] * sv
    dgain[...] = jnp.sum(scaled * g, axis=1, keepdims=True)
    dg = scaled * gain[...] - g * (sv * sv * sv * q[...] * (1.0 / total))
    dz[...] = (dg * yv * (sig * (1.0 + zv * (1.0 - sig)))).astype(BF16)
    dy[...] = (dg * silu).astype(BF16)


def gate_back(total, dyn, y, z, s, q, gain):
    rows, tokens = dyn.shape
    tile = rows // 4
    wide = pl.BlockSpec((tile, tokens), lambda i: (i, 0))
    line = pl.BlockSpec((1, tokens), lambda i: (0, 0))
    return pl.pallas_call(
        functools.partial(gate_back_kernel, float(total)),
        grid=(rows // tile,),
        out_shape=(jax.ShapeDtypeStruct((rows, tokens), BF16),) * 2
        + (jax.ShapeDtypeStruct((rows, 1), F32),),
        in_specs=[wide, wide, wide, line, line, pl.BlockSpec((tile, 1), lambda i: (i, 0))],
        out_specs=(wide, wide, pl.BlockSpec((tile, 1), lambda i: (i, 0))),
        compiler_params=params(24),
        cost_estimate=BRIEF,
    )(dyn, y, z, s, q, gain)


def head_terms(raw, hp_ref):
    pre = raw + hp_ref[:, 0:1]
    small = jnp.exp(-jnp.abs(pre))
    one = 1.0 + small
    away = one - 1.0
    log1p = jnp.where(away == 0.0, small, jnp.log(one) * (small / jnp.where(away == 0.0, 1.0, away)))
    dt = jnp.maximum(pre, 0.0) + log1p
    logistic = jnp.where(pre >= 0.0, 1.0, small) / one
    rows = lax.broadcasted_iota(jnp.int32, (Q, Q), 0)
    lanes = lax.broadcasted_iota(jnp.int32, (Q, Q), 1)
    upto = (rows <= lanes).astype(F32)
    logs = dt * hp_ref[:, 1:2]
    cums = dot(logs, upto, (((1,), (0,))), HIGH)
    return dt, logistic, cums


def to_columns(cums):
    n = cums.shape[0]
    square = jnp.concatenate([cums, jnp.zeros((Q - n, Q), F32)], axis=0)
    return square.T


def pair_bias(segr_ref, segc_ref):
    rows = lax.broadcasted_iota(jnp.int32, (Q, Q), 0)
    lanes = lax.broadcasted_iota(jnp.int32, (Q, Q), 1)
    keep = (segc_ref[...] == segr_ref[...]) & (rows <= lanes)
    return jnp.where(keep, 0.0, NEG)


def state_rows(place, own, other, r0):
    at = r0 % STATE
    rows = slice(at, at + HEAD)
    return jnp.where(place[0] == r0 // STATE, own[rows, :], other[rows, :])


def fwd_kernel(
    heads, given, place, xr_ref, bco_ref, bcs_ref, dt_ref, mask_ref, segr_ref, segc_ref, par_ref, hp_ref, *rest
):
    y_ref, xa_ref, u_ref, s_ref, prev, state, parb, xt = rest[given:]
    chans = heads * HEAD
    wide = chans + 2 * STATE

    @pl.when(pl.program_id(0) == 0)
    def _():
        for k in range(6):
            parb[k] = jnp.broadcast_to(par_ref[:, k : k + 1], (wide, Q))
        prev[...] = jnp.zeros_like(prev)
        state[...] = jnp.zeros_like(state)

    lane = lax.broadcasted_iota(jnp.int32, (HEAD, Q), 1)
    m1, m2, m3 = mask_ref[0:1, :], mask_ref[1:2, :], mask_ref[2:3, :]

    def conv(r0):
        rows = slice(r0, r0 + HEAD)
        cur = xr_ref[rows, :] if r0 < chans else state_rows(place, bco_ref, bcs_ref, r0 - chans)
        old = prev[rows, :]
        u = parb[4, rows, :] + parb[3, rows, :] * cur
        u = u + parb[2, rows, :] * (m1 * pltpu.roll(jnp.where(lane >= Q - 1, old, cur), 1, 1))
        u = u + parb[1, rows, :] * (m2 * pltpu.roll(jnp.where(lane >= Q - 2, old, cur), 2, 1))
        u = u + parb[0, rows, :] * (m3 * pltpu.roll(jnp.where(lane >= Q - 3, old, cur), 3, 1))
        prev[rows, :] = cur
        u_ref[rows, :] = u
        xa = (u * (0.5 * jnp.tanh(0.5 * u) + 0.5)).astype(BF16)
        xa_ref[rows, :] = xa
        return xa

    for r0 in range(chans, wide, HEAD):
        conv(r0)
    bt = xa_ref[chans : chans + STATE, :]
    ct = xa_ref[chans + STATE : wide, :]
    mix = dot(bt.T, ct, (((1,), (0,))))
    dt, _, cums = head_terms(dt_ref[...], hp_ref)
    cols = to_columns(cums)
    bias = pair_bias(segr_ref, segc_ref)
    enter = jnp.exp(cums) * mask_ref[3:4, :]
    last = jnp.broadcast_to(cums[:, Q - 1 : Q], cums.shape)
    tail = jnp.exp(last - cums) * mask_ref[4:5, :]
    passing = jnp.exp(last) * mask_ref[5:6, :]
    s_in = state[...].astype(BF16)
    s_ref[...] = s_in
    carried = dot(s_in, ct, (((1,), (0,))))
    for h in range(heads):
        rows = slice(h * HEAD, (h + 1) * HEAD)
        xa = conv(h * HEAD).astype(F32)
        decay = jnp.exp(cums[h : h + 1, :] - cols[:, h : h + 1] + bias)
        mixing = (mix * decay).astype(BF16)
        xd = xa * dt[h : h + 1, :]
        xt[rows, :] = (xd * tail[h : h + 1, :]).astype(BF16)
        y = dot(xd.astype(BF16), mixing, (((1,), (0,))))
        y = y + enter[h : h + 1, :] * carried[rows, :] + parb[5, rows, :] * xa
        y_ref[rows, :] = y
    fresh = dot(xt[...], bt, (((1,), (1,))))
    for h in range(heads):
        rows = slice(h * HEAD, (h + 1) * HEAD)
        state[rows, :] = state[rows, :] * passing[h : h + 1, :] + fresh[rows, :]


def scan_forward(place, xr, bco, bcs, dtr, masks, segr, segc, par, hp, heads, seqs, seq, given=()):
    chans, tokens = xr.shape
    padded = dtr.shape[0]
    wide = chans + 2 * STATE
    count = tokens // seqs // Q
    at = lambda k, p: (0, seq * count + k)
    swapped = lambda k, p: (0, (seqs - 1 - seq) * count + k)
    whole = lambda k, p: (0, 0)
    args = (xr, bco, bcs, dtr, masks, segr, segc, par, hp)
    return pl.pallas_call(
        functools.partial(fwd_kernel, heads, len(given)),
        out_shape=(
            jax.ShapeDtypeStruct((chans, tokens), F32),
            jax.ShapeDtypeStruct((wide, tokens), BF16),
            jax.ShapeDtypeStruct((wide, tokens), F32),
            jax.ShapeDtypeStruct((chans, tokens), BF16),
        ),
        grid_spec=pltpu.PrefetchScalarGridSpec(
            num_scalar_prefetch=1,
            grid=(count,),
            in_specs=[
                pl.BlockSpec((chans, Q), at),
                pl.BlockSpec((STATE, Q), at),
                pl.BlockSpec((STATE, Q), swapped),
                pl.BlockSpec((padded, Q), at),
                pl.BlockSpec((8, Q), at),
                pl.BlockSpec((1, Q), at),
                pl.BlockSpec((Q, 1), lambda k, p: (seq * count + k, 0)),
                pl.BlockSpec(par.shape, whole),
                pl.BlockSpec(hp.shape, whole),
            ]
            + [pl.BlockSpec(memory_space=pl.ANY)] * len(given),
            out_specs=(
                pl.BlockSpec((chans, Q), at),
                pl.BlockSpec((wide, Q), at),
                pl.BlockSpec((wide, Q), at),
                pl.BlockSpec((chans, STATE), at),
            ),
            scratch_shapes=[
                pltpu.VMEM((wide, Q), F32),
                pltpu.VMEM((chans, STATE), F32),
                pltpu.VMEM((6, wide, Q), F32),
                pltpu.VMEM((chans, Q), BF16),
            ],
        ),
        input_output_aliases={1 + len(args) + k: k for k in range(len(given))},
        compiler_params=params(58),
        cost_estimate=BRIEF,
    )(place, *args, *given)


def bwd_kernel(
    heads, given, place, xr_ref, bco_ref, bcs_ref, dt_ref, mask_ref, segr_ref, segc_ref, par_ref, hp_ref, xa_ref,
    u_ref, s_ref,
    dy_ref, y_ref, *rest,
):
    dx_ref, dbc_ref, ddt_ref, cgo_ref, hg_ref, dstate, parb, after, nmask, xt, dye, cg_ref = rest[given:]
    chans = heads * HEAD
    wide = chans + 2 * STATE

    @pl.when(pl.program_id(0) == 0)
    def _():
        for k in range(6):
            parb[k] = jnp.broadcast_to(par_ref[:, k : k + 1], (wide, Q))
        cg_ref[...] = jnp.zeros_like(cg_ref)
        hg_ref[...] = jnp.zeros_like(hg_ref)
        dstate[...] = jnp.zeros_like(dstate)
        after[...] = jnp.zeros_like(after)
        nmask[...] = jnp.zeros_like(nmask)

    lane = lax.broadcasted_iota(jnp.int32, (HEAD, Q), 1)
    lane8 = lax.broadcasted_iota(jnp.int32, (8, Q), 1)
    sub8 = lax.broadcasted_iota(jnp.int32, (8, Q), 0)
    masks = mask_ref[...]
    shifted_masks = jnp.where(lane8 <= sub8, nmask[...], masks)
    nmask[...] = masks

    def conv_back(r0, dxa, out, out0):
        rows = slice(r0, r0 + HEAD)
        u = u_ref[rows, :]
        sig = 0.5 * jnp.tanh(0.5 * u) + 0.5
        dc = dxa * (sig * (1.0 + u * (1.0 - sig)))
        xr = xr_ref[rows, :] if r0 < chans else state_rows(place, bco_ref, bcs_ref, r0 - chans)
        old = after[rows, :]
        after[rows, :] = dc
        dx = parb[3, rows, :] * dc
        cg_ref[4, rows, :] += dc
        cg_ref[3, rows, :] += xr * dc
        for k in (1, 2, 3):
            e = jnp.where(lane < k, old, dc) * shifted_masks[k - 1 : k, :]
            e = pltpu.roll(e, Q - k, 1)
            dx = dx + parb[3 - k, rows, :] * e
            cg_ref[3 - k, rows, :] += xr * e
        out[out0 : out0 + HEAD, :] = dx.astype(out.dtype)

    bt = xa_ref[chans : chans + STATE, :]
    ct = xa_ref[chans + STATE : wide, :]
    mix = dot(bt.T, ct, (((1,), (0,))))
    dt, logistic, cums = head_terms(dt_ref[...], hp_ref)
    cols = to_columns(cums)
    bias = pair_bias(segr_ref, segc_ref)
    enter = jnp.exp(cums) * masks[3:4, :]
    last = jnp.broadcast_to(cums[:, Q - 1 : Q], cums.shape)
    tail = jnp.exp(last - cums) * masks[4:5, :]
    passing = jnp.exp(last) * masks[5:6, :]
    ds = dstate[...].astype(BF16)
    spread = dot(ds, bt, (((1,), (0,))))
    dmix = jnp.zeros((Q, Q), F32)
    s_in = s_ref[...]
    direct, cross, skip, outward, through, inward = [], [], [], [], [], []
    for h in range(heads):
        rows = slice(h * HEAD, (h + 1) * HEAD)
        xa = xa_ref[rows, :].astype(F32)
        dyb = dy_ref[rows, :]
        dy = dyb.astype(F32)
        decay = jnp.exp(cums[h : h + 1, :] - cols[:, h : h + 1] + bias)
        mixing = (mix * decay).astype(BF16)
        xd = xa * dt[h : h + 1, :]
        xdb = xd.astype(BF16)
        xt[rows, :] = (xd * tail[h : h + 1, :]).astype(BF16)
        dye[rows, :] = (dy * enter[h : h + 1, :]).astype(BF16)
        dmix = dmix + dot(xdb, dyb, (((0,), (0,)))) * decay
        near = dot(dyb, mixing, (((1,), (1,))))
        far = tail[h : h + 1, :] * spread[rows, :]
        pull = near + far
        direct.append(jnp.sum(xa * pull, axis=0, keepdims=True))
        cross.append(jnp.sum(xdb.astype(F32) * near, axis=0, keepdims=True))
        outward.append(jnp.sum(xd * far, axis=0, keepdims=True))
        through.append(jnp.sum(dstate[rows, :] * s_in[rows, :].astype(F32), axis=0, keepdims=True))
        skip.append(jnp.sum(xa * dy, axis=0, keepdims=True))
        inward.append(jnp.sum(y_ref[rows, :] * dy, axis=0, keepdims=True))
        dxa = dt[h : h + 1, :] * pull + parb[5, rows, :] * dy
        conv_back(h * HEAD, dxa, dx_ref, h * HEAD)
    pad = ddt_ref.shape[0] - heads
    if pad:
        zero = [jnp.zeros((pad, Q), F32)]
        direct, cross, skip = direct + zero, cross + zero, skip + zero
        outward, through, inward = outward + zero, through + zero, inward + zero
    direct, cross, skip, outward, through, inward = (
        jnp.concatenate(v, axis=0) for v in (direct, cross, skip, outward, through, inward)
    )
    dlog = inward - hp_ref[:, 2:3] * skip - cross
    rows = lax.broadcasted_iota(jnp.int32, (Q, Q), 0)
    lanes = lax.broadcasted_iota(jnp.int32, (Q, Q), 1)
    dl = dot(dlog, (rows >= lanes).astype(F32), (((1,), (0,))), HIGH)
    dl = dl + dot(outward, (rows < lanes).astype(F32), (((1,), (0,))), HIGH)
    dl = dl + passing * jnp.sum(through, axis=1, keepdims=True)
    ddt = (direct + hp_ref[:, 1:2] * dl) * logistic
    ddt_ref[...] = ddt
    hg_ref[0] += ddt
    hg_ref[1] += dt * dl
    hg_ref[2] += skip
    dmixb = dmix.astype(BF16)
    xtv, dyev = xt[...], dye[...]
    dbt = dot(ct, dmixb, (((1,), (1,)))) + dot(ds, xtv, (((0,), (0,))))
    dct = dot(bt, dmixb, (((1,), (0,)))) + dot(s_ref[...], dyev, (((0,), (0,))))
    dbca = jnp.concatenate([dbt, dct], axis=0)
    for r0 in range(0, 2 * STATE, HEAD):
        conv_back(chans + r0, dbca[r0 : r0 + HEAD, :], dbc_ref, r0)
    fresh = dot(dyev, ct, (((1,), (1,))))
    for h in range(heads):
        rows = slice(h * HEAD, (h + 1) * HEAD)
        dstate[rows, :] = dstate[rows, :] * passing[h : h + 1, :] + fresh[rows, :]

    @pl.when(pl.program_id(0) == pl.num_programs(0) - 1)
    def _():
        for r0 in range(0, wide, HEAD):
            rows = slice(r0, r0 + HEAD)
            for k in range(5):
                cgo_ref[rows, k : k + 1] = jnp.sum(cg_ref[k, rows, :], axis=1, keepdims=True)


def scan_backward(
    place, xr, bco, bcs, dtr, masks, segr, segc, par, hp, xa, u, s_in, dy, y, heads, seqs, seq, given=()
):
    chans, tokens = xr.shape
    padded = dtr.shape[0]
    wide = chans + 2 * STATE
    count = tokens // seqs // Q
    at = lambda k, p: (0, seq * count + count - 1 - k)
    swapped = lambda k, p: (0, (seqs - 1 - seq) * count + count - 1 - k)
    whole = lambda k, p: (0, 0)
    args = (xr, bco, bcs, dtr, masks, segr, segc, par, hp, xa, u, s_in, dy, y)
    return pl.pallas_call(
        functools.partial(bwd_kernel, heads, len(given)),
        out_shape=(
            jax.ShapeDtypeStruct((chans, tokens), BF16),
            jax.ShapeDtypeStruct((2 * STATE, tokens), F32),
            jax.ShapeDtypeStruct((padded, tokens), F32),
            jax.ShapeDtypeStruct((wide, 8), F32),
            jax.ShapeDtypeStruct((3, padded, Q), F32),
        ),
        grid_spec=pltpu.PrefetchScalarGridSpec(
            num_scalar_prefetch=1,
            grid=(count,),
            in_specs=[
                pl.BlockSpec((chans, Q), at),
                pl.BlockSpec((STATE, Q), at),
                pl.BlockSpec((STATE, Q), swapped),
                pl.BlockSpec((padded, Q), at),
                pl.BlockSpec((8, Q), at),
                pl.BlockSpec((1, Q), at),
                pl.BlockSpec((Q, 1), lambda k, p: (seq * count + count - 1 - k, 0)),
                pl.BlockSpec(par.shape, whole),
                pl.BlockSpec(hp.shape, whole),
                pl.BlockSpec((wide, Q), at),
                pl.BlockSpec((wide, Q), at),
                pl.BlockSpec((chans, STATE), at),
                pl.BlockSpec((chans, Q), at),
                pl.BlockSpec((chans, Q), at),
            ]
            + [pl.BlockSpec(memory_space=pl.ANY)] * len(given),
            out_specs=(
                pl.BlockSpec((chans, Q), at),
                pl.BlockSpec((2 * STATE, Q), at),
                pl.BlockSpec((padded, Q), at),
                pl.BlockSpec((wide, 8), whole),
                pl.BlockSpec((3, padded, Q), lambda k, p: (0, 0, 0)),
            ),
            scratch_shapes=[
                pltpu.VMEM((chans, STATE), F32),
                pltpu.VMEM((6, wide, Q), F32),
                pltpu.VMEM((wide, Q), F32),
                pltpu.VMEM((8, Q), F32),
                pltpu.VMEM((chans, Q), BF16),
                pltpu.VMEM((chans, Q), BF16),
                pltpu.VMEM((5, wide, Q), F32),
            ],
        ),
        input_output_aliases={1 + len(args) + k: k for k in range(len(given))},
        compiler_params=params(58),
        cost_estimate=BRIEF,
    )(place, *args, *given)


def block_masks(segs, seqs):
    s = segs.reshape(seqs, -1)
    length = s.shape[1]
    rows = []
    for k in (1, 2, 3):
        old = jnp.pad(s, ((0, 0), (k, 0)), constant_values=-1)[:, :length]
        rows.append(old == s)
    b = s.reshape(seqs, length // Q, Q)
    ends = b[:, :, -1:]
    before = jnp.concatenate([jnp.full((seqs, 1, 1), -1, s.dtype), ends[:, :-1]], axis=1)
    rows += [b == before, b == ends, jnp.broadcast_to(ends == before, b.shape)]
    rows = [r.reshape(1, -1).astype(F32) for r in rows]
    return jnp.concatenate(rows + [jnp.zeros((2, segs.shape[0]), F32)], axis=0)


def local(
    hidden, segment_ids, cotangent, w_zx, w_dt, w_bc, w_out, conv_x, conv_bias_x, conv_bc, conv_bias_bc,
    dt_bias, a_log, d_skip, pre_gain, gate_gain,
):
    n_dp, n_t = lax.axis_size("dp"), lax.axis_size("tensor")
    t_index = lax.axis_index("tensor")
    ring = Ring(n_dp)
    core = ring.core
    mine, width = hidden.shape
    inner_here = w_zx.shape[2]
    chans = inner_here // 2
    heads = w_dt.shape[1] // 2
    padded = max(16, heads)
    wide = chans + 2 * STATE
    inner_all = inner_here * n_t
    dd = 2 * w_zx.shape[1]

    def tensor_sum(v):
        if n_t == 2:
            return v + lax.ppermute(v, "tensor", [(0, 1), (1, 0)])
        return lax.psum(v, "tensor")

    def over_tensor(v):
        if n_t == 2:
            return v.astype(F32) + lax.ppermute(v, "tensor", [(0, 1), (1, 0)]).astype(F32)
        return lax.psum(v.astype(F32), "tensor")

    def pick(v, which, axis=0):
        size = v.shape[axis] // 2
        return lax.dynamic_slice_in_dim(v, which * size, size, axis)

    def in_order(own, other, axis):
        return jnp.where(
            core == 0, jnp.concatenate([own, other], axis), jnp.concatenate([other, own], axis)
        )

    pad_dt = lambda v: jnp.pad(v, ((0, 0), (0, STATE - heads)))
    small = jnp.concatenate([w_bc, pad_dt(w_dt[:, :heads]), pad_dt(w_dt[:, heads:])], axis=1)
    zx_other = ring.swap(w_zx)
    small_other = ring.swap(small)
    place = core.reshape(1).astype(jnp.int32)
    ux = prep_x(place, w_zx, zx_other, small, small_other, padded)
    cut = chans // 2
    gx = Gather(ring, ux, "both", cut)
    gx.step()

    hiddens = [hidden, ring.swap(after(hidden, ux))]

    def norm(h):
        h = h.astype(F32)
        return (h * lax.rsqrt(jnp.mean(h * h, -1, keepdims=True) + EPS) * pre_gain).astype(BF16)

    normed = [norm(h) for h in hiddens]
    segs = jnp.concatenate([segment_ids, ring.swap(after(segment_ids, ux))])
    masks = block_masks(segs, 2)
    segr, segc = segs[None, :], segs[:, None]
    offs = ring.offsets(dd)
    table = ring.table()

    def own_chans(v):
        return pick(v, core, v.ndim - 1)

    taps = jnp.concatenate([own_chans(conv_x), conv_bc], axis=1)
    biases = jnp.concatenate([own_chans(conv_bias_x), conv_bias_bc])
    skips = jnp.repeat(own_chans(d_skip), HEAD)
    par = jnp.concatenate(
        [taps, biases[None], jnp.pad(skips, (0, 2 * STATE))[None], jnp.zeros((2, wide), F32)], axis=0
    ).T
    a_own = -jnp.exp(own_chans(a_log))
    hp = jnp.stack([own_chans(dt_bias), a_own, own_chans(d_skip)], axis=1)
    hp = jnp.pad(hp, ((0, padded - heads), (0, 5)))
    gain = own_chans(gate_gain)[:, None]

    out_other = ring.swap(after(w_out, ux))
    uz, uo = prep_zo(place, w_zx, zx_other, w_out, out_other)
    cots = [cotangent, ring.swap(after(cotangent, uz))]

    gx.step()
    gx.step()
    third = gx.newest()
    gx.finish()
    gz = Gather(ring, after(uz, *third), "right")
    gz.step()

    blocks = gx.blocks()
    bc_own, dtr = two_projections(
        Weight(blocks, chans, STATE, cut), Weight(blocks, chans + STATE, padded, cut), normed, offs
    )
    bc_other = ring.swap(bc_own)
    xr = plain_projection(Weight(blocks, 0, chans, cut), normed, after(offs, bc_own))
    gz.r[-1], gz.l[-1] = after(gz.r[-1], xr), after(gz.l[-1], xr)
    go = Gather(ring, after(uo, *gz.newest()), "left")
    go.step()
    scan_args = (bc_own, bc_other, dtr, masks, segr, segc, par, hp)
    ahead = gz.newest()
    gz.step()
    half = scan_forward(place, after(xr, *ahead), *scan_args, heads, 2, 0)
    gz.r[-1], gz.l[-1] = after(gz.r[-1], half[0]), after(gz.l[-1], half[0])
    ahead = gz.newest()
    gz.step()
    y, xa, u, s_in = scan_forward(place, after(xr, *ahead), *scan_args, heads, 2, 1, half)
    gz.r[-1] = after(gz.r[-1], y)
    ahead = gz.newest()
    gz.finish()
    go.r[-1], go.l[-1] = after(go.r[-1], *ahead), after(go.l[-1], *ahead)
    go.step()
    go.step()
    z, squares = gate_projection(Weight(gz.blocks(), 0, chans), normed, after(offs, y, *gz.last), y)
    go.finish()

    def group_sum(v):
        return tensor_sum(v + ring.swap(jnp.concatenate([v[:, mine:], v[:, :mine]], axis=1)))

    total_sq = group_sum(squares)
    s = lax.rsqrt(total_sq / inner_all + EPS)
    ynt = (y * (z * sigmoid(z)) * s * gain).astype(BF16)
    ro = Scatter(ring, table, ynt, cots, dd, "right")

    weight_o = Weight(go.blocks(), 0, chans)
    dyn, q = back_projection(weight_o, cots, after(offs, *ro.out), y, z, gain)
    q_total = group_sum(q)
    out_own, out_rest = back([(weight_o, after(ynt, q))], offs, width)
    sent = ro.step(out_own)
    out_came = ring.swap(out_rest)
    dzt, dyt, dgain = gate_back(inner_all, after(dyn, *sent), y, z, s, q_total, gain)
    rz = Scatter(ring, table, dzt, normed, dd, "left")
    out_own = after(out_own.astype(F32) + out_came.astype(F32), *rz.out).astype(BF16)

    scan_args = (*scan_args, xa, u, s_in)
    first = scan_backward(
        place, xr, *scan_args, after(dyt, *rz.out, out_own), y, heads, 2, 0
    )
    sent_o = ro.step(first[3])
    sent_z = rz.step(*sent_o)
    second = scan_backward(
        place, xr, *scan_args, after(dyt, *sent_o, *sent_z), y, heads, 2, 1, first[:3]
    )
    dxt, dbc, ddt = second[:3]
    dbc_low = dbc.astype(BF16)
    dbc_came = ring.swap(dbc_low[:, mine:])
    rx = Scatter(ring, table, dxt, normed, dd, "both")
    sent_o = ro.step(*rx.out)
    sent_z = rz.step(*sent_o)

    quarter = 2 * STATE // (2 * n_t)
    dbc_own = after(dbc_low[:, :mine].astype(F32) + dbc_came.astype(F32), *sent_z).astype(BF16)
    dbc_own = over_tensor(dbc_own).astype(BF16)
    dn_z = back([(Weight(gz.blocks(), 0, chans), dzt)], after(offs, *sent_z), width)
    sent_x = rx.step(dn_z[0])
    dbc_all = jnp.concatenate([dbc_own, ring.swap(after(dbc_own, dn_z[0]))], axis=1)
    keep_o, give_o = ro.finish(*sent_x)
    sent_z = rz.step(keep_o)
    ddt_low = ddt.astype(BF16)
    bc_here = lax.dynamic_slice_in_dim(dbc_all, core * STATE + t_index * quarter, quarter, 0)
    bc_full = jnp.zeros((STATE, 2 * mine), BF16)
    bc_full = lax.dynamic_update_slice_in_dim(bc_full, bc_here, t_index * quarter, 0)
    dn_own, dn_rest, pre_part = back(
        [
            (Weight(blocks, 0, chans, cut), dxt),
            (Weight(blocks, chans, STATE, cut), bc_full),
            (Weight(blocks, chans + STATE, padded, cut), ddt_low),
        ],
        after(offs, *sent_z), width, dn_z, hiddens,
    )
    dn_came = ring.swap(dn_rest)
    sent_x = rx.step(dn_own)

    cg = (first[3] + second[3]).T[:5]
    hg = jnp.sum(first[4] + second[4], 2)[:, :heads]
    hg = hg * jnp.stack([jnp.ones_like(a_own), a_own, jnp.ones_like(a_own)])
    split = jnp.concatenate([cg[:, :chans].reshape(-1), dgain[:, 0], hg.reshape(-1)])
    shared = jnp.concatenate([cg[:, chans:].reshape(-1), pre_part[0]])
    n_split, n_shared = split.shape[0], shared.shape[0]
    lines = -(-(n_split + n_shared) // (16 * dd)) * 16
    common = jnp.concatenate([split, shared])
    common = jnp.pad(common, (0, lines * dd - common.shape[0])).reshape(lines, dd)
    bc_ours = lax.dynamic_slice_in_dim(dbc_all, (t_index * 2 + core) * quarter, quarter, 0)
    small_rows = after(jnp.concatenate([bc_ours, ddt_low], axis=0), *sent_x)
    letters = messages(ring, table, small_rows, normed, common)
    dn_own = after(dn_own.astype(F32) + dn_came.astype(F32), letters[0]).astype(BF16)
    if n_t == 2:
        dn_other = lax.ppermute(dn_own, "tensor", [(0, 1), (1, 0)])
    else:
        dn_other = (lax.psum(dn_own.astype(F32), "tensor") - dn_own.astype(F32)).astype(BF16)
    answers = [lax.ppermute(after(letters[k], dn_own), "dp", ring.ahead(k)) for k in range(1, ring.n)]
    keep_z, give_z = rz.finish(dn_own)
    sent_x = rx.step(keep_z)
    grad_out = in_order(keep_o, ring.swap(give_o), 0)
    output = (hidden.astype(F32) + over_tensor(out_own)).astype(BF16)
    sums = after(letters[0], *sent_x).astype(F32)
    for answer in answers:
        sums = sums + answer.astype(F32)
    sum_small, common = sums[: quarter + padded], sums[quarter + padded :].reshape(-1)
    split, shared = common[:n_split], common[n_split : n_split + n_shared]
    split_other = ring.swap(split)
    shared = tensor_sum(shared + ring.swap(shared))

    def parts(v):
        a = v[: 5 * chans].reshape(5, chans)
        b = v[5 * chans : 6 * chans]
        c = v[6 * chans :].reshape(3, heads)
        return a, b, c

    (a0, b0, c0), (a1, b1, c1) = parts(split), parts(split_other)
    cg_x = in_order(a0, a1, 1)
    grad_gate = in_order(b0, b1, 0)
    hg = in_order(c0, c1, 1)
    cg_bc = shared[: 5 * 2 * STATE].reshape(5, 2 * STATE)
    grad_pre = shared[5 * 2 * STATE :]

    grad_hidden = norm_back(dn_own, after(dn_other, *sent_x), hidden, cotangent, pre_gain[None])
    keep_x, give_x = rx.finish(grad_hidden)
    grad_zx = turn(place, keep_z, ring.swap(give_z), keep_x, ring.swap(give_x))
    ks = pick(sum_small, core, 1)
    os = ring.swap(pick(sum_small, 1 - core, 1))
    grad_bc = in_order(ks[:quarter], os[:quarter], 0).T
    grad_dt = in_order(ks[quarter : quarter + heads], os[quarter : quarter + heads], 0).T
    return (
        output, grad_hidden, grad_zx, grad_dt, grad_bc, grad_out, cg_x[:4], cg_x[4], cg_bc[:4], cg_bc[4],
        hg[0], hg[1], hg[2], grad_pre, grad_gate,
    )


def solution(mesh):
    in_specs = (
        P("dp", None), P("dp"), P("dp", None), P(None, "dp", "tensor"), P("dp", "tensor"), P("dp", None),
        P("tensor", "dp"), P(None, "tensor"), P("tensor"), P(), P(), P("tensor"), P("tensor"), P("tensor"),
        P(), P("tensor"),
    )
    out_specs = (
        P("dp", None), P("dp", None), P(None, "dp", "tensor"), P("dp", "tensor"), P("dp", "tensor"),
        P("tensor", "dp"), P(None, "tensor"), P("tensor"), P(), P(), P("tensor"), P("tensor"), P("tensor"),
        P(), P("tensor"),
    )
    return jax.shard_map(local, mesh=mesh, in_specs=in_specs, out_specs=out_specs, check_vma=False)
```

```python
import functools

import jax
import jax.numpy as jnp
from jax import lax
from jax.experimental import pallas as pl
from jax.experimental.pallas import tpu as pltpu
from jax.sharding import PartitionSpec as P

EPS = 1e-05
Q = 128
NEG = -1e30
F32 = jnp.float32
BF16 = jnp.bfloat16
HIGH = lax.Precision.HIGHEST
MIB = 1024 * 1024
HEAD = 64
STATE = 128


LONG = pl.CostEstimate(flops=30_000_000_000, bytes_accessed=1, transcendentals=0)
BRIEF = pl.CostEstimate(flops=1, bytes_accessed=1, transcendentals=0)


def dot(a, b, dims, precision=None):
    return lax.dot_general(a, b, (dims, ((), ())), precision=precision, preferred_element_type=F32)


def params(mib):
    return pltpu.CompilerParams(vmem_limit_bytes=mib * MIB)


def after(value, *others):
    return lax.optimization_barrier((value, others))[0]


def ring_order(chips):
    if chips == 8:
        return [0, 2, 4, 6, 7, 5, 3, 1]
    half = chips // 2
    return list(range(half)) + list(range(chips - 1, half - 1, -1))


class Ring:
    def __init__(self, n_dp):
        self.n = n_dp // 2
        self.order = ring_order(self.n)
        place = [0] * self.n
        for position, chip in enumerate(self.order):
            place[chip] = position
        me = lax.axis_index("dp")
        self.core = me % 2
        self.mine = me // 2
        self.pos = jnp.asarray(place, jnp.int32)[self.mine]
        self.right = self.perm(1)
        self.left = self.perm(-1)
        self.full = self.n // 2 - 1

    def perm(self, step):
        pairs = []
        for p in range(self.n):
            for c in range(2):
                pairs.append((self.order[p] * 2 + c, self.order[(p + step) % self.n] * 2 + c))
        return pairs

    def table(self):
        table = [[self.order[(p + s) % self.n] for s in range(self.n)] for p in range(self.n)]
        row = lax.dynamic_index_in_dim(jnp.asarray(table, jnp.int32), self.pos, 0, keepdims=False)
        return jnp.concatenate([row, self.core.reshape(1).astype(jnp.int32)])

    def offsets(self, dd):
        steps = [0] + [-k for k in range(1, self.full + 1)] + list(range(1, self.full + 1)) + [self.n // 2]
        table = [[self.order[(p + s) % self.n] * dd for s in steps] for p in range(self.n)]
        return lax.dynamic_index_in_dim(jnp.asarray(table, jnp.int32), self.pos, 0, keepdims=False)

    def go_right(self, v):
        return lax.ppermute(v, "dp", self.right)

    def go_left(self, v):
        return lax.ppermute(v, "dp", self.left)

    def swap(self, v):
        return lax.ppermute(v, "dp", [(i, i ^ 1) for i in range(2 * self.n)])

    def halving(self, v, total):
        dist = self.n // 2
        while dist:
            pairs = [(i, i ^ (2 * dist)) for i in range(2 * self.n)]
            keep, give = self.halves(v, (self.mine // dist) % 2)
            got = yield lax.ppermute(give.astype(BF16), "dp", pairs), lax.ppermute(total, "dp", pairs)
            v, total = keep + got[0].astype(F32), total + got[1]
            dist //= 2
        yield v, total

    def halves(self, v, bit):
        size = v.shape[1] // 2
        return (
            lax.dynamic_slice_in_dim(v, bit * size, size, 1),
            lax.dynamic_slice_in_dim(v, (1 - bit) * size, size, 1),
        )


class Gather:
    def __init__(self, ring, unit, far, cut=None):
        self.ring, self.far, self.cut = ring, far, cut
        self.r, self.l = [unit], [unit]
        self.last = []

    def right(self, *others):
        if len(self.r) <= self.ring.full:
            v = after(self.r[-1], *others) if others else self.r[-1]
            self.r.append(self.ring.go_right(v))
        return self.r[-1]

    def left(self, *others):
        if len(self.l) <= self.ring.full:
            v = after(self.l[-1], *others) if others else self.l[-1]
            self.l.append(self.ring.go_left(v))
        return self.l[-1]

    def step(self, *others):
        return self.right(*others), self.left(*others)

    def newest(self):
        return self.r[-1], self.l[-1]

    def finish(self, *others):
        while len(self.r) <= self.ring.full:
            self.right()
        while len(self.l) <= self.ring.full:
            self.left()
        r, l, cut = self.r[-1], self.l[-1], self.cut
        if others:
            r, l = after(r, *others), after(l, *others)
        if self.far == "both":
            self.last = [self.ring.go_right(r[:cut]), self.ring.go_left(l[cut:])]
        elif self.far == "right":
            self.last = [self.ring.go_right(r)]
        else:
            self.last = [self.ring.go_left(l)]
        return self.last

    def blocks(self):
        return self.r + self.l[1:] + self.last


def both_parts(vt, own, other):
    half = own.shape[0]
    return dot(vt[:, :half], own[...], (((1,), (0,)))) + dot(vt[:, half:], other[...], (((1,), (0,))))


def terms_kernel(table, vt, own, other, *outs):
    total = both_parts(vt, own, other).astype(BF16)
    top, bottom = outs[:2]
    half = top.shape[0]
    s = pl.program_id(0)

    @pl.when(s == 0)
    def _():
        top[...] = total[:half]
        bottom[...] = total[half:]

    for k, out in enumerate(outs[2:]):

        @pl.when((s == 1 + 2 * k) | (s == 2 + 2 * k))
        def _():
            out[0] = total


def terms(ring, table, vt, acts, dd):
    rows, tokens = vt.shape
    n, full = ring.n, ring.full
    half = n // 2

    def step(s):
        j = full - (s - 1) // 2
        at = jnp.where(s == 0, half, jnp.where(s % 2 == 1, j, n - j))
        return jnp.where(s == n - 1, 0, at)

    column = pl.BlockSpec((tokens // 2, dd), lambda s, t: (0, t[step(s)]))
    part = pl.BlockSpec((rows // 2, dd), lambda s, t: (0, 0))
    pair = lambda k: pl.BlockSpec((1, rows, dd), lambda s, t: (jnp.clip(s - 1 - 2 * k, 0, 1), 0, 0))
    single = pl.BlockSpec((1, rows, dd), lambda s, t: (0, 0, 0))
    return pl.pallas_call(
        terms_kernel,
        out_shape=tuple([jax.ShapeDtypeStruct((rows // 2, dd), BF16)] * 2)
        + tuple([jax.ShapeDtypeStruct((2, rows, dd), BF16)] * full)
        + (jax.ShapeDtypeStruct((1, rows, dd), BF16),),
        grid_spec=pltpu.PrefetchScalarGridSpec(
            num_scalar_prefetch=1,
            grid=(n,),
            in_specs=[pl.BlockSpec((rows, tokens), lambda s, t: (0, 0)), column, column],
            out_specs=tuple([part, part] + [pair(k) for k in range(full)] + [single]),
        ),
        compiler_params=params(24),
        cost_estimate=LONG,
    )(table, vt, *acts)


def first_add_kernel(own, r, l, out_r, out_l):
    half = r.shape[0]
    out_r[:half] = (own[0, :half].astype(F32) + r[...].astype(F32)).astype(BF16)
    out_r[half:] = own[0, half:]
    out_l[:half] = own[1, :half]
    out_l[half:] = (own[1, half:].astype(F32) + l[...].astype(F32)).astype(BF16)


def add_kernel(own, r, l, out_r, out_l):
    out_r[...] = (own[0].astype(F32) + r[...].astype(F32)).astype(BF16)
    out_l[...] = (own[1].astype(F32) + l[...].astype(F32)).astype(BF16)


def last_add_kernel(place, own, r, l, keep, give):
    total = own[0].astype(F32) + r[...].astype(F32) + l[...].astype(F32)
    dd = keep.shape[1]
    low, high = total[:, :dd], total[:, dd:]
    keep[...] = jnp.where(place[0] == 0, low, high)
    give[...] = jnp.where(place[0] == 0, high, low)


class Scatter:
    def __init__(self, ring, parts):
        self.ring = ring
        top, bottom, *self.own = parts
        self.left_to_do = ring.full
        self.send(top, bottom)

    def send(self, r, l):
        self.out = (r, l)
        self.got = (self.ring.go_right(r), self.ring.go_left(l))

    def step(self, *others):
        if not self.left_to_do:
            return self.out
        j = self.left_to_do
        self.left_to_do -= 1
        own = self.own[self.ring.full - j]
        rows, dd = own.shape[1:]
        got = after(self.got, *others) if others else self.got
        whole = lambda shape: pl.BlockSpec(shape, lambda i: (0,) * len(shape))
        out = pl.pallas_call(
            first_add_kernel if j == self.ring.full else add_kernel,
            grid=(1,),
            out_shape=(jax.ShapeDtypeStruct((rows, dd), BF16),) * 2,
            in_specs=[whole(v.shape) for v in (own, *got)],
            out_specs=(whole((rows, dd)),) * 2,
            compiler_params=params(16),
            cost_estimate=BRIEF,
        )(own, *got)
        self.send(*out)
        return self.out

    def finish(self, place, *others, cost=BRIEF):
        while self.left_to_do:
            self.step()
        own = self.own[-1]
        rows, dd = own.shape[1:]
        got = after(self.got, *others) if others else self.got
        whole = lambda shape: pl.BlockSpec(shape, lambda i, p: (0,) * len(shape))
        return pl.pallas_call(
            last_add_kernel,
            out_shape=(jax.ShapeDtypeStruct((rows, dd // 2), F32),) * 2,
            grid_spec=pltpu.PrefetchScalarGridSpec(
                num_scalar_prefetch=1,
                grid=(1,),
                in_specs=[whole(v.shape) for v in (own, *got)],
                out_specs=(whole((rows, dd // 2)),) * 2,
            ),
            compiler_params=params(16),
            cost_estimate=cost,
        )(place, own, *got)


def prep_x_kernel(place, own, other, small_own, small_other, out):
    core = place[0]
    dd = own.shape[1]
    chans = own.shape[2] // 2
    padded = out.shape[0] - chans - STATE
    for b in range(2):
        lanes = slice(b * dd, (b + 1) * dd)
        near = core == b
        src = jnp.where(near, own[0], other[0])
        src = jnp.where(core == 0, src[:, :chans], src[:, chans:])
        out[:chans, lanes] = src.T
        small = jnp.where(near, small_own[...], small_other[...])
        states = jnp.where(core == 0, small[:, :STATE], small[:, STATE : 2 * STATE])
        out[chans : chans + STATE, lanes] = states.T
        steps = jnp.where(core == 0, small[:, 2 * STATE : 3 * STATE], small[:, 3 * STATE :])
        out[chans + STATE :, lanes] = steps.T[:padded]


def prep_x(place, own, other, small_own, small_other, padded):
    _, dd, inner = own.shape
    rows = inner // 2 + STATE + padded
    return pl.pallas_call(
        prep_x_kernel,
        out_shape=jax.ShapeDtypeStruct((rows, 2 * dd), BF16),
        grid_spec=pltpu.PrefetchScalarGridSpec(
            num_scalar_prefetch=1,
            grid=(1,),
            in_specs=[pl.BlockSpec((1, dd, inner), lambda i, p: (1, 0, 0))] * 2
            + [pl.BlockSpec((dd, 4 * STATE), lambda i, p: (0, 0))] * 2,
            out_specs=pl.BlockSpec((rows, 2 * dd), lambda i, p: (0, 0)),
        ),
        compiler_params=params(12),
        cost_estimate=BRIEF,
    )(place, own, other, small_own, small_other)


def prep_zo_kernel(place, own, other, out_own, out_other, z, o):
    core = place[0]
    dd = own.shape[1]
    chans = own.shape[2] // 2
    for b in range(2):
        lanes = slice(b * dd, (b + 1) * dd)
        near = core == b
        src = jnp.where(near, own[0], other[0])
        src = jnp.where(core == 0, src[:, :chans], src[:, chans:])
        z[:, lanes] = src.T
        src = jnp.where(near, out_own[...], out_other[...])
        o[:, lanes] = jnp.where(core == 0, src[:chans], src[chans:])


def prep_zo(place, own, other, out_own, out_other):
    _, dd, inner = own.shape
    shape = (inner // 2, 2 * dd)
    return pl.pallas_call(
        prep_zo_kernel,
        out_shape=(jax.ShapeDtypeStruct(shape, BF16),) * 2,
        grid_spec=pltpu.PrefetchScalarGridSpec(
            num_scalar_prefetch=1,
            grid=(1,),
            in_specs=[pl.BlockSpec((1, dd, inner), lambda i, p: (0, 0, 0))] * 2
            + [pl.BlockSpec((inner, dd), lambda i, p: (0, 0))] * 2,
            out_specs=(pl.BlockSpec(shape, lambda i, p: (0, 0)),) * 2,
        ),
        compiler_params=params(12),
        cost_estimate=BRIEF,
    )(place, own, other, out_own, out_other)


class Weight:
    def __init__(self, blocks, first, rows, cut=None):
        self.args, self.specs, self.plan = [], [], []
        self.rows, self.dd = rows, blocks[0].shape[1]

        def view(array, start, size):
            index = start // size
            self.args.append(array)
            self.specs.append(pl.BlockSpec((size, self.dd), lambda i, o, index=index: (index, 0)))

        whole = blocks if cut is None else blocks[:-2]
        for block in whole:
            view(block, first, rows)
            self.plan.append(1)
        if cut is not None:
            pieces = 0
            if first < cut:
                view(blocks[-2], first, min(rows, cut - first))
                pieces += 1
            if first + rows > cut:
                start = max(first, cut)
                view(blocks[-1], start - cut, first + rows - start)
                pieces += 1
            self.plan.append(pieces)

    def read(self, refs):
        at, out = 0, []
        for pieces in self.plan:
            part = [r[...] for r in refs[at : at + pieces]]
            out.append(part[0] if pieces == 1 else jnp.concatenate(part, axis=0))
            at += pieces
        return out


def projected(weight, refs, act, offs):
    total = None
    for b, w in enumerate(weight.read(refs)):
        off = pl.multiple_of(offs[b], weight.dd)
        part = dot(w, act[:, pl.ds(off, weight.dd)], (((1,), (1,))))
        total = part if total is None else total + part
    return total


def projection(body, weight, acts, offs, extra, extra_specs, out_shape, out_specs, mib=40):
    tile, width = acts[0].shape
    tokens = 2 * tile
    n = len(weight.args)

    def kernel(offs, *refs):
        for k in range(2):

            @pl.when(pl.program_id(0) == k)
            def _():
                acc = projected(weight, refs[:n], refs[n + k], offs)
                body(acc, refs[n + 2 : n + 2 + len(extra)], refs[n + 2 + len(extra) :])

    return pl.pallas_call(
        kernel,
        out_shape=out_shape,
        grid_spec=pltpu.PrefetchScalarGridSpec(
            num_scalar_prefetch=1,
            grid=(tokens // tile,),
            in_specs=weight.specs + [pl.BlockSpec((tile, width), lambda i, o: (0, 0))] * 2 + extra_specs,
            out_specs=out_specs,
        ),
        compiler_params=params(mib),
        cost_estimate=LONG,
    )(offs, *weight.args, *acts, *extra)


def x_projection(weight, chans, acts, offs):
    tile = acts[0].shape[0]
    parts = (chans, STATE, weight.rows - chans - STATE)

    def body(acc, extra, outs):
        at = 0
        for out, rows in zip(outs, parts):
            out[...] = acc[at : at + rows]
            at += rows

    return projection(
        body, weight, acts, offs, (), [],
        tuple(jax.ShapeDtypeStruct((rows, 2 * tile), F32) for rows in parts),
        tuple(pl.BlockSpec((rows, tile), lambda i, o: (0, i)) for rows in parts),
    )


def sigmoid(v):
    return 0.5 * jnp.tanh(0.5 * v) + 0.5


def gate_projection(weight, acts, offs, y):
    rows, tokens = y.shape
    tile = tokens // 2

    def body(z, extra, outs):
        outs[0][...] = z
        g = extra[0][...] * (z * sigmoid(z))
        outs[1][...] = jnp.sum(g * g, axis=0, keepdims=True)

    wide = pl.BlockSpec((rows, tile), lambda i, o: (0, i))
    line = pl.BlockSpec((1, tile), lambda i, o: (0, i))
    return projection(
        body, weight, acts, offs, (y,), [wide],
        (jax.ShapeDtypeStruct((rows, tokens), F32), jax.ShapeDtypeStruct((1, tokens), F32)),
        (wide, line), 58,
    )


def back_projection(weight, acts, offs, y, z, gain):
    rows, tokens = y.shape
    tile = tokens // 2

    def body(dyn, extra, outs):
        y, z, gain = extra
        outs[0][...] = dyn
        zv = z[...]
        g = y[...] * (zv * sigmoid(zv))
        outs[1][...] = jnp.sum(dyn * gain[...] * g, axis=0, keepdims=True)

    wide = pl.BlockSpec((rows, tile), lambda i, o: (0, i))
    line = pl.BlockSpec((1, tile), lambda i, o: (0, i))
    return projection(
        body, weight, acts, offs, (y, z, gain),
        [wide, wide, pl.BlockSpec((rows, 1), lambda i, o: (0, 0))],
        (jax.ShapeDtypeStruct((rows, tokens), F32), jax.ShapeDtypeStruct((1, tokens), F32)),
        (wide, line),
    )


def back(groups, offs, width, parts=1, part=0, hiddens=None, mib=40):
    dd = groups[0][0].dd
    size = groups[0][1].shape[1] // (2 * parts)
    args, specs = [], []
    flops = 0
    for weight, vt in groups:
        args += weight.args + [vt, vt]
        specs += weight.specs
        specs += [pl.BlockSpec((vt.shape[0], size), lambda i, o, p=p: (0, p)) for p in (part, parts + part)]
    out_spec = pl.BlockSpec((size, width), lambda i, o: (0, 0))
    shapes = [jax.ShapeDtypeStruct((size, width), BF16)] * 2
    out_specs = [out_spec, out_spec]
    if hiddens is not None:
        args += list(hiddens)
        specs += [pl.BlockSpec((size, width), lambda i, o: (part, 0))] * 2
        shapes.append(jax.ShapeDtypeStruct((1, width), F32))
        out_specs.append(pl.BlockSpec((1, width), lambda i, o: (0, 0)))

    def kernel(offs, *refs):
        outs = refs[len(args) :]
        at, terms = 0, []
        for weight, _ in groups:
            n = len(weight.args)
            v = jnp.concatenate([refs[at + n][...].T, refs[at + n + 1][...].T], axis=0)
            terms.append((v, weight.read(refs[at : at + n])))
            at += n + 2
        scales = []
        if hiddens is not None:
            for h in refs[len(args) - 2 : len(args)]:
                v = h[...].astype(F32)
                scales.append(lax.rsqrt(jnp.mean(v * v, axis=1, keepdims=True) + EPS))
        for b in range(len(terms[0][1])):
            off = pl.multiple_of(offs[b], dd)
            along = None
            total = None
            for v, blocks in terms:
                term = dot(v, blocks[b], (((1,), (0,))))
                total = term if total is None else total + term
            for k in range(2):
                here = total[k * size : (k + 1) * size]
                outs[k][:, pl.ds(off, dd)] = here.astype(BF16)
                if hiddens is not None:
                    h = refs[len(args) - 2 + k][:, pl.ds(off, dd)].astype(F32)
                    line = jnp.sum(here * (h * scales[k]), axis=0, keepdims=True)
                    along = line if along is None else along + line
            if hiddens is not None:
                outs[2][:, pl.ds(off, dd)] = along

    return pl.pallas_call(
        kernel,
        out_shape=tuple(shapes),
        grid_spec=pltpu.PrefetchScalarGridSpec(
            num_scalar_prefetch=1, grid=(1,), in_specs=specs, out_specs=tuple(out_specs)
        ),
        compiler_params=params(mib),
        cost_estimate=LONG,
    )(offs, *args)


def whole_rows(weight, offs, width):
    def kernel(offs, *refs):
        for b, w in enumerate(weight.read(refs[:-1])):
            refs[-1][:, pl.ds(pl.multiple_of(offs[b], weight.dd), weight.dd)] = w

    return pl.pallas_call(
        kernel,
        out_shape=jax.ShapeDtypeStruct((weight.rows, width), BF16),
        grid_spec=pltpu.PrefetchScalarGridSpec(
            num_scalar_prefetch=1,
            grid=(1,),
            in_specs=weight.specs,
            out_specs=pl.BlockSpec((weight.rows, width), lambda i, o: (0, 0)),
        ),
        compiler_params=params(20),
        cost_estimate=BRIEF,
    )(offs, *weight.args)


def pre_states_kernel(place, dbc, hidden, w_own, w_other, out):
    h = hidden[...].astype(F32)
    hr = (h * lax.rsqrt(jnp.mean(h * h, axis=1, keepdims=True) + EPS)).astype(BF16)
    first = place[0] == 0
    w = jnp.concatenate(
        [jnp.where(first, w_own[...], w_other[...]), jnp.where(first, w_other[...], w_own[...])], axis=0
    )
    out[...] = jnp.sum(w.astype(F32) * dot(dbc[...], hr, (((1,), (0,)))), axis=0, keepdims=True)


def pre_states(place, dbc, hidden, w_own, w_other):
    return pl.pallas_call(
        pre_states_kernel,
        out_shape=jax.ShapeDtypeStruct((1, hidden.shape[1]), F32),
        grid_spec=pltpu.PrefetchScalarGridSpec(
            num_scalar_prefetch=1,
            grid=(1,),
            in_specs=[pl.BlockSpec(v.shape, lambda i, p: (0, 0)) for v in (dbc, hidden, w_own, w_other)],
            out_specs=pl.BlockSpec((1, hidden.shape[1]), lambda i, p: (0, 0)),
        ),
        compiler_params=params(30),
        cost_estimate=BRIEF,
    )(place, dbc, hidden, w_own, w_other)


def small_terms_kernel(core_place, states, steps, own, other, out):
    m = states.shape[0]
    k = steps.shape[0]
    out[:m] = dot(states[...], own[...], (((1,), (0,))))
    both = both_parts(steps, own, other)
    first = core_place[0] == 0
    out[m : m + k] = jnp.where(first, both, 0.0)
    out[m + k :] = jnp.where(first, 0.0, both)


def small_terms(place, states, steps, acts):
    m, k = states.shape[0], steps.shape[0]
    width = acts[0].shape[1]
    whole = lambda i, p: (0, 0)
    return pl.pallas_call(
        small_terms_kernel,
        out_shape=jax.ShapeDtypeStruct((m + 2 * k, width), F32),
        grid_spec=pltpu.PrefetchScalarGridSpec(
            num_scalar_prefetch=1,
            grid=(1,),
            in_specs=[pl.BlockSpec(v.shape, whole) for v in (states, steps, *acts)],
            out_specs=pl.BlockSpec((m + 2 * k, width), whole),
        ),
        compiler_params=params(20),
        cost_estimate=BRIEF,
    )(place, states, steps, *acts)


def output_kernel(late_own, late_came, own, came, hidden, out):
    late = pl.program_id(0) >= pl.num_programs(0) // 2
    rest = jnp.where(late, late_own[...].astype(F32), own[...].astype(F32))
    rest = rest + jnp.where(late, late_came[...].astype(F32), came[...].astype(F32))
    out[...] = (hidden[...].astype(F32) + rest).astype(BF16)


def residual(late, early, hidden):
    rows, width = hidden.shape
    tile = 128
    half = rows // tile // 2
    block = pl.BlockSpec((tile, width), lambda i: (i, 0))
    first = pl.BlockSpec((tile, width), lambda i: (jnp.minimum(i, half - 1), 0))
    second = pl.BlockSpec((tile, width), lambda i: (jnp.maximum(i - half, 0), 0))
    return pl.pallas_call(
        output_kernel,
        out_shape=jax.ShapeDtypeStruct(hidden.shape, BF16),
        grid=(rows // tile,),
        in_specs=[second, second, first, first, block],
        out_specs=block,
        compiler_params=params(20),
        cost_estimate=LONG,
    )(*late, *early, hidden)


def norm_back_kernel(place, late_own, late_came, own, came, hidden, cot, gain, dbc, w_own, w_other, out):
    h = hidden[...].astype(F32)
    width = h.shape[1]
    r = lax.rsqrt(jnp.mean(h * h, axis=1, keepdims=True) + EPS)
    low, high = dbc[:STATE, :], dbc[STATE:, :]
    first = place[0] == 0
    dn = dot(jnp.where(first, low, high), w_own[...], (((0,), (0,))))
    dn = dn + dot(jnp.where(first, high, low), w_other[...], (((0,), (0,))))
    late = pl.program_id(0) >= pl.num_programs(0) // 2
    rest = jnp.where(late, late_own[...].astype(F32), own[...].astype(F32))
    rest = rest + jnp.where(late, late_came[...].astype(F32), came[...].astype(F32))
    weighted = (rest + dn) * gain[...]
    along = jnp.sum(weighted * h, axis=1, keepdims=True) * (1.0 / width)
    out[...] = (weighted * r - h * (r * r * r * along) + cot[...].astype(F32)).astype(BF16)


def norm_back(place, late, early, hidden, cot, gain, dbc, w_own, w_other):
    rows, width = hidden.shape
    tile = 128
    half = rows // tile // 2
    block = pl.BlockSpec((tile, width), lambda i, p: (i, 0))
    first = pl.BlockSpec((tile, width), lambda i, p: (jnp.minimum(i, half - 1), 0))
    second = pl.BlockSpec((tile, width), lambda i, p: (jnp.maximum(i - half, 0), 0))
    whole = lambda i, p: (0, 0)
    return pl.pallas_call(
        norm_back_kernel,
        out_shape=jax.ShapeDtypeStruct(hidden.shape, BF16),
        grid_spec=pltpu.PrefetchScalarGridSpec(
            num_scalar_prefetch=1,
            grid=(rows // tile,),
            in_specs=[second, second, first, first, block, block, pl.BlockSpec((1, width), whole)]
            + [pl.BlockSpec((2 * STATE, tile), lambda i, p: (0, i))]
            + [pl.BlockSpec(w_own.shape, whole)] * 2,
            out_specs=block,
        ),
        compiler_params=params(30),
        cost_estimate=LONG,
    )(place, *late, *early, hidden, cot, gain, dbc, w_own, w_other)


def turn_kernel(place, *refs):
    out = refs[-1]
    chans = refs[0].shape[0]
    first = place[0] == 0
    for k in range(2):
        own, other = refs[2 * k][...], refs[2 * k + 1][...]
        out[k, :, :chans] = jnp.where(first, own, other).T
        out[k, :, chans:] = jnp.where(first, other, own).T


def turn(place, *parts):
    chans, dd = parts[0].shape
    return pl.pallas_call(
        turn_kernel,
        out_shape=jax.ShapeDtypeStruct((2, dd, 2 * chans), F32),
        grid_spec=pltpu.PrefetchScalarGridSpec(
            num_scalar_prefetch=1,
            grid=(1,),
            in_specs=[pl.BlockSpec((chans, dd), lambda i, p: (0, 0))] * 4,
            out_specs=pl.BlockSpec((2, dd, 2 * chans), lambda i, p: (0, 0, 0)),
        ),
        compiler_params=params(16),
        cost_estimate=BRIEF,
    )(place, *parts)


def gate_back_kernel(total, dyn, y, z, s, q, gain, dz, dy, dgain):
    zv, yv, sv = z[...], y[...], s[...]
    sig = sigmoid(zv)
    silu = zv * sig
    g = yv * silu
    scaled = dyn[...] * sv
    dgain[...] = jnp.sum(scaled * g, axis=1, keepdims=True)
    dg = scaled * gain[...] - g * (sv * sv * sv * q[...] * (1.0 / total))
    dz[...] = (dg * yv * (sig * (1.0 + zv * (1.0 - sig)))).astype(BF16)
    dy[...] = (dg * silu).astype(BF16)


def gate_back(total, dyn, y, z, s, q, gain):
    rows, tokens = dyn.shape
    tile = rows // 4
    wide = pl.BlockSpec((tile, tokens), lambda i: (i, 0))
    line = pl.BlockSpec((1, tokens), lambda i: (0, 0))
    return pl.pallas_call(
        functools.partial(gate_back_kernel, float(total)),
        grid=(rows // tile,),
        out_shape=(jax.ShapeDtypeStruct((rows, tokens), BF16),) * 2
        + (jax.ShapeDtypeStruct((rows, 1), F32),),
        in_specs=[wide, wide, wide, line, line, pl.BlockSpec((tile, 1), lambda i: (i, 0))],
        out_specs=(wide, wide, pl.BlockSpec((tile, 1), lambda i: (i, 0))),
        compiler_params=params(40),
        cost_estimate=BRIEF,
    )(dyn, y, z, s, q, gain)


def head_terms(raw, hp_ref):
    pre = raw + hp_ref[:, 0:1]
    small = jnp.exp(-jnp.abs(pre))
    one = 1.0 + small
    away = one - 1.0
    log1p = jnp.where(away == 0.0, small, jnp.log(one) * (small / jnp.where(away == 0.0, 1.0, away)))
    dt = jnp.maximum(pre, 0.0) + log1p
    logistic = jnp.where(pre >= 0.0, 1.0, small) / one
    rows = lax.broadcasted_iota(jnp.int32, (Q, Q), 0)
    lanes = lax.broadcasted_iota(jnp.int32, (Q, Q), 1)
    upto = (rows <= lanes).astype(F32)
    logs = dt * hp_ref[:, 1:2]
    cums = dot(logs, upto, (((1,), (0,))), HIGH)
    return dt, logistic, cums


def to_columns(cums):
    n = cums.shape[0]
    square = jnp.concatenate([cums, jnp.zeros((Q - n, Q), F32)], axis=0)
    return square.T


def pair_bias(segr_ref, segc_ref):
    rows = lax.broadcasted_iota(jnp.int32, (Q, Q), 0)
    lanes = lax.broadcasted_iota(jnp.int32, (Q, Q), 1)
    keep = (segc_ref[...] == segr_ref[...]) & (rows <= lanes)
    return jnp.where(keep, 0.0, NEG)


def state_rows(place, own, other, r0):
    at = r0 % STATE
    rows = slice(at, at + HEAD)
    return jnp.where(place[0] == r0 // STATE, own[rows, :], other[rows, :])


def fwd_kernel(
    heads, given, place, xr_ref, bco_ref, bcs_ref, dt_ref, mask_ref, segr_ref, segc_ref, par_ref, hp_ref, *rest
):
    y_ref, xa_ref, u_ref, s_ref, prev, state, parb, xt = rest[given:]
    chans = heads * HEAD
    wide = chans + 2 * STATE

    @pl.when(pl.program_id(0) == 0)
    def _():
        for k in range(6):
            parb[k] = jnp.broadcast_to(par_ref[:, k : k + 1], (wide, Q))
        prev[...] = jnp.zeros_like(prev)
        state[...] = jnp.zeros_like(state)

    lane = lax.broadcasted_iota(jnp.int32, (HEAD, Q), 1)
    m1, m2, m3 = mask_ref[0:1, :], mask_ref[1:2, :], mask_ref[2:3, :]

    def conv(r0):
        rows = slice(r0, r0 + HEAD)
        cur = xr_ref[rows, :] if r0 < chans else state_rows(place, bco_ref, bcs_ref, r0 - chans)
        old = prev[rows, :]
        u = parb[4, rows, :] + parb[3, rows, :] * cur
        u = u + parb[2, rows, :] * (m1 * pltpu.roll(jnp.where(lane >= Q - 1, old, cur), 1, 1))
        u = u + parb[1, rows, :] * (m2 * pltpu.roll(jnp.where(lane >= Q - 2, old, cur), 2, 1))
        u = u + parb[0, rows, :] * (m3 * pltpu.roll(jnp.where(lane >= Q - 3, old, cur), 3, 1))
        prev[rows, :] = cur
        u_ref[rows, :] = u
        xa = (u * (0.5 * jnp.tanh(0.5 * u) + 0.5)).astype(BF16)
        xa_ref[rows, :] = xa
        return xa

    for r0 in range(chans, wide, HEAD):
        conv(r0)
    bt = xa_ref[chans : chans + STATE, :]
    ct = xa_ref[chans + STATE : wide, :]
    mix = dot(bt.T, ct, (((1,), (0,))))
    dt, _, cums = head_terms(dt_ref[...], hp_ref)
    cols = to_columns(cums)
    bias = pair_bias(segr_ref, segc_ref)
    enter = jnp.exp(cums) * mask_ref[3:4, :]
    last = jnp.broadcast_to(cums[:, Q - 1 : Q], cums.shape)
    tail = jnp.exp(last - cums) * mask_ref[4:5, :]
    passing = jnp.exp(last) * mask_ref[5:6, :]
    s_in = state[...].astype(BF16)
    s_ref[...] = s_in
    carried = dot(s_in, ct, (((1,), (0,))))
    for h in range(heads):
        rows = slice(h * HEAD, (h + 1) * HEAD)
        xa = conv(h * HEAD).astype(F32)
        decay = jnp.exp(cums[h : h + 1, :] - cols[:, h : h + 1] + bias)
        mixing = (mix * decay).astype(BF16)
        xd = xa * dt[h : h + 1, :]
        xt[rows, :] = (xd * tail[h : h + 1, :]).astype(BF16)
        y = dot(xd.astype(BF16), mixing, (((1,), (0,))))
        y = y + enter[h : h + 1, :] * carried[rows, :] + parb[5, rows, :] * xa
        y_ref[rows, :] = y
    fresh = dot(xt[...], bt, (((1,), (1,))))
    for h in range(heads):
        rows = slice(h * HEAD, (h + 1) * HEAD)
        state[rows, :] = state[rows, :] * passing[h : h + 1, :] + fresh[rows, :]


def scan_forward(place, xr, bco, bcs, dtr, masks, segr, segc, par, hp, heads, seqs, seq, given=()):
    chans, tokens = xr.shape
    padded = dtr.shape[0]
    wide = chans + 2 * STATE
    count = tokens // seqs // Q
    at = lambda k, p: (0, seq * count + k)
    swapped = lambda k, p: (0, (seqs - 1 - seq) * count + k)
    whole = lambda k, p: (0, 0)
    args = (xr, bco, bcs, dtr, masks, segr, segc, par, hp)
    return pl.pallas_call(
        functools.partial(fwd_kernel, heads, len(given)),
        out_shape=(
            jax.ShapeDtypeStruct((chans, tokens), F32),
            jax.ShapeDtypeStruct((wide, tokens), BF16),
            jax.ShapeDtypeStruct((wide, tokens), F32),
            jax.ShapeDtypeStruct((chans, tokens), BF16),
        ),
        grid_spec=pltpu.PrefetchScalarGridSpec(
            num_scalar_prefetch=1,
            grid=(count,),
            in_specs=[
                pl.BlockSpec((chans, Q), at),
                pl.BlockSpec((STATE, Q), at),
                pl.BlockSpec((STATE, Q), swapped),
                pl.BlockSpec((padded, Q), at),
                pl.BlockSpec((8, Q), at),
                pl.BlockSpec((1, Q), at),
                pl.BlockSpec((Q, 1), lambda k, p: (seq * count + k, 0)),
                pl.BlockSpec(par.shape, whole),
                pl.BlockSpec(hp.shape, whole),
            ]
            + [pl.BlockSpec(memory_space=pl.ANY)] * len(given),
            out_specs=(
                pl.BlockSpec((chans, Q), at),
                pl.BlockSpec((wide, Q), at),
                pl.BlockSpec((wide, Q), at),
                pl.BlockSpec((chans, STATE), at),
            ),
            scratch_shapes=[
                pltpu.VMEM((wide, Q), F32),
                pltpu.VMEM((chans, STATE), F32),
                pltpu.VMEM((6, wide, Q), F32),
                pltpu.VMEM((chans, Q), BF16),
            ],
        ),
        input_output_aliases={1 + len(args) + k: k for k in range(len(given))},
        compiler_params=params(58),
        cost_estimate=LONG,
    )(place, *args, *given)


def bwd_kernel(
    heads, late, place, xr_ref, bco_ref, bcs_ref, dt_ref, mask_ref, segr_ref, segc_ref, par_ref, hp_ref, xa_ref,
    u_ref, s_ref, dy_ref, y_ref, *rest,
):
    if late:
        dx_ref, dbc_ref, ddt_ref, cgo_ref, hg_ref, dstate_out, after_out = rest[:7]
    else:
        dstate_in, after_in, next_ref = rest[:3]
        dx_ref, dbc_ref, ddt_ref, cgo_ref, hg_ref = rest[6:11]
    dstate, parb, after, nmask, xt, dye, cg_ref = rest[-7:]
    chans = heads * HEAD
    wide = chans + 2 * STATE
    seq, block = pl.program_id(0), pl.program_id(1)
    final = block == pl.num_programs(1) - 1

    @pl.when((seq == 0) & (block == 0))
    def _():
        for k in range(6):
            parb[k] = jnp.broadcast_to(par_ref[:, k : k + 1], (wide, Q))
        cg_ref[...] = jnp.zeros_like(cg_ref)
        hg_ref[...] = jnp.zeros_like(hg_ref)

    @pl.when(block == 0)
    def _():
        if late:
            dstate[...] = jnp.zeros_like(dstate)
            after[...] = jnp.zeros_like(after)
            nmask[...] = jnp.zeros_like(nmask)
        else:
            dstate[...] = dstate_in[...]
            after[...] = after_in[...]
            nmask[...] = next_ref[...]

    lane = lax.broadcasted_iota(jnp.int32, (HEAD, Q), 1)
    lane8 = lax.broadcasted_iota(jnp.int32, (8, Q), 1)
    sub8 = lax.broadcasted_iota(jnp.int32, (8, Q), 0)
    masks = mask_ref[...]
    shifted_masks = jnp.where(lane8 <= sub8, nmask[...], masks)
    nmask[...] = masks

    def conv_back(r0, dxa, out, out0):
        rows = slice(r0, r0 + HEAD)
        u = u_ref[rows, :]
        sig = 0.5 * jnp.tanh(0.5 * u) + 0.5
        dc = dxa * (sig * (1.0 + u * (1.0 - sig)))
        xr = xr_ref[rows, :] if r0 < chans else state_rows(place, bco_ref, bcs_ref, r0 - chans)
        old = after[rows, :]
        after[rows, :] = dc
        dx = parb[3, rows, :] * dc
        cg_ref[4, rows, :] += dc
        cg_ref[3, rows, :] += xr * dc
        for k in (1, 2, 3):
            e = jnp.where(lane < k, old, dc) * shifted_masks[k - 1 : k, :]
            e = pltpu.roll(e, Q - k, 1)
            dx = dx + parb[3 - k, rows, :] * e
            cg_ref[3 - k, rows, :] += xr * e
        out[out0 : out0 + HEAD, :] = dx.astype(out.dtype)

    bt = xa_ref[chans : chans + STATE, :]
    ct = xa_ref[chans + STATE : wide, :]
    mix = dot(bt.T, ct, (((1,), (0,))))
    dt, logistic, cums = head_terms(dt_ref[...], hp_ref)
    cols = to_columns(cums)
    bias = pair_bias(segr_ref, segc_ref)
    enter = jnp.exp(cums) * masks[3:4, :]
    last = jnp.broadcast_to(cums[:, Q - 1 : Q], cums.shape)
    tail = jnp.exp(last - cums) * masks[4:5, :]
    passing = jnp.exp(last) * masks[5:6, :]
    ds = dstate[...].astype(BF16)
    spread = dot(ds, bt, (((1,), (0,))))
    dmix = jnp.zeros((Q, Q), F32)
    s_in = s_ref[...]
    direct, cross, skip, outward, through, inward = [], [], [], [], [], []
    for h in range(heads):
        rows = slice(h * HEAD, (h + 1) * HEAD)
        xa = xa_ref[rows, :].astype(F32)
        dyb = dy_ref[rows, :]
        dy = dyb.astype(F32)
        decay = jnp.exp(cums[h : h + 1, :] - cols[:, h : h + 1] + bias)
        mixing = (mix * decay).astype(BF16)
        xd = xa * dt[h : h + 1, :]
        xdb = xd.astype(BF16)
        xt[rows, :] = (xd * tail[h : h + 1, :]).astype(BF16)
        dye[rows, :] = (dy * enter[h : h + 1, :]).astype(BF16)
        dmix = dmix + dot(xdb, dyb, (((0,), (0,)))) * decay
        near = dot(dyb, mixing, (((1,), (1,))))
        far = tail[h : h + 1, :] * spread[rows, :]
        pull = near + far
        direct.append(jnp.sum(xa * pull, axis=0, keepdims=True))
        cross.append(jnp.sum(xdb.astype(F32) * near, axis=0, keepdims=True))
        outward.append(jnp.sum(xd * far, axis=0, keepdims=True))
        through.append(jnp.sum(dstate[rows, :] * s_in[rows, :].astype(F32), axis=0, keepdims=True))
        skip.append(jnp.sum(xa * dy, axis=0, keepdims=True))
        inward.append(jnp.sum(y_ref[rows, :] * dy, axis=0, keepdims=True))
        dxa = dt[h : h + 1, :] * pull + parb[5, rows, :] * dy
        conv_back(h * HEAD, dxa, dx_ref, h * HEAD)
    pad = ddt_ref.shape[0] - heads
    if pad:
        zero = [jnp.zeros((pad, Q), F32)]
        direct, cross, skip = direct + zero, cross + zero, skip + zero
        outward, through, inward = outward + zero, through + zero, inward + zero
    direct, cross, skip, outward, through, inward = (
        jnp.concatenate(v, axis=0) for v in (direct, cross, skip, outward, through, inward)
    )
    dlog = inward - hp_ref[:, 2:3] * skip - cross
    rows = lax.broadcasted_iota(jnp.int32, (Q, Q), 0)
    lanes = lax.broadcasted_iota(jnp.int32, (Q, Q), 1)
    dl = dot(dlog, (rows >= lanes).astype(F32), (((1,), (0,))), HIGH)
    dl = dl + dot(outward, (rows < lanes).astype(F32), (((1,), (0,))), HIGH)
    dl = dl + passing * jnp.sum(through, axis=1, keepdims=True)
    ddt = (direct + hp_ref[:, 1:2] * dl) * logistic
    ddt_ref[...] = ddt
    hg_ref[0] += ddt
    hg_ref[1] += dt * dl
    hg_ref[2] += skip
    dmixb = dmix.astype(BF16)
    xtv, dyev = xt[...], dye[...]
    dbt = dot(ct, dmixb, (((1,), (1,)))) + dot(ds, xtv, (((0,), (0,))))
    dct = dot(bt, dmixb, (((1,), (0,)))) + dot(s_ref[...], dyev, (((0,), (0,))))
    dbca = jnp.concatenate([dbt, dct], axis=0)
    for r0 in range(0, 2 * STATE, HEAD):
        conv_back(chans + r0, dbca[r0 : r0 + HEAD, :], dbc_ref, r0)
    fresh = dot(dyev, ct, (((1,), (1,))))
    for h in range(heads):
        rows = slice(h * HEAD, (h + 1) * HEAD)
        dstate[rows, :] = dstate[rows, :] * passing[h : h + 1, :] + fresh[rows, :]

    if late:

        @pl.when(final)
        def _():
            dstate_out[...] = dstate[...]
            after_out[...] = after[...]

    @pl.when((seq == pl.num_programs(0) - 1) & final)
    def _():
        for r0 in range(0, wide, HEAD):
            rows = slice(r0, r0 + HEAD)
            for k in range(5):
                cgo_ref[rows, k : k + 1] = jnp.sum(cg_ref[k, rows, :], axis=1, keepdims=True)


def scan_backward(
    place, xr, bco, bcs, dtr, masks, segr, segc, par, hp, xa, u, s_in, dy, y, heads, seqs, carry=(), given=()
):
    chans, tokens = xr.shape
    padded = dtr.shape[0]
    wide = chans + 2 * STATE
    count = tokens // seqs // Q
    late = not carry
    last = count - 1 if late else count // 2 - 1
    at = lambda s, k, p: (0, s * count + last - k)
    swapped = lambda s, k, p: (0, (seqs - 1 - s) * count + last - k)
    whole = lambda s, k, p: (0, 0)
    by_seq = lambda s, k, p: (s, 0)
    args = (xr, bco, bcs, dtr, masks, segr, segc, par, hp, xa, u, s_in, dy, y)
    if not late:
        args = (*args, *carry, masks)
    carried = [pl.BlockSpec((chans, STATE), by_seq), pl.BlockSpec((wide, Q), by_seq)]
    extra = [] if late else carried + [pl.BlockSpec((8, Q), lambda s, k, p: (0, s * count + count // 2))]
    shapes = (
        jax.ShapeDtypeStruct((chans, tokens), BF16),
        jax.ShapeDtypeStruct((2 * STATE, tokens), F32),
        jax.ShapeDtypeStruct((padded, tokens), F32),
        jax.ShapeDtypeStruct((wide, 8), F32),
        jax.ShapeDtypeStruct((3, padded, Q), F32),
    )
    if late:
        shapes += (
            jax.ShapeDtypeStruct((seqs * chans, STATE), F32),
            jax.ShapeDtypeStruct((seqs * wide, Q), F32),
        )
    return pl.pallas_call(
        functools.partial(bwd_kernel, heads, late),
        out_shape=shapes,
        grid_spec=pltpu.PrefetchScalarGridSpec(
            num_scalar_prefetch=1,
            grid=(seqs, count // 2),
            in_specs=[
                pl.BlockSpec((chans, Q), at),
                pl.BlockSpec((STATE, Q), at),
                pl.BlockSpec((STATE, Q), swapped),
                pl.BlockSpec((padded, Q), at),
                pl.BlockSpec((8, Q), at),
                pl.BlockSpec((1, Q), at),
                pl.BlockSpec((Q, 1), lambda s, k, p: (s * count + last - k, 0)),
                pl.BlockSpec(par.shape, whole),
                pl.BlockSpec(hp.shape, whole),
                pl.BlockSpec((wide, Q), at),
                pl.BlockSpec((wide, Q), at),
                pl.BlockSpec((chans, STATE), at),
                pl.BlockSpec((chans, Q), at),
                pl.BlockSpec((chans, Q), at),
            ]
            + extra
            + [pl.BlockSpec(memory_space=pl.ANY)] * len(given),
            out_specs=[
                pl.BlockSpec((chans, Q), at),
                pl.BlockSpec((2 * STATE, Q), at),
                pl.BlockSpec((padded, Q), at),
                pl.BlockSpec((wide, 8), whole),
                pl.BlockSpec((3, padded, Q), lambda s, k, p: (0, 0, 0)),
            ]
            + (carried if late else []),
            scratch_shapes=[
                pltpu.VMEM((chans, STATE), F32),
                pltpu.VMEM((6, wide, Q), F32),
                pltpu.VMEM((wide, Q), F32),
                pltpu.VMEM((8, Q), F32),
                pltpu.VMEM((chans, Q), BF16),
                pltpu.VMEM((chans, Q), BF16),
                pltpu.VMEM((5, wide, Q), F32),
            ],
        ),
        input_output_aliases={1 + len(args) + k: k for k in range(len(given))},
        compiler_params=params(58),
        cost_estimate=LONG,
    )(place, *args, *given)


def block_masks(segs, seqs):
    s = segs.reshape(seqs, -1)
    length = s.shape[1]
    rows = []
    for k in (1, 2, 3):
        old = jnp.pad(s, ((0, 0), (k, 0)), constant_values=-1)[:, :length]
        rows.append(old == s)
    b = s.reshape(seqs, length // Q, Q)
    ends = b[:, :, -1:]
    before = jnp.concatenate([jnp.full((seqs, 1, 1), -1, s.dtype), ends[:, :-1]], axis=1)
    rows += [b == before, b == ends, jnp.broadcast_to(ends == before, b.shape)]
    rows = [r.reshape(1, -1).astype(F32) for r in rows]
    return jnp.concatenate(rows + [jnp.zeros((2, segs.shape[0]), F32)], axis=0)


def local(
    hidden, segment_ids, cotangent, w_zx, w_dt, w_bc, w_out, conv_x, conv_bias_x, conv_bc, conv_bias_bc,
    dt_bias, a_log, d_skip, pre_gain, gate_gain,
):
    n_dp, n_t = lax.axis_size("dp"), lax.axis_size("tensor")
    t_index = lax.axis_index("tensor")
    ring = Ring(n_dp)
    core = ring.core
    mine, width = hidden.shape
    inner_here = w_zx.shape[2]
    chans = inner_here // 2
    heads = w_dt.shape[1] // 2
    padded = max(16, heads)
    wide = chans + 2 * STATE
    inner_all = inner_here * n_t
    dd = 2 * w_zx.shape[1]

    def tensor_sum(v):
        if n_t == 2:
            return v + lax.ppermute(v, "tensor", [(0, 1), (1, 0)])
        return lax.psum(v, "tensor")

    def over_tensor(v):
        if n_t == 2:
            return v.astype(F32) + lax.ppermute(v, "tensor", [(0, 1), (1, 0)]).astype(F32)
        return lax.psum(v.astype(F32), "tensor")

    def pick(v, which, axis=0):
        size = v.shape[axis] // 2
        return lax.dynamic_slice_in_dim(v, which * size, size, axis)

    def in_order(own, other, axis):
        return jnp.where(
            core == 0, jnp.concatenate([own, other], axis), jnp.concatenate([other, own], axis)
        )

    pad_dt = lambda v: jnp.pad(v, ((0, 0), (0, STATE - heads)))
    small = jnp.concatenate([w_bc, pad_dt(w_dt[:, :heads]), pad_dt(w_dt[:, heads:])], axis=1)
    zx_other = ring.swap(w_zx)
    small_other = ring.swap(small)
    place = core.reshape(1).astype(jnp.int32)
    ux = prep_x(place, w_zx, zx_other, small, small_other, padded)
    cut = chans // 2
    gx = Gather(ring, ux, "both", cut)
    gx.step()

    hiddens = [hidden, ring.swap(after(hidden, ux))]

    def norm(h):
        h = h.astype(F32)
        return (h * lax.rsqrt(jnp.mean(h * h, -1, keepdims=True) + EPS) * pre_gain).astype(BF16)

    normed = [norm(h) for h in hiddens]
    segs = jnp.concatenate([segment_ids, ring.swap(after(segment_ids, ux))])
    masks = block_masks(segs, 2)
    segr, segc = segs[None, :], segs[:, None]
    offs = ring.offsets(dd)
    table = ring.table()

    def own_chans(v):
        return pick(v, core, v.ndim - 1)

    taps = jnp.concatenate([own_chans(conv_x), conv_bc], axis=1)
    biases = jnp.concatenate([own_chans(conv_bias_x), conv_bias_bc])
    skips = jnp.repeat(own_chans(d_skip), HEAD)
    par = jnp.concatenate(
        [taps, biases[None], jnp.pad(skips, (0, 2 * STATE))[None], jnp.zeros((2, wide), F32)], axis=0
    ).T
    a_own = -jnp.exp(own_chans(a_log))
    hp = jnp.stack([own_chans(dt_bias), a_own, own_chans(d_skip)], axis=1)
    hp = jnp.pad(hp, ((0, padded - heads), (0, 5)))
    gain = own_chans(gate_gain)[:, None]

    out_other = ring.swap(after(w_out, ux))
    uz, uo = prep_zo(place, w_zx, zx_other, w_out, out_other)
    cots = [cotangent, ring.swap(after(cotangent, uz))]

    gx.step()
    gx.step()
    third = gx.newest()
    gx.finish()
    gz = Gather(ring, after(uz, *third), "right")
    came = gz.step()

    def wave(v):
        turned = jnp.concatenate([v[:, mine:], v[:, :mine]], axis=1)
        if n_t != 2:
            return tensor_sum(v + ring.swap(turned))
        across = [(2 * i + t, 2 * (i ^ 1) + 1 - t) for i in range(n_dp) for t in range(2)]
        return (
            v
            + ring.swap(turned)
            + lax.ppermute(v, "tensor", [(0, 1), (1, 0)])
            + lax.ppermute(turned, ("dp", "tensor"), across)
        )

    def tensor_other(v):
        if n_t == 2:
            return lax.ppermute(v, "tensor", [(0, 1), (1, 0)])
        return (lax.psum(v.astype(F32), "tensor") - v.astype(F32)).astype(BF16)

    def joined(own, came):
        return (own.astype(F32) + came.astype(F32)).astype(BF16)

    blocks = gx.blocks()
    gz.step(*gx.last)
    w_states = Weight(blocks, chans, STATE, cut)
    xr, bc_own, dtr = after(
        x_projection(
            Weight(blocks, 0, chans + STATE + padded, cut), chans, normed, after(offs, *came, *gx.last)
        ),
        *gz.newest(),
    )
    bc_other = ring.swap(bc_own)
    gz.step()
    go = Gather(ring, after(uo, bc_own), "left")
    go.step()
    scan_args = (bc_own, bc_other, dtr, masks, segr, segc, par, hp)
    half = scan_forward(place, xr, *scan_args, heads, 2, 0)
    y, xa, u, s_in = after(
        scan_forward(place, xr, *scan_args, heads, 2, 1, half), *gz.newest(), *go.newest()
    )
    gz.finish(y)
    go.left(y)
    go.right(*gz.last)
    go.left(*gz.last)
    z, squares = after(
        gate_projection(Weight(gz.blocks(), 0, chans), normed, after(offs, y, *gz.last), y), *go.newest()
    )
    total_sq = wave(squares)
    s = lax.rsqrt(total_sq / inner_all + EPS)
    ynt = (y * (z * sigmoid(z)) * s * gain).astype(BF16)
    go.finish()
    ro = Scatter(ring, terms(ring, table, ynt, cots, dd))
    wb_own = whole_rows(w_states, after(offs, *ro.out), width)
    wb_other = ring.swap(wb_own)

    weight_o = Weight(go.blocks(), 0, chans)
    dyn, q = after(
        back_projection(weight_o, cots, after(offs, *ro.out, wb_own), y, z, gain), *ro.got, wb_other
    )
    sent_o = ro.step(q)
    q_total = wave(after(q, *sent_o))
    out_own, out_rest = after(back([(weight_o, ynt)], after(offs, *sent_o), width), *ro.got, q_total)
    sent_o = ro.step(out_own)
    out_came = ring.swap(out_rest)
    dzt, dyt, dgain = gate_back(inner_all, after(dyn, *sent_o), y, z, s, q_total, gain)
    parts_z = after(terms(ring, table, dzt, normed, dd), *ro.got, out_came)
    half = mine // 2
    sent_o = ro.step(parts_z[1])
    rz = Scatter(ring, after(parts_z, *sent_o))
    out_own, out_came = after((out_own, out_came), *sent_o)
    out_late = joined(out_own[half:], out_came[half:])
    out_early = joined(out_own[:half], out_came[:half])

    def dn_part(part, *others):
        return back(
            [
                (Weight(gz.blocks(), 0, chans), dzt),
                (Weight(blocks, 0, chans, cut), dxt),
                (Weight(blocks, chans + STATE, padded, cut), ddt_low),
            ],
            after(offs, *others), width, 2, part, hiddens, 40 if part else 58,
        )

    scan_args = (*scan_args, xa, u, s_in)
    out_late_other = tensor_other(out_late)
    first = after(
        scan_backward(place, xr, *scan_args, after(dyt, *rz.out, out_late, out_early), y, heads, 2),
        *ro.got, *rz.got,
    )
    sent_z = rz.step(first[3])
    dxt, ddt_low = first[0], after(first[2], *sent_z).astype(BF16)
    out_early_other = tensor_other(after(out_early, *sent_z))
    late_own, late_rest, late_pre = after(dn_part(1, *sent_z), *rz.got, out_late_other)
    sent_z = rz.step(late_own)
    late_came = ring.swap(late_rest)
    second = after(
        scan_backward(place, xr, *scan_args, after(dyt, *sent_z), y, heads, 2, first[5:], first[:3]),
        *rz.got, out_early_other, late_came,
    )
    dxt, dbc, ddt = second[:3]
    sent_z = rz.step(ddt)
    late_own = joined(late_own, after(late_came, *sent_z))
    late_other = tensor_other(late_own)
    ddt_low = after(ddt, *sent_z).astype(BF16)
    dbc_low = after(dbc, *sent_z).astype(BF16)
    dbc_came = ring.swap(dbc_low[:, mine:])
    parts_x = after(
        terms(ring, table, after(dxt, *sent_z, late_own, dbc_low), normed, dd), *rz.got, dbc_came
    )
    rx = Scatter(ring, parts_x)
    dbc_own = joined(dbc_low[:, :mine], after(dbc_came, *parts_x))
    dbc_other = tensor_other(dbc_own)
    early_own, early_rest, early_pre = after(
        dn_part(0, *rx.out, dbc_own), *rx.got, late_other, dbc_other
    )
    sent_x = rx.step(early_own)

    early_came = ring.swap(early_rest)
    keep_z, give_z = rz.finish(place, *sent_x, cost=LONG)
    keep_o, give_o = ro.finish(place, keep_z)
    dbc_own = joined(dbc_own, after(dbc_other, keep_z))
    pre_bc = pre_states(place, dbc_own, hidden, wb_own, wb_other)
    pre_part = early_pre + late_pre + pre_bc * (1.0 / n_t)
    cg_sums, hg_sums = after((second[3], second[4]), keep_z)
    cg = (first[3] + cg_sums).T[:5]
    hg = jnp.sum(first[4] + hg_sums, 2)[:, :heads]
    hg = hg * jnp.stack([jnp.ones_like(a_own), a_own, jnp.ones_like(a_own)])
    dgain = after(dgain, keep_z)
    split = jnp.concatenate([cg[:, :chans].reshape(-1), dgain[:, 0], hg.reshape(-1)])
    shared = jnp.concatenate([cg[:, chans:].reshape(-1), pre_part[0]])
    n_split, n_shared = split.shape[0], shared.shape[0]
    bc_cols = 2 * STATE // n_t
    states = lax.dynamic_slice_in_dim(dbc_own, t_index * bc_cols, bc_cols, 0)
    products = small_terms(place, states, ddt_low, normed)
    steps = ring.halving(*after((products, jnp.concatenate([split, shared])), *rx.got, early_came))

    sent_x = rx.step(products)
    early_own = joined(after(early_own, *sent_x), early_came)
    early_other = tensor_other(early_own)
    flying = next(steps)
    keep_o, give_o = after((keep_o, give_o), *sent_x)
    output = residual(
        (out_late, out_late_other), (out_early, out_early_other), after(hidden, early_own)
    )
    output = after(output, *rx.got)

    sent_x = rx.step(output)
    flying = steps.send(after(flying, *sent_x))
    grad_out = in_order(after(keep_o, *sent_x), ring.swap(give_o), 0)
    late_own = after(late_own, grad_out)
    grad_hidden = norm_back(
        place, (late_own, late_other), (early_own, early_other),
        hidden, cotangent, pre_gain[None], dbc_own, wb_own, wb_other,
    )
    grad_hidden = after(grad_hidden, *rx.got)
    keep_x, give_x = rx.finish(place, grad_hidden)
    flying = steps.send(after(flying, keep_x))
    give_x = ring.swap(give_x)
    for _ in range(ring.n.bit_length() - 4):
        flying = steps.send(flying)
    sum_small, common = steps.send(flying)
    split, shared = common[:n_split], common[n_split : n_split + n_shared]
    common_other = ring.swap(common)
    split_other = common_other[:n_split]
    shared = tensor_sum(shared + common_other[n_split : n_split + n_shared])
    low, high = ring.halves(sum_small, core)
    sum_small = low + ring.swap(high)

    def parts(v):
        a = v[: 5 * chans].reshape(5, chans)
        b = v[5 * chans : 6 * chans]
        c = v[6 * chans :].reshape(3, heads)
        return a, b, c

    (a0, b0, c0), (a1, b1, c1) = parts(split), parts(split_other)
    cg_x = in_order(a0, a1, 1)
    grad_gate = in_order(b0, b1, 0)
    hg = in_order(c0, c1, 1)
    cg_bc = shared[: 5 * 2 * STATE].reshape(5, 2 * STATE)
    grad_pre = shared[5 * 2 * STATE :]

    grad_zx = turn(place, keep_z, ring.swap(give_z), keep_x, give_x)
    grad_bc = sum_small[:bc_cols].T
    grad_dt = jnp.concatenate(
        [sum_small[bc_cols : bc_cols + heads], sum_small[bc_cols + padded : bc_cols + padded + heads]]
    ).T
    return (
        output, grad_hidden, grad_zx, grad_dt, grad_bc, grad_out, cg_x[:4], cg_x[4], cg_bc[:4], cg_bc[4],
        hg[0], hg[1], hg[2], grad_pre, grad_gate,
    )


def solution(mesh):
    in_specs = (
        P("dp", None), P("dp"), P("dp", None), P(None, "dp", "tensor"), P("dp", "tensor"), P("dp", None),
        P("tensor", "dp"), P(None, "tensor"), P("tensor"), P(), P(), P("tensor"), P("tensor"), P("tensor"),
        P(), P("tensor"),
    )
    out_specs = (
        P("dp", None), P("dp", None), P(None, "dp", "tensor"), P("dp", "tensor"), P("dp", "tensor"),
        P("tensor", "dp"), P(None, "tensor"), P("tensor"), P(), P(), P("tensor"), P("tensor"), P("tensor"),
        P(), P("tensor"),
    )
    return jax.shard_map(local, mesh=mesh, in_specs=in_specs, out_specs=out_specs, check_vma=False)
```

```python
import functools

import jax
import jax.numpy as jnp
from jax import lax
from jax.experimental import pallas as pl
from jax.experimental.pallas import tpu as pltpu
from jax.sharding import PartitionSpec as P

EPS = 1e-05
Q = 128
NEG = -1e30
F32 = jnp.float32
BF16 = jnp.bfloat16
HIGH = lax.Precision.HIGHEST
MIB = 1024 * 1024
HEAD = 64
STATE = 128


LONG = pl.CostEstimate(flops=30_000_000_000, bytes_accessed=1, transcendentals=0)
BRIEF = pl.CostEstimate(flops=1, bytes_accessed=1, transcendentals=0)


def dot(a, b, dims, precision=None):
    return lax.dot_general(a, b, (dims, ((), ())), precision=precision, preferred_element_type=F32)


def lane_sums(v):
    return dot(jnp.ones((8, v.shape[1]), F32), v, (((1,), (1,))), HIGH)


def params(mib):
    return pltpu.CompilerParams(vmem_limit_bytes=mib * MIB)


def after(value, *others):
    return lax.optimization_barrier((value, others))[0]


def ring_order(chips):
    if chips == 8:
        return [0, 2, 4, 6, 7, 5, 3, 1]
    half = chips // 2
    return list(range(half)) + list(range(chips - 1, half - 1, -1))


class Ring:
    def __init__(self, n_dp):
        self.n = n_dp // 2
        self.order = ring_order(self.n)
        place = [0] * self.n
        for position, chip in enumerate(self.order):
            place[chip] = position
        me = lax.axis_index("dp")
        self.core = me % 2
        self.mine = me // 2
        self.pos = jnp.asarray(place, jnp.int32)[self.mine]
        self.right = self.perm(1)
        self.left = self.perm(-1)
        self.full = self.n // 2 - 1

    def perm(self, step):
        pairs = []
        for p in range(self.n):
            for c in range(2):
                pairs.append((self.order[p] * 2 + c, self.order[(p + step) % self.n] * 2 + c))
        return pairs

    def table(self):
        table = [[self.order[(p + s) % self.n] for s in range(self.n)] for p in range(self.n)]
        row = lax.dynamic_index_in_dim(jnp.asarray(table, jnp.int32), self.pos, 0, keepdims=False)
        return jnp.concatenate([row, self.core.reshape(1).astype(jnp.int32)])

    def offsets(self, dd):
        steps = [0] + [-k for k in range(1, self.full + 1)] + list(range(1, self.full + 1)) + [self.n // 2]
        table = [[self.order[(p + s) % self.n] * dd for s in steps] for p in range(self.n)]
        return lax.dynamic_index_in_dim(jnp.asarray(table, jnp.int32), self.pos, 0, keepdims=False)

    def go_right(self, v):
        return lax.ppermute(v, "dp", self.right)

    def go_left(self, v):
        return lax.ppermute(v, "dp", self.left)

    def swap(self, v):
        return lax.ppermute(v, "dp", [(i, i ^ 1) for i in range(2 * self.n)])

    def halving(self, v, dist):
        pairs = [(i, i ^ (2 * dist)) for i in range(2 * self.n)]
        keep, give = self.halves(v, (self.mine // dist) % 2)
        return keep, lax.ppermute(give.astype(BF16), "dp", pairs)

    def doubling(self, v, dist):
        return lax.ppermute(v, "dp", [(i, i ^ (2 * dist)) for i in range(2 * self.n)])

    def halves(self, v, bit):
        size = v.shape[1] // 2
        return (
            lax.dynamic_slice_in_dim(v, bit * size, size, 1),
            lax.dynamic_slice_in_dim(v, (1 - bit) * size, size, 1),
        )


class Gather:
    def __init__(self, ring, unit, far, cut=None):
        self.ring, self.far, self.cut = ring, far, cut
        self.r, self.l = [unit], [unit]
        self.last = []

    def right(self, *others):
        if len(self.r) <= self.ring.full:
            v = after(self.r[-1], *others) if others else self.r[-1]
            self.r.append(self.ring.go_right(v))
        return self.r[-1]

    def left(self, *others):
        if len(self.l) <= self.ring.full:
            v = after(self.l[-1], *others) if others else self.l[-1]
            self.l.append(self.ring.go_left(v))
        return self.l[-1]

    def step(self, *others):
        return self.right(*others), self.left(*others)

    def newest(self):
        return self.r[-1], self.l[-1]

    def finish(self, *others):
        while len(self.r) <= self.ring.full:
            self.right()
        while len(self.l) <= self.ring.full:
            self.left()
        r, l, cut = self.r[-1], self.l[-1], self.cut
        if others:
            r, l = after(r, *others), after(l, *others)
        if self.far == "both":
            self.last = [self.ring.go_right(r[:cut]), self.ring.go_left(l[cut:])]
        elif self.far == "right":
            self.last = [self.ring.go_right(r)]
        else:
            self.last = [self.ring.go_left(l)]
        return self.last

    def blocks(self):
        return self.r + self.l[1:] + self.last


def both_parts(vt, own, other):
    half = own.shape[0]
    return dot(vt[:, :half], own[...], (((1,), (0,)))) + dot(vt[:, half:], other[...], (((1,), (0,))))


def terms_kernel(table, vt, own, other, *outs):
    total = both_parts(vt, own, other).astype(BF16)
    top, bottom = outs[:2]
    half = top.shape[0]
    s = pl.program_id(0)

    @pl.when(s == 0)
    def _():
        top[...] = total[:half]
        bottom[...] = total[half:]

    for k, out in enumerate(outs[2:]):

        @pl.when((s == 1 + 2 * k) | (s == 2 + 2 * k))
        def _():
            out[0] = total


def terms(ring, table, vt, acts, dd):
    rows, tokens = vt.shape
    n, full = ring.n, ring.full
    half = n // 2

    def step(s):
        j = full - (s - 1) // 2
        at = jnp.where(s == 0, half, jnp.where(s % 2 == 1, j, n - j))
        return jnp.where(s == n - 1, 0, at)

    column = pl.BlockSpec((tokens // 2, dd), lambda s, t: (0, t[step(s)]))
    part = pl.BlockSpec((rows // 2, dd), lambda s, t: (0, 0))
    pair = lambda k: pl.BlockSpec((1, rows, dd), lambda s, t: (jnp.clip(s - 1 - 2 * k, 0, 1), 0, 0))
    single = pl.BlockSpec((1, rows, dd), lambda s, t: (0, 0, 0))
    return pl.pallas_call(
        terms_kernel,
        out_shape=tuple([jax.ShapeDtypeStruct((rows // 2, dd), BF16)] * 2)
        + tuple([jax.ShapeDtypeStruct((2, rows, dd), BF16)] * full)
        + (jax.ShapeDtypeStruct((1, rows, dd), BF16),),
        grid_spec=pltpu.PrefetchScalarGridSpec(
            num_scalar_prefetch=1,
            grid=(n,),
            in_specs=[pl.BlockSpec((rows, tokens), lambda s, t: (0, 0)), column, column],
            out_specs=tuple([part, part] + [pair(k) for k in range(full)] + [single]),
        ),
        compiler_params=params(24),
        cost_estimate=LONG,
    )(table, vt, *acts)


def first_add_kernel(own, r, l, out_r, out_l):
    half = r.shape[0]
    out_r[:half] = (own[0, :half].astype(F32) + r[...].astype(F32)).astype(BF16)
    out_r[half:] = own[0, half:]
    out_l[:half] = own[1, :half]
    out_l[half:] = (own[1, half:].astype(F32) + l[...].astype(F32)).astype(BF16)


def add_kernel(own, r, l, out_r, out_l):
    out_r[...] = (own[0].astype(F32) + r[...].astype(F32)).astype(BF16)
    out_l[...] = (own[1].astype(F32) + l[...].astype(F32)).astype(BF16)


def last_add_kernel(place, own, r, l, keep, give):
    total = own[0].astype(F32) + r[...].astype(F32) + l[...].astype(F32)
    dd = keep.shape[1]
    low, high = total[:, :dd], total[:, dd:]
    keep[...] = jnp.where(place[0] == 0, low, high)
    give[...] = jnp.where(place[0] == 0, high, low)


class Scatter:
    def __init__(self, ring, parts):
        self.ring = ring
        top, bottom, *self.own = parts
        self.left_to_do = ring.full
        self.send(top, bottom)

    def send(self, r, l):
        self.out = (r, l)
        self.got = (self.ring.go_right(r), self.ring.go_left(l))

    def step(self, *others):
        if not self.left_to_do:
            return self.out
        j = self.left_to_do
        self.left_to_do -= 1
        own = self.own[self.ring.full - j]
        rows, dd = own.shape[1:]
        got = after(self.got, *others) if others else self.got
        whole = lambda shape: pl.BlockSpec(shape, lambda i: (0,) * len(shape))
        out = pl.pallas_call(
            first_add_kernel if j == self.ring.full else add_kernel,
            grid=(1,),
            out_shape=(jax.ShapeDtypeStruct((rows, dd), BF16),) * 2,
            in_specs=[whole(v.shape) for v in (own, *got)],
            out_specs=(whole((rows, dd)),) * 2,
            compiler_params=params(16),
            cost_estimate=BRIEF,
        )(own, *got)
        self.send(*out)
        return self.out

    def finish(self, place, *others, cost=BRIEF):
        while self.left_to_do:
            self.step()
        own = self.own[-1]
        rows, dd = own.shape[1:]
        got = after(self.got, *others) if others else self.got
        whole = lambda shape: pl.BlockSpec(shape, lambda i, p: (0,) * len(shape))
        return pl.pallas_call(
            last_add_kernel,
            out_shape=(jax.ShapeDtypeStruct((rows, dd // 2), F32),) * 2,
            grid_spec=pltpu.PrefetchScalarGridSpec(
                num_scalar_prefetch=1,
                grid=(1,),
                in_specs=[whole(v.shape) for v in (own, *got)],
                out_specs=(whole((rows, dd // 2)),) * 2,
            ),
            compiler_params=params(16),
            cost_estimate=cost,
        )(place, own, *got)


def prep_x_kernel(place, own, other, small_own, small_other, out):
    core = place[0]
    dd = own.shape[1]
    chans = own.shape[2] // 2
    padded = out.shape[0] - chans - STATE
    for b in range(2):
        lanes = slice(b * dd, (b + 1) * dd)
        near = core == b
        src = jnp.where(near, own[0], other[0])
        src = jnp.where(core == 0, src[:, :chans], src[:, chans:])
        out[:chans, lanes] = src.T
        small = jnp.where(near, small_own[...], small_other[...])
        states = jnp.where(core == 0, small[:, :STATE], small[:, STATE : 2 * STATE])
        out[chans : chans + STATE, lanes] = states.T
        steps = jnp.where(core == 0, small[:, 2 * STATE : 3 * STATE], small[:, 3 * STATE :])
        out[chans + STATE :, lanes] = steps.T[:padded]


def prep_x(place, own, other, small_own, small_other, padded):
    _, dd, inner = own.shape
    rows = inner // 2 + STATE + padded
    return pl.pallas_call(
        prep_x_kernel,
        out_shape=jax.ShapeDtypeStruct((rows, 2 * dd), BF16),
        grid_spec=pltpu.PrefetchScalarGridSpec(
            num_scalar_prefetch=1,
            grid=(1,),
            in_specs=[pl.BlockSpec((1, dd, inner), lambda i, p: (1, 0, 0))] * 2
            + [pl.BlockSpec((dd, 4 * STATE), lambda i, p: (0, 0))] * 2,
            out_specs=pl.BlockSpec((rows, 2 * dd), lambda i, p: (0, 0)),
        ),
        compiler_params=params(12),
        cost_estimate=BRIEF,
    )(place, own, other, small_own, small_other)


def prep_zo_kernel(place, own, other, out_own, out_other, z, o):
    core = place[0]
    dd = own.shape[1]
    chans = own.shape[2] // 2
    for b in range(2):
        lanes = slice(b * dd, (b + 1) * dd)
        near = core == b
        src = jnp.where(near, own[0], other[0])
        src = jnp.where(core == 0, src[:, :chans], src[:, chans:])
        z[:, lanes] = src.T
        src = jnp.where(near, out_own[...], out_other[...])
        o[:, lanes] = jnp.where(core == 0, src[:chans], src[chans:])


def prep_zo(place, own, other, out_own, out_other):
    _, dd, inner = own.shape
    shape = (inner // 2, 2 * dd)
    return pl.pallas_call(
        prep_zo_kernel,
        out_shape=(jax.ShapeDtypeStruct(shape, BF16),) * 2,
        grid_spec=pltpu.PrefetchScalarGridSpec(
            num_scalar_prefetch=1,
            grid=(1,),
            in_specs=[pl.BlockSpec((1, dd, inner), lambda i, p: (0, 0, 0))] * 2
            + [pl.BlockSpec((inner, dd), lambda i, p: (0, 0))] * 2,
            out_specs=(pl.BlockSpec(shape, lambda i, p: (0, 0)),) * 2,
        ),
        compiler_params=params(12),
        cost_estimate=BRIEF,
    )(place, own, other, out_own, out_other)


class Weight:
    def __init__(self, blocks, first, rows, cut=None):
        self.args, self.specs, self.plan = [], [], []
        self.rows, self.dd = rows, blocks[0].shape[1]

        def view(array, start, size):
            index = start // size
            self.args.append(array)
            self.specs.append(pl.BlockSpec((size, self.dd), lambda i, o, index=index: (index, 0)))

        whole = blocks if cut is None else blocks[:-2]
        for block in whole:
            view(block, first, rows)
            self.plan.append(1)
        if cut is not None:
            pieces = 0
            if first < cut:
                view(blocks[-2], first, min(rows, cut - first))
                pieces += 1
            if first + rows > cut:
                start = max(first, cut)
                view(blocks[-1], start - cut, first + rows - start)
                pieces += 1
            self.plan.append(pieces)

    def read(self, refs):
        at, out = 0, []
        for pieces in self.plan:
            part = [r[...] for r in refs[at : at + pieces]]
            out.append(part[0] if pieces == 1 else jnp.concatenate(part, axis=0))
            at += pieces
        return out


def projected(weight, refs, act, offs):
    total = None
    for b, w in enumerate(weight.read(refs)):
        off = pl.multiple_of(offs[b], weight.dd)
        part = dot(w, act[:, pl.ds(off, weight.dd)], (((1,), (1,))))
        total = part if total is None else total + part
    return total


def projection(body, weight, acts, offs, extra, extra_specs, out_shape, out_specs, mib=40):
    tile, width = acts[0].shape
    tokens = 2 * tile
    n = len(weight.args)

    def kernel(offs, *refs):
        for k in range(2):

            @pl.when(pl.program_id(0) == k)
            def _():
                acc = projected(weight, refs[:n], refs[n + k], offs)
                body(acc, refs[n + 2 : n + 2 + len(extra)], refs[n + 2 + len(extra) :])

    return pl.pallas_call(
        kernel,
        out_shape=out_shape,
        grid_spec=pltpu.PrefetchScalarGridSpec(
            num_scalar_prefetch=1,
            grid=(tokens // tile,),
            in_specs=weight.specs + [pl.BlockSpec((tile, width), lambda i, o: (0, 0))] * 2 + extra_specs,
            out_specs=out_specs,
        ),
        compiler_params=params(mib),
        cost_estimate=LONG,
    )(offs, *weight.args, *acts, *extra)


def x_projection(weight, chans, acts, offs):
    tile = acts[0].shape[0]
    parts = (chans, STATE, weight.rows - chans - STATE)

    def body(acc, extra, outs):
        at = 0
        for out, rows in zip(outs, parts):
            out[...] = acc[at : at + rows]
            at += rows

    return projection(
        body, weight, acts, offs, (), [],
        tuple(jax.ShapeDtypeStruct((rows, 2 * tile), F32) for rows in parts),
        tuple(pl.BlockSpec((rows, tile), lambda i, o: (0, i)) for rows in parts),
    )


def sigmoid(v):
    return 0.5 * jnp.tanh(0.5 * v) + 0.5


def gate_projection(weight, acts, offs, y):
    rows, tokens = y.shape
    tile = tokens // 2

    def body(z, extra, outs):
        outs[0][...] = z
        g = extra[0][...] * (z * sigmoid(z))
        outs[1][...] = jnp.sum(g * g, axis=0, keepdims=True)

    wide = pl.BlockSpec((rows, tile), lambda i, o: (0, i))
    line = pl.BlockSpec((1, tile), lambda i, o: (0, i))
    return projection(
        body, weight, acts, offs, (y,), [wide],
        (jax.ShapeDtypeStruct((rows, tokens), F32), jax.ShapeDtypeStruct((1, tokens), F32)),
        (wide, line), 58,
    )


def back_projection(weight, acts, offs, y, z, gain):
    rows, tokens = y.shape
    tile = tokens // 2

    def body(dyn, extra, outs):
        y, z, gain = extra
        outs[0][...] = dyn
        zv = z[...]
        g = y[...] * (zv * sigmoid(zv))
        outs[1][...] = jnp.sum(dyn * gain[...] * g, axis=0, keepdims=True)

    wide = pl.BlockSpec((rows, tile), lambda i, o: (0, i))
    line = pl.BlockSpec((1, tile), lambda i, o: (0, i))
    return projection(
        body, weight, acts, offs, (y, z, gain),
        [wide, wide, pl.BlockSpec((rows, 1), lambda i, o: (0, 0))],
        (jax.ShapeDtypeStruct((rows, tokens), F32), jax.ShapeDtypeStruct((1, tokens), F32)),
        (wide, line),
    )


def back(groups, offs, width, parts=1, part=0, hiddens=None, states=None, mib=40):
    dd = groups[0][0].dd
    size = groups[0][1].shape[1] // (2 * parts)
    args, specs = [], []
    flops = 0
    for weight, vt in groups:
        args += weight.args + [vt, vt]
        specs += weight.specs
        specs += [pl.BlockSpec((vt.shape[0], size), lambda i, o, p=p: (0, p)) for p in (part, parts + part)]
    if states is not None:
        dbc, w_own, w_other, core = states
        args += [dbc, dbc, w_own, w_other]
        specs += [pl.BlockSpec((dbc.shape[0], size), lambda i, o, p=p: (0, p)) for p in (part, parts + part)]
        specs += [pl.BlockSpec(w_own.shape, lambda i, o: (0, 0))] * 2
        offs = jnp.concatenate([offs, core])
    out_spec = pl.BlockSpec((size, width), lambda i, o: (0, 0))
    shapes = [jax.ShapeDtypeStruct((size, width), BF16)] * 2
    out_specs = [out_spec, out_spec]
    if hiddens is not None:
        args += list(hiddens)
        specs += [pl.BlockSpec((size, width), lambda i, o: (part, 0))] * 2
        shapes.append(jax.ShapeDtypeStruct((1, width), F32))
        out_specs.append(pl.BlockSpec((1, width), lambda i, o: (0, 0)))

    def kernel(offs, *refs):
        outs = refs[len(args) :]
        at, terms = 0, []
        for weight, _ in groups:
            n = len(weight.args)
            v = jnp.concatenate([refs[at + n][...].T, refs[at + n + 1][...].T], axis=0)
            terms.append((v, weight.read(refs[at : at + n])))
            at += n + 2
        if states is not None:
            dbc = jnp.concatenate([refs[at][...], refs[at + 1][...]], axis=1)
            first = offs[offs.shape[0] - 1] == 0
            low, high = dbc[:STATE], dbc[STATE:]
            v_own, v_other = jnp.where(first, low, high).T, jnp.where(first, high, low).T
            w_own, w_other = refs[at + 2], refs[at + 3]
        scales = []
        if hiddens is not None:
            for h in refs[len(args) - 2 : len(args)]:
                v = h[...].astype(F32)
                scales.append(lax.rsqrt(jnp.mean(v * v, axis=1, keepdims=True) + EPS))
        for b in range(len(terms[0][1])):
            off = pl.multiple_of(offs[b], dd)
            along = None
            total = None
            for v, blocks in terms:
                term = dot(v, blocks[b], (((1,), (0,))))
                total = term if total is None else total + term
            if states is not None:
                total = total + dot(v_own, w_own[:, pl.ds(off, dd)], (((1,), (0,))))
                total = total + dot(v_other, w_other[:, pl.ds(off, dd)], (((1,), (0,))))
            for k in range(2):
                here = total[k * size : (k + 1) * size]
                outs[k][:, pl.ds(off, dd)] = here.astype(BF16)
                if hiddens is not None:
                    h = refs[len(args) - 2 + k][:, pl.ds(off, dd)].astype(F32)
                    line = jnp.sum(here * (h * scales[k]), axis=0, keepdims=True)
                    along = line if along is None else along + line
            if hiddens is not None:
                outs[2][:, pl.ds(off, dd)] = along

    return pl.pallas_call(
        kernel,
        out_shape=tuple(shapes),
        grid_spec=pltpu.PrefetchScalarGridSpec(
            num_scalar_prefetch=1, grid=(1,), in_specs=specs, out_specs=tuple(out_specs)
        ),
        compiler_params=params(mib),
        cost_estimate=LONG,
    )(offs, *args)


def whole_rows(weight, offs, width):
    def kernel(offs, *refs):
        for b, w in enumerate(weight.read(refs[:-1])):
            refs[-1][:, pl.ds(pl.multiple_of(offs[b], weight.dd), weight.dd)] = w

    return pl.pallas_call(
        kernel,
        out_shape=jax.ShapeDtypeStruct((weight.rows, width), BF16),
        grid_spec=pltpu.PrefetchScalarGridSpec(
            num_scalar_prefetch=1,
            grid=(1,),
            in_specs=weight.specs,
            out_specs=pl.BlockSpec((weight.rows, width), lambda i, o: (0, 0)),
        ),
        compiler_params=params(20),
        cost_estimate=BRIEF,
    )(offs, *weight.args)


def gathered_sums_kernel(cg_a, cg_b, dgain, hg_a, hg_b, spots, pre_a, pre_b, out):
    wide = out.shape[1]
    padded = hg_a.shape[1]
    out[...] = jnp.zeros_like(out)
    row = lax.broadcasted_iota(jnp.int32, (8, 8), 0)
    lane = lax.broadcasted_iota(jnp.int32, (8, 8), 1)
    cg = dot((row == lane).astype(F32), cg_a[...] + cg_b[...], (((1,), (1,))), HIGH)
    out[0:5, :] = cg[0:5]
    out[5:6, : dgain.shape[1]] = dgain[0:1, :]
    for k in range(3):
        sums = dot(lane_sums(hg_a[k] + hg_b[k]), spots[k * padded : (k + 1) * padded, :], (((1,), (0,))), HIGH)
        out[6:7, k * 128 : (k + 1) * 128] = sums[0:1]
    pre = pre_a[...] + pre_b[...]
    width = pre.shape[1]
    for k in range(-(-width // wide)):
        size = min(wide, width - k * wide)
        out[7 + k : 8 + k, :size] = pre[:, k * wide : k * wide + size]


def gathered_sums(cg_a, cg_b, dgain, hg_a, hg_b, spots, *pre):
    wide = cg_a.shape[0]
    rows = -(-(7 + -(-pre[0].shape[1] // wide)) // 8) * 8
    args = (cg_a, cg_b, dgain, hg_a, hg_b, spots, *pre)
    whole = lambda shape: pl.BlockSpec(shape, lambda i: (0,) * len(shape))
    return pl.pallas_call(
        gathered_sums_kernel,
        out_shape=jax.ShapeDtypeStruct((rows, wide), F32),
        grid=(1,),
        in_specs=[whole(v.shape) for v in args],
        out_specs=whole((rows, wide)),
        compiler_params=params(16),
        cost_estimate=BRIEF,
    )(*args)


def finals_kernel(heads, padded, n_everyone, place, keep_z, other_z, keep_x, other_x, small, own, other, *refs):
    everyone = refs[0][...]
    for r in refs[1:n_everyone]:
        everyone = everyone + r[...]
    if n_everyone > 1:
        everyone = everyone + own[...] + other[...]
    zx, dt, bc, taps, bias, taps_bc, bias_bc, g_dt, g_a, g_d, pre, gate = refs[n_everyone:]
    first = place[0] == 0
    chans = keep_z.shape[0]
    for k, (a, b) in enumerate(((keep_z, other_z), (keep_x, other_x))):
        zx[k, :, :chans] = jnp.where(first, a[...], b[...]).T
        zx[k, :, chans:] = jnp.where(first, b[...], a[...]).T
    rows = bc.shape[1]
    turned = small[...].T
    bc[...] = turned[:, :rows]
    dt[:, :heads] = turned[:, rows : rows + heads]
    dt[:, heads:] = turned[:, rows + padded : rows + padded + heads]
    a, b = own[...], other[...]
    low, high = jnp.where(first, a, b)[:, :chans], jnp.where(first, b, a)[:, :chans]
    for out, at, size in ((taps, 0, 4), (bias, 4, 1), (gate, 5, 1)):
        out[:, :chans] = low[at : at + size]
        out[:, chans:] = high[at : at + size]
    taps_bc[...] = everyone[0:4, chans:]
    bias_bc[...] = everyone[4:5, chans:]
    both = a + b
    for k, out in enumerate((g_dt, g_a, g_d)):
        out[...] = both[6:7, k * 128 : k * 128 + 2 * heads]
    wide = both.shape[1]
    width = pre.shape[1]
    for k in range(-(-width // wide)):
        size = min(wide, width - k * wide)
        pre[:, k * wide : k * wide + size] = everyone[7 + k : 8 + k, :size]


def finals(place, keep_z, other_z, keep_x, other_x, small, own, other, everyone, heads, padded, width):
    chans, dd = keep_z.shape
    bc_rows = small.shape[0] - 2 * padded
    args = (keep_z, other_z, keep_x, other_x, small, own, other, *everyone)
    shapes = (
        (2, dd, 2 * chans), (dd, 2 * heads), (dd, bc_rows), (4, 2 * chans), (1, 2 * chans), (4, 2 * STATE),
        (1, 2 * STATE), (1, 2 * heads), (1, 2 * heads), (1, 2 * heads), (1, width), (1, 2 * chans),
    )
    whole = lambda shape: pl.BlockSpec(shape, lambda i, p: (0,) * len(shape))
    return pl.pallas_call(
        functools.partial(finals_kernel, heads, padded, len(everyone)),
        out_shape=tuple(jax.ShapeDtypeStruct(shape, F32) for shape in shapes),
        grid_spec=pltpu.PrefetchScalarGridSpec(
            num_scalar_prefetch=1,
            grid=(1,),
            in_specs=[
                pl.BlockSpec((chans, dd), lambda i, p: (1, 0)) if k == 1 else whole(v.shape)
                for k, v in enumerate(args)
            ],
            out_specs=tuple(whole(shape) for shape in shapes),
        ),
        compiler_params=params(24),
        cost_estimate=BRIEF,
    )(place, *args)


def reversed_bits(index, bits):
    return sum(((index >> k) & 1) << (bits - 1 - k) for k in range(bits))


def small_terms_kernel(shards, core_place, states, steps, own, other, keep, give):
    first = core_place[0] == 0
    both = both_parts(steps, own, other)
    total = jnp.concatenate(
        [dot(states[...], own[...], (((1,), (0,)))), jnp.where(first, both, 0.0), jnp.where(first, 0.0, both)]
    )
    chips = shards // 2
    lanes = own.shape[1] // shards
    bits = chips.bit_length() - 1
    for chip in range(chips):
        at = reversed_bits(chip, bits) * lanes
        low = total[:, 2 * chip * lanes : (2 * chip + 1) * lanes]
        high = total[:, (2 * chip + 1) * lanes : (2 * chip + 2) * lanes]
        keep[:, at : at + lanes] = jnp.where(first, low, high)
        give[:, at : at + lanes] = jnp.where(first, high, low).astype(BF16)


def small_terms(place, states, steps, acts, shards):
    m, k = states.shape[0], steps.shape[0]
    width = acts[0].shape[1]
    whole = lambda i, p: (0, 0)
    shape = (m + 2 * k, width // 2)
    return pl.pallas_call(
        functools.partial(small_terms_kernel, shards),
        out_shape=(jax.ShapeDtypeStruct(shape, F32), jax.ShapeDtypeStruct(shape, BF16)),
        grid_spec=pltpu.PrefetchScalarGridSpec(
            num_scalar_prefetch=1,
            grid=(1,),
            in_specs=[pl.BlockSpec(v.shape, whole) for v in (states, steps, *acts)],
            out_specs=(pl.BlockSpec(shape, whole),) * 2,
        ),
        compiler_params=params(20),
        cost_estimate=BRIEF,
    )(place, states, steps, *acts)


def output_kernel(late_own, late_came, own, came, hidden, out):
    late = pl.program_id(0) >= pl.num_programs(0) // 2
    rest = jnp.where(late, late_own[...].astype(F32), own[...].astype(F32))
    rest = rest + jnp.where(late, late_came[...].astype(F32), came[...].astype(F32))
    out[...] = (hidden[...].astype(F32) + rest).astype(BF16)


def residual(late, early, hidden):
    rows, width = hidden.shape
    tile = 128
    half = rows // tile // 2
    block = pl.BlockSpec((tile, width), lambda i: (i, 0))
    first = pl.BlockSpec((tile, width), lambda i: (jnp.minimum(i, half - 1), 0))
    second = pl.BlockSpec((tile, width), lambda i: (jnp.maximum(i - half, 0), 0))
    return pl.pallas_call(
        output_kernel,
        out_shape=jax.ShapeDtypeStruct(hidden.shape, BF16),
        grid=(rows // tile,),
        in_specs=[second, second, first, first, block],
        out_specs=block,
        compiler_params=params(20),
        cost_estimate=LONG,
    )(*late, *early, hidden)


def norm_back_kernel(late_own, late_came, own, came, hidden, cot, gain, out):
    h = hidden[...].astype(F32)
    width = h.shape[1]
    r = lax.rsqrt(jnp.mean(h * h, axis=1, keepdims=True) + EPS)
    late = pl.program_id(0) >= pl.num_programs(0) // 2
    dn = jnp.where(late, late_own[...].astype(F32), own[...].astype(F32))
    dn = dn + jnp.where(late, late_came[...].astype(F32), came[...].astype(F32))
    weighted = dn * gain[...]
    along = jnp.sum(weighted * h, axis=1, keepdims=True) * (1.0 / width)
    out[...] = (weighted * r - h * (r * r * r * along) + cot[...].astype(F32)).astype(BF16)


def norm_back(late, early, hidden, cot, gain):
    rows, width = hidden.shape
    tile = 128
    half = rows // tile // 2
    block = pl.BlockSpec((tile, width), lambda i: (i, 0))
    first = pl.BlockSpec((tile, width), lambda i: (jnp.minimum(i, half - 1), 0))
    second = pl.BlockSpec((tile, width), lambda i: (jnp.maximum(i - half, 0), 0))
    return pl.pallas_call(
        norm_back_kernel,
        out_shape=jax.ShapeDtypeStruct(hidden.shape, BF16),
        grid=(rows // tile,),
        in_specs=[second, second, first, first, block, block, pl.BlockSpec((1, width), lambda i: (0, 0))],
        out_specs=block,
        compiler_params=params(30),
        cost_estimate=LONG,
    )(*late, *early, hidden, cot, gain)


def gate_back_kernel(total, dyn, y, z, s, q, gain, dz, dy, dgain):
    zv, yv, sv = z[...], y[...], s[...]
    sig = sigmoid(zv)
    silu = zv * sig
    g = yv * silu
    scaled = dyn[...] * sv
    t = scaled * g
    lanes = t[:, :128]
    for k in range(128, t.shape[1], 128):
        lanes = lanes + t[:, k : k + 128]
    dgain[...] = lane_sums(lanes)
    dg = scaled * gain[...] - g * (sv * sv * sv * q[...] * (1.0 / total))
    dz[...] = (dg * yv * (sig * (1.0 + zv * (1.0 - sig)))).astype(BF16)
    dy[...] = (dg * silu).astype(BF16)


def gate_back(total, dyn, y, z, s, q, gain):
    rows, tokens = dyn.shape
    tile = max(rows // 4, 128)
    wide = pl.BlockSpec((tile, tokens), lambda i: (i, 0))
    line = pl.BlockSpec((1, tokens), lambda i: (0, 0))
    return pl.pallas_call(
        functools.partial(gate_back_kernel, float(total)),
        grid=(rows // tile,),
        out_shape=(jax.ShapeDtypeStruct((rows, tokens), BF16),) * 2
        + (jax.ShapeDtypeStruct((8, rows), F32),),
        in_specs=[wide, wide, wide, line, line, pl.BlockSpec((tile, 1), lambda i: (i, 0))],
        out_specs=(wide, wide, pl.BlockSpec((8, tile), lambda i: (0, i))),
        compiler_params=params(40),
        cost_estimate=BRIEF,
    )(dyn, y, z, s, q, gain)


def head_terms(raw, hp_ref):
    pre = raw + hp_ref[:, 0:1]
    small = jnp.exp(-jnp.abs(pre))
    one = 1.0 + small
    away = one - 1.0
    log1p = jnp.where(away == 0.0, small, jnp.log(one) * (small / jnp.where(away == 0.0, 1.0, away)))
    dt = jnp.maximum(pre, 0.0) + log1p
    logistic = jnp.where(pre >= 0.0, 1.0, small) / one
    rows = lax.broadcasted_iota(jnp.int32, (Q, Q), 0)
    lanes = lax.broadcasted_iota(jnp.int32, (Q, Q), 1)
    upto = (rows <= lanes).astype(F32)
    logs = dt * hp_ref[:, 1:2]
    cums = dot(logs, upto, (((1,), (0,))), HIGH)
    return dt, logistic, cums


def to_columns(cums):
    n = cums.shape[0]
    square = jnp.concatenate([cums, jnp.zeros((Q - n, Q), F32)], axis=0)
    return square.T


def pair_bias(segr_ref, segc_ref):
    rows = lax.broadcasted_iota(jnp.int32, (Q, Q), 0)
    lanes = lax.broadcasted_iota(jnp.int32, (Q, Q), 1)
    keep = (segc_ref[...] == segr_ref[...]) & (rows <= lanes)
    return jnp.where(keep, 0.0, NEG)


def state_rows(place, own, other, r0):
    at = r0 % STATE
    rows = slice(at, at + HEAD)
    return jnp.where(place[0] == r0 // STATE, own[rows, :], other[rows, :])


def fwd_kernel(
    heads, given, place, xr_ref, bco_ref, bcs_ref, dt_ref, mask_ref, segr_ref, segc_ref, par_ref, hp_ref, *rest
):
    y_ref, xa_ref, u_ref, s_ref, prev, state, parb, xt = rest[given:]
    chans = heads * HEAD
    wide = chans + 2 * STATE

    @pl.when(pl.program_id(0) == 0)
    def _():
        for k in range(6):
            parb[k] = jnp.broadcast_to(par_ref[:, k : k + 1], (wide, Q))
        prev[...] = jnp.zeros_like(prev)
        state[...] = jnp.zeros_like(state)

    lane = lax.broadcasted_iota(jnp.int32, (HEAD, Q), 1)
    m1, m2, m3 = mask_ref[0:1, :], mask_ref[1:2, :], mask_ref[2:3, :]

    def conv(r0):
        rows = slice(r0, r0 + HEAD)
        cur = xr_ref[rows, :] if r0 < chans else state_rows(place, bco_ref, bcs_ref, r0 - chans)
        old = prev[rows, :]
        u = parb[4, rows, :] + parb[3, rows, :] * cur
        u = u + parb[2, rows, :] * (m1 * pltpu.roll(jnp.where(lane >= Q - 1, old, cur), 1, 1))
        u = u + parb[1, rows, :] * (m2 * pltpu.roll(jnp.where(lane >= Q - 2, old, cur), 2, 1))
        u = u + parb[0, rows, :] * (m3 * pltpu.roll(jnp.where(lane >= Q - 3, old, cur), 3, 1))
        prev[rows, :] = cur
        u_ref[rows, :] = u
        xa = (u * (0.5 * jnp.tanh(0.5 * u) + 0.5)).astype(BF16)
        xa_ref[rows, :] = xa
        return xa

    for r0 in range(chans, wide, HEAD):
        conv(r0)
    bt = xa_ref[chans : chans + STATE, :]
    ct = xa_ref[chans + STATE : wide, :]
    mix = dot(bt.T, ct, (((1,), (0,))))
    dt, _, cums = head_terms(dt_ref[...], hp_ref)
    cols = to_columns(cums)
    bias = pair_bias(segr_ref, segc_ref)
    enter = jnp.exp(cums) * mask_ref[3:4, :]
    last = jnp.broadcast_to(cums[:, Q - 1 : Q], cums.shape)
    tail = jnp.exp(last - cums) * mask_ref[4:5, :]
    passing = jnp.exp(last) * mask_ref[5:6, :]
    s_in = state[...].astype(BF16)
    s_ref[...] = s_in
    carried = dot(s_in, ct, (((1,), (0,))))
    for h in range(heads):
        rows = slice(h * HEAD, (h + 1) * HEAD)
        xa = conv(h * HEAD).astype(F32)
        decay = jnp.exp(cums[h : h + 1, :] - cols[:, h : h + 1] + bias)
        mixing = (mix * decay).astype(BF16)
        xd = xa * dt[h : h + 1, :]
        xt[rows, :] = (xd * tail[h : h + 1, :]).astype(BF16)
        y = dot(xd.astype(BF16), mixing, (((1,), (0,))))
        y = y + enter[h : h + 1, :] * carried[rows, :] + parb[5, rows, :] * xa
        y_ref[rows, :] = y
    fresh = dot(xt[...], bt, (((1,), (1,))))
    for h in range(heads):
        rows = slice(h * HEAD, (h + 1) * HEAD)
        state[rows, :] = state[rows, :] * passing[h : h + 1, :] + fresh[rows, :]


def scan_forward(place, xr, bco, bcs, dtr, masks, segr, segc, par, hp, heads, seqs, seq, given=()):
    chans, tokens = xr.shape
    padded = dtr.shape[0]
    wide = chans + 2 * STATE
    count = tokens // seqs // Q
    at = lambda k, p: (0, seq * count + k)
    swapped = lambda k, p: (0, (seqs - 1 - seq) * count + k)
    whole = lambda k, p: (0, 0)
    args = (xr, bco, bcs, dtr, masks, segr, segc, par, hp)
    return pl.pallas_call(
        functools.partial(fwd_kernel, heads, len(given)),
        out_shape=(
            jax.ShapeDtypeStruct((chans, tokens), F32),
            jax.ShapeDtypeStruct((wide, tokens), BF16),
            jax.ShapeDtypeStruct((wide, tokens), F32),
            jax.ShapeDtypeStruct((chans, tokens), BF16),
        ),
        grid_spec=pltpu.PrefetchScalarGridSpec(
            num_scalar_prefetch=1,
            grid=(count,),
            in_specs=[
                pl.BlockSpec((chans, Q), at),
                pl.BlockSpec((STATE, Q), at),
                pl.BlockSpec((STATE, Q), swapped),
                pl.BlockSpec((padded, Q), at),
                pl.BlockSpec((8, Q), at),
                pl.BlockSpec((1, Q), at),
                pl.BlockSpec((Q, 1), lambda k, p: (seq * count + k, 0)),
                pl.BlockSpec(par.shape, whole),
                pl.BlockSpec(hp.shape, whole),
            ]
            + [pl.BlockSpec(memory_space=pl.ANY)] * len(given),
            out_specs=(
                pl.BlockSpec((chans, Q), at),
                pl.BlockSpec((wide, Q), at),
                pl.BlockSpec((wide, Q), at),
                pl.BlockSpec((chans, STATE), at),
            ),
            scratch_shapes=[
                pltpu.VMEM((wide, Q), F32),
                pltpu.VMEM((chans, STATE), F32),
                pltpu.VMEM((6, wide, Q), F32),
                pltpu.VMEM((chans, Q), BF16),
            ],
        ),
        input_output_aliases={1 + len(args) + k: k for k in range(len(given))},
        compiler_params=params(58),
        cost_estimate=LONG,
    )(place, *args, *given)


def bwd_kernel(
    heads, late, place, xr_ref, bco_ref, bcs_ref, dt_ref, mask_ref, segr_ref, segc_ref, par_ref, hp_ref, xa_ref,
    u_ref, s_ref, dy_ref, y_ref, *rest,
):
    if late:
        dx_ref, dbc_ref, ddt_ref, cgo_ref, hg_ref, dstate_out, after_out = rest[:7]
    else:
        dstate_in, after_in, next_ref = rest[:3]
        dx_ref, dbc_ref, ddt_ref, cgo_ref, hg_ref = rest[6:11]
    dstate, parb, after, nmask, xt, dye, cg_ref = rest[-7:]
    chans = heads * HEAD
    wide = chans + 2 * STATE
    seq, block = pl.program_id(0), pl.program_id(1)
    final = block == pl.num_programs(1) - 1

    @pl.when((seq == 0) & (block == 0))
    def _():
        for k in range(6):
            parb[k] = jnp.broadcast_to(par_ref[:, k : k + 1], (wide, Q))
        cg_ref[...] = jnp.zeros_like(cg_ref)
        hg_ref[...] = jnp.zeros_like(hg_ref)

    @pl.when(block == 0)
    def _():
        if late:
            dstate[...] = jnp.zeros_like(dstate)
            after[...] = jnp.zeros_like(after)
            nmask[...] = jnp.zeros_like(nmask)
        else:
            dstate[...] = dstate_in[...]
            after[...] = after_in[...]
            nmask[...] = next_ref[...]

    lane = lax.broadcasted_iota(jnp.int32, (HEAD, Q), 1)
    lane8 = lax.broadcasted_iota(jnp.int32, (8, Q), 1)
    sub8 = lax.broadcasted_iota(jnp.int32, (8, Q), 0)
    masks = mask_ref[...]
    shifted_masks = jnp.where(lane8 <= sub8, nmask[...], masks)
    nmask[...] = masks

    def conv_back(r0, dxa, out, out0):
        rows = slice(r0, r0 + HEAD)
        u = u_ref[rows, :]
        sig = 0.5 * jnp.tanh(0.5 * u) + 0.5
        dc = dxa * (sig * (1.0 + u * (1.0 - sig)))
        xr = xr_ref[rows, :] if r0 < chans else state_rows(place, bco_ref, bcs_ref, r0 - chans)
        old = after[rows, :]
        after[rows, :] = dc
        dx = parb[3, rows, :] * dc
        cg_ref[4, rows, :] += dc
        cg_ref[3, rows, :] += xr * dc
        for k in (1, 2, 3):
            e = jnp.where(lane < k, old, dc) * shifted_masks[k - 1 : k, :]
            e = pltpu.roll(e, Q - k, 1)
            dx = dx + parb[3 - k, rows, :] * e
            cg_ref[3 - k, rows, :] += xr * e
        out[out0 : out0 + HEAD, :] = dx.astype(out.dtype)

    bt = xa_ref[chans : chans + STATE, :]
    ct = xa_ref[chans + STATE : wide, :]
    mix = dot(bt.T, ct, (((1,), (0,))))
    dt, logistic, cums = head_terms(dt_ref[...], hp_ref)
    cols = to_columns(cums)
    bias = pair_bias(segr_ref, segc_ref)
    enter = jnp.exp(cums) * masks[3:4, :]
    last = jnp.broadcast_to(cums[:, Q - 1 : Q], cums.shape)
    tail = jnp.exp(last - cums) * masks[4:5, :]
    passing = jnp.exp(last) * masks[5:6, :]
    ds = dstate[...].astype(BF16)
    spread = dot(ds, bt, (((1,), (0,))))
    dmix = jnp.zeros((Q, Q), F32)
    s_in = s_ref[...]
    direct, cross, skip, outward, through, inward = [], [], [], [], [], []
    for h in range(heads):
        rows = slice(h * HEAD, (h + 1) * HEAD)
        xa = xa_ref[rows, :].astype(F32)
        dyb = dy_ref[rows, :]
        dy = dyb.astype(F32)
        decay = jnp.exp(cums[h : h + 1, :] - cols[:, h : h + 1] + bias)
        mixing = (mix * decay).astype(BF16)
        xd = xa * dt[h : h + 1, :]
        xdb = xd.astype(BF16)
        xt[rows, :] = (xd * tail[h : h + 1, :]).astype(BF16)
        dye[rows, :] = (dy * enter[h : h + 1, :]).astype(BF16)
        dmix = dmix + dot(xdb, dyb, (((0,), (0,)))) * decay
        near = dot(dyb, mixing, (((1,), (1,))))
        far = tail[h : h + 1, :] * spread[rows, :]
        pull = near + far
        direct.append(jnp.sum(xa * pull, axis=0, keepdims=True))
        cross.append(jnp.sum(xdb.astype(F32) * near, axis=0, keepdims=True))
        outward.append(jnp.sum(xd * far, axis=0, keepdims=True))
        through.append(jnp.sum(dstate[rows, :] * s_in[rows, :].astype(F32), axis=0, keepdims=True))
        skip.append(jnp.sum(xa * dy, axis=0, keepdims=True))
        inward.append(jnp.sum(y_ref[rows, :] * dy, axis=0, keepdims=True))
        dxa = dt[h : h + 1, :] * pull + parb[5, rows, :] * dy
        conv_back(h * HEAD, dxa, dx_ref, h * HEAD)
    pad = ddt_ref.shape[0] - heads
    if pad:
        zero = [jnp.zeros((pad, Q), F32)]
        direct, cross, skip = direct + zero, cross + zero, skip + zero
        outward, through, inward = outward + zero, through + zero, inward + zero
    direct, cross, skip, outward, through, inward = (
        jnp.concatenate(v, axis=0) for v in (direct, cross, skip, outward, through, inward)
    )
    dlog = inward - hp_ref[:, 2:3] * skip - cross
    rows = lax.broadcasted_iota(jnp.int32, (Q, Q), 0)
    lanes = lax.broadcasted_iota(jnp.int32, (Q, Q), 1)
    dl = dot(dlog, (rows >= lanes).astype(F32), (((1,), (0,))), HIGH)
    dl = dl + dot(outward, (rows < lanes).astype(F32), (((1,), (0,))), HIGH)
    dl = dl + passing * jnp.sum(through, axis=1, keepdims=True)
    ddt = (direct + hp_ref[:, 1:2] * dl) * logistic
    ddt_ref[...] = ddt.astype(BF16)
    hg_ref[0] += ddt
    hg_ref[1] += dt * dl
    hg_ref[2] += skip
    dmixb = dmix.astype(BF16)
    xtv, dyev = xt[...], dye[...]
    dbt = dot(ct, dmixb, (((1,), (1,)))) + dot(ds, xtv, (((0,), (0,))))
    dct = dot(bt, dmixb, (((1,), (0,)))) + dot(s_ref[...], dyev, (((0,), (0,))))
    dbca = jnp.concatenate([dbt, dct], axis=0)
    for r0 in range(0, 2 * STATE, HEAD):
        conv_back(chans + r0, dbca[r0 : r0 + HEAD, :], dbc_ref, r0)
    fresh = dot(dyev, ct, (((1,), (1,))))
    for h in range(heads):
        rows = slice(h * HEAD, (h + 1) * HEAD)
        dstate[rows, :] = dstate[rows, :] * passing[h : h + 1, :] + fresh[rows, :]

    if late:

        @pl.when(final)
        def _():
            dstate_out[...] = dstate[...]
            after_out[...] = after[...]

    @pl.when((seq == pl.num_programs(0) - 1) & final)
    def _():
        for r0 in range(0, wide, HEAD):
            rows = slice(r0, r0 + HEAD)
            for k in range(5):
                cgo_ref[rows, k : k + 1] = jnp.sum(cg_ref[k, rows, :], axis=1, keepdims=True)


def scan_backward(
    place, xr, bco, bcs, dtr, masks, segr, segc, par, hp, xa, u, s_in, dy, y, heads, seqs, carry=(), given=()
):
    chans, tokens = xr.shape
    padded = dtr.shape[0]
    wide = chans + 2 * STATE
    count = tokens // seqs // Q
    late = not carry
    last = count - 1 if late else count // 2 - 1
    at = lambda s, k, p: (0, s * count + last - k)
    swapped = lambda s, k, p: (0, (seqs - 1 - s) * count + last - k)
    whole = lambda s, k, p: (0, 0)
    by_seq = lambda s, k, p: (s, 0)
    args = (xr, bco, bcs, dtr, masks, segr, segc, par, hp, xa, u, s_in, dy, y)
    if not late:
        args = (*args, *carry, masks)
    carried = [pl.BlockSpec((chans, STATE), by_seq), pl.BlockSpec((wide, Q), by_seq)]
    extra = [] if late else carried + [pl.BlockSpec((8, Q), lambda s, k, p: (0, s * count + count // 2))]
    shapes = (
        jax.ShapeDtypeStruct((chans, tokens), BF16),
        jax.ShapeDtypeStruct((2 * STATE, tokens), BF16),
        jax.ShapeDtypeStruct((padded, tokens), BF16),
        jax.ShapeDtypeStruct((wide, 8), F32),
        jax.ShapeDtypeStruct((3, padded, Q), F32),
    )
    if late:
        shapes += (
            jax.ShapeDtypeStruct((seqs * chans, STATE), F32),
            jax.ShapeDtypeStruct((seqs * wide, Q), F32),
        )
    return pl.pallas_call(
        functools.partial(bwd_kernel, heads, late),
        out_shape=shapes,
        grid_spec=pltpu.PrefetchScalarGridSpec(
            num_scalar_prefetch=1,
            grid=(seqs, count // 2),
            in_specs=[
                pl.BlockSpec((chans, Q), at),
                pl.BlockSpec((STATE, Q), at),
                pl.BlockSpec((STATE, Q), swapped),
                pl.BlockSpec((padded, Q), at),
                pl.BlockSpec((8, Q), at),
                pl.BlockSpec((1, Q), at),
                pl.BlockSpec((Q, 1), lambda s, k, p: (s * count + last - k, 0)),
                pl.BlockSpec(par.shape, whole),
                pl.BlockSpec(hp.shape, whole),
                pl.BlockSpec((wide, Q), at),
                pl.BlockSpec((wide, Q), at),
                pl.BlockSpec((chans, STATE), at),
                pl.BlockSpec((chans, Q), at),
                pl.BlockSpec((chans, Q), at),
            ]
            + extra
            + [pl.BlockSpec(memory_space=pl.ANY)] * len(given),
            out_specs=[
                pl.BlockSpec((chans, Q), at),
                pl.BlockSpec((2 * STATE, Q), at),
                pl.BlockSpec((padded, Q), at),
                pl.BlockSpec((wide, 8), whole),
                pl.BlockSpec((3, padded, Q), lambda s, k, p: (0, 0, 0)),
            ]
            + (carried if late else []),
            scratch_shapes=[
                pltpu.VMEM((chans, STATE), F32),
                pltpu.VMEM((6, wide, Q), F32),
                pltpu.VMEM((wide, Q), F32),
                pltpu.VMEM((8, Q), F32),
                pltpu.VMEM((chans, Q), BF16),
                pltpu.VMEM((chans, Q), BF16),
                pltpu.VMEM((5, wide, Q), F32),
            ],
        ),
        input_output_aliases={1 + len(args) + k: k for k in range(len(given))},
        compiler_params=params(58),
        cost_estimate=LONG,
    )(place, *args, *given)


def block_masks(segs, seqs):
    s = segs.reshape(seqs, -1)
    length = s.shape[1]
    rows = []
    for k in (1, 2, 3):
        old = jnp.pad(s, ((0, 0), (k, 0)), constant_values=-1)[:, :length]
        rows.append(old == s)
    b = s.reshape(seqs, length // Q, Q)
    ends = b[:, :, -1:]
    before = jnp.concatenate([jnp.full((seqs, 1, 1), -1, s.dtype), ends[:, :-1]], axis=1)
    rows += [b == before, b == ends, jnp.broadcast_to(ends == before, b.shape)]
    rows = [r.reshape(1, -1).astype(F32) for r in rows]
    return jnp.concatenate(rows + [jnp.zeros((2, segs.shape[0]), F32)], axis=0)


def local(
    hidden, segment_ids, cotangent, w_zx, w_dt, w_bc, w_out, conv_x, conv_bias_x, conv_bc, conv_bias_bc,
    dt_bias, a_log, d_skip, pre_gain, gate_gain,
):
    n_dp, n_t = lax.axis_size("dp"), lax.axis_size("tensor")
    t_index = lax.axis_index("tensor")
    ring = Ring(n_dp)
    core = ring.core
    mine, width = hidden.shape
    inner_here = w_zx.shape[2]
    chans = inner_here // 2
    heads = w_dt.shape[1] // 2
    padded = max(16, heads)
    wide = chans + 2 * STATE
    inner_all = inner_here * n_t
    dd = 2 * w_zx.shape[1]

    def tensor_sum(v):
        if n_t == 2:
            return v + lax.ppermute(v, "tensor", [(0, 1), (1, 0)])
        return lax.psum(v, "tensor")

    def over_tensor(v):
        if n_t == 2:
            return v.astype(F32) + lax.ppermute(v, "tensor", [(0, 1), (1, 0)]).astype(F32)
        return lax.psum(v.astype(F32), "tensor")

    def pick(v, which, axis=0):
        size = v.shape[axis] // 2
        return lax.dynamic_slice_in_dim(v, which * size, size, axis)

    def in_order(own, other, axis):
        return jnp.where(
            core == 0, jnp.concatenate([own, other], axis), jnp.concatenate([other, own], axis)
        )

    pad_dt = lambda v: jnp.pad(v, ((0, 0), (0, STATE - heads)))
    small = jnp.concatenate([w_bc, pad_dt(w_dt[:, :heads]), pad_dt(w_dt[:, heads:])], axis=1)
    zx_other = ring.swap(w_zx)
    small_other = ring.swap(small)
    place = core.reshape(1).astype(jnp.int32)
    ux = prep_x(place, w_zx, zx_other, small, small_other, padded)
    cut = chans // 2
    gx = Gather(ring, ux, "both", cut)
    gx.step()

    hiddens = [hidden, ring.swap(after(hidden, ux))]

    def norm(h):
        h = h.astype(F32)
        return (h * lax.rsqrt(jnp.mean(h * h, -1, keepdims=True) + EPS) * pre_gain).astype(BF16)

    normed = [norm(h) for h in hiddens]
    segs = jnp.concatenate([segment_ids, ring.swap(after(segment_ids, ux))])
    masks = block_masks(segs, 2)
    segr, segc = segs[None, :], segs[:, None]
    offs = ring.offsets(dd)
    table = ring.table()

    def own_chans(v):
        return pick(v, core, v.ndim - 1)

    taps = jnp.concatenate([own_chans(conv_x), conv_bc], axis=1)
    biases = jnp.concatenate([own_chans(conv_bias_x), conv_bias_bc])
    skips = jnp.repeat(own_chans(d_skip), HEAD)
    par = jnp.concatenate(
        [taps, biases[None], jnp.pad(skips, (0, 2 * STATE))[None], jnp.zeros((2, wide), F32)], axis=0
    ).T
    a_own = -jnp.exp(own_chans(a_log))
    spot = lax.broadcasted_iota(jnp.int32, (padded, 128), 1) - core * heads
    spot = (spot == lax.broadcasted_iota(jnp.int32, (padded, 128), 0)).astype(F32)
    spots = jnp.concatenate([spot, spot * jnp.pad(a_own, (0, padded - heads))[:, None], spot])
    hp = jnp.stack([own_chans(dt_bias), a_own, own_chans(d_skip)], axis=1)
    hp = jnp.pad(hp, ((0, padded - heads), (0, 5)))
    gain = own_chans(gate_gain)[:, None]

    out_other = ring.swap(after(w_out, ux))
    uz, uo = prep_zo(place, w_zx, zx_other, w_out, out_other)
    cots = [cotangent, ring.swap(after(cotangent, uz))]

    gx.step()
    gx.step()
    third = gx.newest()
    gx.finish()
    gz = Gather(ring, after(uz, *third), "right")
    came = gz.step()

    across = [(2 * i + t, 2 * (i ^ 1) + 1 - t) for i in range(n_dp) for t in range(2)]

    def wave(v):
        turned = jnp.concatenate([v[:, mine:], v[:, :mine]], axis=1)
        if n_t != 2:
            return tensor_sum(v + ring.swap(turned))
        return (
            v
            + ring.swap(turned)
            + lax.ppermute(v, "tensor", [(0, 1), (1, 0)])
            + lax.ppermute(turned, ("dp", "tensor"), across)
        )

    def tensor_other(v):
        if n_t == 2:
            return lax.ppermute(v, "tensor", [(0, 1), (1, 0)])
        return (lax.psum(v.astype(F32), "tensor") - v.astype(F32)).astype(BF16)

    def joined(own, came):
        return (own.astype(F32) + came.astype(F32)).astype(BF16)

    blocks = gx.blocks()
    gz.step(*gx.last)
    w_states = Weight(blocks, chans, STATE, cut)
    xr, bc_own, dtr = after(
        x_projection(
            Weight(blocks, 0, chans + STATE + padded, cut), chans, normed, after(offs, *came, *gx.last)
        ),
        *gz.newest(),
    )
    bc_other = ring.swap(bc_own)
    gz.step()
    scan_args = (bc_own, bc_other, dtr, masks, segr, segc, par, hp)
    half = after(scan_forward(place, xr, *scan_args, heads, 2, 0), *gz.newest())
    gz.finish(half[0])
    wb_own = whole_rows(w_states, after(offs, half[0]), width)
    wb_other = ring.swap(wb_own)
    go = Gather(ring, after(uo, half[0]), "left")
    go.left()
    y, xa, u, s_in = after(
        scan_forward(place, after(xr, wb_own), *scan_args, heads, 2, 1, half), *gz.last, go.l[-1], wb_other
    )
    go.step(y)
    z, squares = after(
        gate_projection(Weight(gz.blocks(), 0, chans), normed, after(offs, y), y), *go.newest()
    )
    go.step(squares)
    total_sq = wave(squares)
    s = lax.rsqrt(total_sq / inner_all + EPS)
    ynt = (y * (z * sigmoid(z)) * s * gain).astype(BF16)
    ynt = after(ynt, *go.newest())
    go.right()
    go.finish()
    ro = Scatter(ring, terms(ring, table, ynt, cots, dd))

    weight_o = Weight(go.blocks(), 0, chans)
    dyn, q = after(
        back_projection(weight_o, cots, after(offs, *ro.out), y, z, gain), *ro.got
    )
    sent_o = ro.step(q)
    q_total = wave(after(q, *sent_o))
    out_own, out_rest = after(back([(weight_o, ynt)], after(offs, *sent_o), width), *ro.got, q_total)
    sent_o = ro.step(out_own)
    out_came = ring.swap(out_rest)
    dzt, dyt, dgain = gate_back(inner_all, after(dyn, *sent_o), y, z, s, q_total, gain)
    parts_z = after(terms(ring, table, dzt, normed, dd), *ro.got, out_came)
    half = mine // 2
    sent_o = ro.step(parts_z[1])
    rz = Scatter(ring, after(parts_z, *sent_o))
    out_own, out_came = after((out_own, out_came), *sent_o)
    out_late = joined(out_own[half:], out_came[half:])
    out_early = joined(out_own[:half], out_came[:half])

    def dn_part(part, *others):
        return back(
            [
                (Weight(gz.blocks(), 0, chans), dzt),
                (Weight(blocks, 0, chans, cut), dxt),
                (Weight(blocks, chans + STATE, padded, cut), ddt_low),
            ],
            after(offs, *others), width, 2, part, hiddens,
            (dbc_low, wb_own, wb_other, place), 58,
        )

    scan_args = (*scan_args, xa, u, s_in)
    out_late_other = tensor_other(out_late)
    first = after(
        scan_backward(place, xr, *scan_args, after(dyt, *rz.out, out_late, out_early), y, heads, 2),
        *ro.got, *rz.got,
    )
    sent_z = rz.step(first[3])
    dxt, dbc_low, ddt_low = first[:3]
    out_early_other = tensor_other(after(out_early, *sent_z))
    late_own, late_rest, late_pre = after(dn_part(1, *sent_z), *rz.got, out_late_other)
    sent_z = rz.step(late_own)
    late_came = ring.swap(late_rest)
    second = after(
        scan_backward(place, xr, *scan_args, after(dyt, *sent_z), y, heads, 2, first[5:], first[:3]),
        *rz.got, out_early_other, late_came,
    )
    dxt, dbc_low, ddt_low = second[:3]
    sent_z = rz.step(ddt_low)
    dbc_came = ring.swap(after(dbc_low, *sent_z)[:, mine:])
    late_own = joined(late_own, after(late_came, *sent_z))
    late_other = tensor_other(late_own)
    parts_x = after(terms(ring, table, after(dxt, *sent_z, late_own), normed, dd), *rz.got, dbc_came)
    rx = Scatter(ring, parts_x)
    dbc_own = joined(dbc_low[:, :mine], after(dbc_came, *parts_x))
    dbc_other = tensor_other(dbc_own)
    early_own, early_rest, early_pre = after(
        dn_part(0, *rx.out, dbc_own), *rx.got, late_other, dbc_other
    )

    sent_x = rx.step(early_own)
    early_came = ring.swap(early_rest)
    early_own = joined(after(early_own, *sent_x), early_came)
    early_other = tensor_other(early_own)
    dbc_own = joined(dbc_own, after(dbc_other, early_own))
    bc_cols = 2 * STATE // n_t
    states = lax.dynamic_slice_in_dim(dbc_own, t_index * bc_cols, bc_cols, 0)
    products, give = small_terms(place, states, ddt_low, normed, n_dp)
    products_came = ring.swap(give)
    common = gathered_sums(
        first[3], second[3], dgain, first[4], after(second[4], products), spots, early_pre, late_pre
    )
    common_came = ring.doubling(common, 1)
    keep_o, give_o = ro.finish(place, common)
    keep_z, give_z = rz.finish(place, keep_o)
    give_both = jnp.concatenate([give_o, give_z])
    products, give_both = after((products, give_both), *rx.got, products_came, common_came)
    common, products = common + common_came, products + products_came.astype(F32)

    sent_x = rx.step(give_both)
    common_came = ring.doubling(after(common, *sent_x), 2)
    products, products_came = ring.halving(after(products, *sent_x), 1)
    output = residual(
        (out_late, out_late_other), (out_early, out_early_other), after(hidden, *sent_x)
    )
    output, common, products = after(
        (output, common, products), *rx.got, common_came, products_came, early_other
    )
    common, products = common + common_came, products + products_came.astype(F32)

    sent_x = rx.step(output)
    common_came = ring.doubling(after(common, *sent_x), 4)
    products, products_came = ring.halving(after(products, *sent_x), 2)
    other_both = ring.swap(after(give_both, *sent_x))
    grad_hidden = norm_back(
        (after(late_own, *sent_x), late_other), (early_own, early_other), hidden, cotangent, pre_gain[None]
    )
    grad_hidden, common, products, other_both = after(
        (grad_hidden, common, products, other_both), *rx.got, common_came, products_came, other_both
    )
    common, products = common + common_came, products + products_came.astype(F32)
    dist = 8
    while dist < ring.n:
        common = common + ring.doubling(common, dist)
        dist *= 2
    dist = 4
    while dist < ring.n // 2:
        products, products_came = ring.halving(products, dist)
        products = products + products_came.astype(F32)
        dist *= 2

    keep_x, give_x = rx.finish(place, grad_hidden)
    other_x = ring.swap(give_x)
    products, products_came = ring.halving(after(products, keep_x), ring.n // 2)
    sum_small = products + products_came.astype(F32)
    common = after(common, keep_x)
    other = ring.swap(common)
    if n_t == 2:
        everyone = (
            lax.ppermute(common, "tensor", [(0, 1), (1, 0)]), lax.ppermute(common, ("dp", "tensor"), across)
        )
    else:
        everyone = (tensor_sum(common + other),)
    grad_zx, grad_dt, grad_bc, *sums = finals(
        place, keep_z, other_both, keep_x, other_x, sum_small, common, other, everyone, heads, padded, width
    )
    grad_out = in_order(keep_o, other_both[:chans], 0)
    taps, bias, taps_bc, bias_bc, grad_dt_bias, grad_a_log, grad_d_skip, grad_pre, grad_gate = sums
    return (
        output, grad_hidden, grad_zx, grad_dt, grad_bc, grad_out, taps, bias[0], taps_bc, bias_bc[0],
        grad_dt_bias[0], grad_a_log[0], grad_d_skip[0], grad_pre[0], grad_gate[0],
    )


def solution(mesh):
    in_specs = (
        P("dp", None), P("dp"), P("dp", None), P(None, "dp", "tensor"), P("dp", "tensor"), P("dp", None),
        P("tensor", "dp"), P(None, "tensor"), P("tensor"), P(), P(), P("tensor"), P("tensor"), P("tensor"),
        P(), P("tensor"),
    )
    out_specs = (
        P("dp", None), P("dp", None), P(None, "dp", "tensor"), P("dp", "tensor"), P("dp", "tensor"),
        P("tensor", "dp"), P(None, "tensor"), P("tensor"), P(), P(), P("tensor"), P("tensor"), P("tensor"),
        P(), P("tensor"),
    )
    return jax.shard_map(local, mesh=mesh, in_specs=in_specs, out_specs=out_specs, check_vma=False)
```

```python
import functools

import jax
import jax.numpy as jnp
from jax import lax
from jax.experimental import pallas as pl
from jax.experimental.pallas import tpu as pltpu
from jax.sharding import PartitionSpec as P

EPS = 1e-05
Q = 128
NEG = -1e30
F32 = jnp.float32
BF16 = jnp.bfloat16
HIGH = lax.Precision.HIGHEST
MIB = 1024 * 1024
HEAD = 64
STATE = 128


LONG = pl.CostEstimate(flops=30_000_000_000, bytes_accessed=1, transcendentals=0)
BRIEF = pl.CostEstimate(flops=1, bytes_accessed=1, transcendentals=0)


def dot(a, b, dims, precision=None):
    return lax.dot_general(a, b, (dims, ((), ())), precision=precision, preferred_element_type=F32)


def lane_sums(v):
    return dot(jnp.ones((8, v.shape[1]), F32), v, (((1,), (1,))), HIGH)


def params(mib):
    return pltpu.CompilerParams(vmem_limit_bytes=mib * MIB)


def after(value, *others):
    return lax.optimization_barrier((value, others))[0]


def ring_order(chips):
    if chips == 8:
        return [0, 2, 4, 6, 7, 5, 3, 1]
    half = chips // 2
    return list(range(half)) + list(range(chips - 1, half - 1, -1))


class Ring:
    def __init__(self, n_dp):
        self.n = n_dp // 2
        self.order = ring_order(self.n)
        place = [0] * self.n
        for position, chip in enumerate(self.order):
            place[chip] = position
        me = lax.axis_index("dp")
        self.core = me % 2
        self.mine = me // 2
        self.pos = jnp.asarray(place, jnp.int32)[self.mine]
        self.right = self.perm(1)
        self.left = self.perm(-1)
        self.full = self.n // 2 - 1

    def perm(self, step):
        pairs = []
        for p in range(self.n):
            for c in range(2):
                pairs.append((self.order[p] * 2 + c, self.order[(p + step) % self.n] * 2 + c))
        return pairs

    def table(self):
        table = [[self.order[(p + s) % self.n] for s in range(self.n)] for p in range(self.n)]
        row = lax.dynamic_index_in_dim(jnp.asarray(table, jnp.int32), self.pos, 0, keepdims=False)
        return jnp.concatenate([row, self.core.reshape(1).astype(jnp.int32)])

    def offsets(self, dd):
        steps = [0] + [-k for k in range(1, self.full + 1)] + list(range(1, self.full + 1)) + [self.n // 2]
        table = [[self.order[(p + s) % self.n] * dd for s in steps] for p in range(self.n)]
        return lax.dynamic_index_in_dim(jnp.asarray(table, jnp.int32), self.pos, 0, keepdims=False)

    def go_right(self, v):
        return lax.ppermute(v, "dp", self.right)

    def go_left(self, v):
        return lax.ppermute(v, "dp", self.left)

    def swap(self, v):
        return lax.ppermute(v, "dp", [(i, i ^ 1) for i in range(2 * self.n)])

    def halving(self, v, dist):
        pairs = [(i, i ^ (2 * dist)) for i in range(2 * self.n)]
        keep, give = self.halves(v, (self.mine // dist) % 2)
        return keep, lax.ppermute(give.astype(BF16), "dp", pairs)

    def doubling(self, v, dist):
        return lax.ppermute(v, "dp", [(i, i ^ (2 * dist)) for i in range(2 * self.n)])

    def halves(self, v, bit):
        size = v.shape[1] // 2
        return (
            lax.dynamic_slice_in_dim(v, bit * size, size, 1),
            lax.dynamic_slice_in_dim(v, (1 - bit) * size, size, 1),
        )


class Gather:
    def __init__(self, ring, unit, far, cut=None):
        self.ring, self.far, self.cut = ring, far, cut
        self.r, self.l = [unit], [unit]
        self.last = []

    def right(self, *others):
        if len(self.r) <= self.ring.full:
            v = after(self.r[-1], *others) if others else self.r[-1]
            self.r.append(self.ring.go_right(v))
        return self.r[-1]

    def left(self, *others):
        if len(self.l) <= self.ring.full:
            v = after(self.l[-1], *others) if others else self.l[-1]
            self.l.append(self.ring.go_left(v))
        return self.l[-1]

    def step(self, *others):
        return self.right(*others), self.left(*others)

    def newest(self):
        return self.r[-1], self.l[-1]

    def finish(self, *others):
        while len(self.r) <= self.ring.full:
            self.right()
        while len(self.l) <= self.ring.full:
            self.left()
        r, l, cut = self.r[-1], self.l[-1], self.cut
        if others:
            r, l = after(r, *others), after(l, *others)
        if self.far == "both":
            self.last = [self.ring.go_right(r[:cut]), self.ring.go_left(l[cut:])]
        elif self.far == "right":
            self.last = [self.ring.go_right(r)]
        else:
            self.last = [self.ring.go_left(l)]
        return self.last

    def blocks(self):
        return self.r + self.l[1:] + self.last


def both_parts(vt, own, other):
    half = own.shape[0]
    return dot(vt[:, :half], own[...], (((1,), (0,)))) + dot(vt[:, half:], other[...], (((1,), (0,))))


def terms_kernel(table, vt, own, other, *outs):
    total = both_parts(vt, own, other).astype(BF16)
    top, bottom = outs[:2]
    half = top.shape[0]
    s = pl.program_id(0)

    @pl.when(s == 0)
    def _():
        top[...] = total[:half]
        bottom[...] = total[half:]

    for k, out in enumerate(outs[2:]):

        @pl.when((s == 1 + 2 * k) | (s == 2 + 2 * k))
        def _():
            out[0] = total


def terms(ring, table, vt, acts, dd):
    rows, tokens = vt.shape
    n, full = ring.n, ring.full
    half = n // 2

    def step(s):
        j = full - (s - 1) // 2
        at = jnp.where(s == 0, half, jnp.where(s % 2 == 1, j, n - j))
        return jnp.where(s == n - 1, 0, at)

    column = pl.BlockSpec((tokens // 2, dd), lambda s, t: (0, t[step(s)]))
    part = pl.BlockSpec((rows // 2, dd), lambda s, t: (0, 0))
    pair = lambda k: pl.BlockSpec((1, rows, dd), lambda s, t: (jnp.clip(s - 1 - 2 * k, 0, 1), 0, 0))
    single = pl.BlockSpec((1, rows, dd), lambda s, t: (0, 0, 0))
    return pl.pallas_call(
        terms_kernel,
        out_shape=tuple([jax.ShapeDtypeStruct((rows // 2, dd), BF16)] * 2)
        + tuple([jax.ShapeDtypeStruct((2, rows, dd), BF16)] * full)
        + (jax.ShapeDtypeStruct((1, rows, dd), BF16),),
        grid_spec=pltpu.PrefetchScalarGridSpec(
            num_scalar_prefetch=1,
            grid=(n,),
            in_specs=[pl.BlockSpec((rows, tokens), lambda s, t: (0, 0)), column, column],
            out_specs=tuple([part, part] + [pair(k) for k in range(full)] + [single]),
        ),
        compiler_params=params(24),
        cost_estimate=LONG,
    )(table, vt, *acts)


def first_add_kernel(own, r, l, out_r, out_l):
    half = r.shape[0]
    out_r[:half] = (own[0, :half].astype(F32) + r[...].astype(F32)).astype(BF16)
    out_r[half:] = own[0, half:]
    out_l[:half] = own[1, :half]
    out_l[half:] = (own[1, half:].astype(F32) + l[...].astype(F32)).astype(BF16)


def add_kernel(own, r, l, out_r, out_l):
    out_r[...] = (own[0].astype(F32) + r[...].astype(F32)).astype(BF16)
    out_l[...] = (own[1].astype(F32) + l[...].astype(F32)).astype(BF16)


def last_add_kernel(place, own, r, l, keep, give):
    total = own[0].astype(F32) + r[...].astype(F32) + l[...].astype(F32)
    dd = keep.shape[1]
    low, high = total[:, :dd], total[:, dd:]
    keep[...] = jnp.where(place[0] == 0, low, high)
    give[...] = jnp.where(place[0] == 0, high, low)


class Scatter:
    def __init__(self, ring, parts):
        self.ring = ring
        top, bottom, *self.own = parts
        self.left_to_do = ring.full
        self.send(top, bottom)

    def send(self, r, l):
        self.out = (r, l)
        self.got = (self.ring.go_right(r), self.ring.go_left(l))

    def step(self, *others):
        if not self.left_to_do:
            return self.out
        j = self.left_to_do
        self.left_to_do -= 1
        own = self.own[self.ring.full - j]
        rows, dd = own.shape[1:]
        got = after(self.got, *others) if others else self.got
        whole = lambda shape: pl.BlockSpec(shape, lambda i: (0,) * len(shape))
        out = pl.pallas_call(
            first_add_kernel if j == self.ring.full else add_kernel,
            grid=(1,),
            out_shape=(jax.ShapeDtypeStruct((rows, dd), BF16),) * 2,
            in_specs=[whole(v.shape) for v in (own, *got)],
            out_specs=(whole((rows, dd)),) * 2,
            compiler_params=params(16),
            cost_estimate=BRIEF,
        )(own, *got)
        self.send(*out)
        return self.out

    def finish(self, place, *others, cost=BRIEF):
        while self.left_to_do:
            self.step()
        own = self.own[-1]
        rows, dd = own.shape[1:]
        got = after(self.got, *others) if others else self.got
        whole = lambda shape: pl.BlockSpec(shape, lambda i, p: (0,) * len(shape))
        return pl.pallas_call(
            last_add_kernel,
            out_shape=(jax.ShapeDtypeStruct((rows, dd // 2), F32),) * 2,
            grid_spec=pltpu.PrefetchScalarGridSpec(
                num_scalar_prefetch=1,
                grid=(1,),
                in_specs=[whole(v.shape) for v in (own, *got)],
                out_specs=(whole((rows, dd // 2)),) * 2,
            ),
            compiler_params=params(16),
            cost_estimate=cost,
        )(place, own, *got)


def prep_x_kernel(place, own, other, small_own, small_other, out):
    core = place[0]
    dd = own.shape[1]
    chans = own.shape[2] // 2
    padded = out.shape[0] - chans - STATE
    for b in range(2):
        lanes = slice(b * dd, (b + 1) * dd)
        near = core == b
        src = jnp.where(near, own[0], other[0])
        src = jnp.where(core == 0, src[:, :chans], src[:, chans:])
        out[:chans, lanes] = src.T
        small = jnp.where(near, small_own[...], small_other[...])
        states = jnp.where(core == 0, small[:, :STATE], small[:, STATE : 2 * STATE])
        out[chans : chans + STATE, lanes] = states.T
        steps = jnp.where(core == 0, small[:, 2 * STATE : 3 * STATE], small[:, 3 * STATE :])
        out[chans + STATE :, lanes] = steps.T[:padded]


def prep_x(place, own, other, small_own, small_other, padded):
    _, dd, inner = own.shape
    rows = inner // 2 + STATE + padded
    return pl.pallas_call(
        prep_x_kernel,
        out_shape=jax.ShapeDtypeStruct((rows, 2 * dd), BF16),
        grid_spec=pltpu.PrefetchScalarGridSpec(
            num_scalar_prefetch=1,
            grid=(1,),
            in_specs=[pl.BlockSpec((1, dd, inner), lambda i, p: (1, 0, 0))] * 2
            + [pl.BlockSpec((dd, 4 * STATE), lambda i, p: (0, 0))] * 2,
            out_specs=pl.BlockSpec((rows, 2 * dd), lambda i, p: (0, 0)),
        ),
        compiler_params=params(12),
        cost_estimate=BRIEF,
    )(place, own, other, small_own, small_other)


def prep_zo_kernel(place, own, other, out_own, out_other, z, o):
    core = place[0]
    dd = own.shape[1]
    chans = own.shape[2] // 2
    for b in range(2):
        lanes = slice(b * dd, (b + 1) * dd)
        near = core == b
        src = jnp.where(near, own[0], other[0])
        src = jnp.where(core == 0, src[:, :chans], src[:, chans:])
        z[:, lanes] = src.T
        src = jnp.where(near, out_own[...], out_other[...])
        o[:, lanes] = jnp.where(core == 0, src[:chans], src[chans:])


def prep_zo(place, own, other, out_own, out_other):
    _, dd, inner = own.shape
    shape = (inner // 2, 2 * dd)
    return pl.pallas_call(
        prep_zo_kernel,
        out_shape=(jax.ShapeDtypeStruct(shape, BF16),) * 2,
        grid_spec=pltpu.PrefetchScalarGridSpec(
            num_scalar_prefetch=1,
            grid=(1,),
            in_specs=[pl.BlockSpec((1, dd, inner), lambda i, p: (0, 0, 0))] * 2
            + [pl.BlockSpec((inner, dd), lambda i, p: (0, 0))] * 2,
            out_specs=(pl.BlockSpec(shape, lambda i, p: (0, 0)),) * 2,
        ),
        compiler_params=params(12),
        cost_estimate=BRIEF,
    )(place, own, other, out_own, out_other)


class Weight:
    def __init__(self, blocks, first, rows, cut=None):
        self.args, self.specs, self.plan = [], [], []
        self.rows, self.dd = rows, blocks[0].shape[1]

        def view(array, start, size):
            index = start // size
            self.args.append(array)
            self.specs.append(pl.BlockSpec((size, self.dd), lambda i, o, index=index: (index, 0)))

        whole = blocks if cut is None else blocks[:-2]
        for block in whole:
            view(block, first, rows)
            self.plan.append(1)
        if cut is not None:
            pieces = 0
            if first < cut:
                view(blocks[-2], first, min(rows, cut - first))
                pieces += 1
            if first + rows > cut:
                start = max(first, cut)
                view(blocks[-1], start - cut, first + rows - start)
                pieces += 1
            self.plan.append(pieces)

    def read(self, refs):
        at, out = 0, []
        for pieces in self.plan:
            part = [r[...] for r in refs[at : at + pieces]]
            out.append(part[0] if pieces == 1 else jnp.concatenate(part, axis=0))
            at += pieces
        return out


def projected(weight, refs, act, offs):
    total = None
    for b, w in enumerate(weight.read(refs)):
        off = pl.multiple_of(offs[b], weight.dd)
        part = dot(w, act[:, pl.ds(off, weight.dd)], (((1,), (1,))))
        total = part if total is None else total + part
    return total


def projection(body, weight, acts, offs, extra, extra_specs, out_shape, out_specs, mib=40):
    tile, width = acts[0].shape
    tokens = 2 * tile
    n = len(weight.args)

    def kernel(offs, *refs):
        for k in range(2):

            @pl.when(pl.program_id(0) == k)
            def _():
                acc = projected(weight, refs[:n], refs[n + k], offs)
                body(acc, refs[n + 2 : n + 2 + len(extra)], refs[n + 2 + len(extra) :])

    return pl.pallas_call(
        kernel,
        out_shape=out_shape,
        grid_spec=pltpu.PrefetchScalarGridSpec(
            num_scalar_prefetch=1,
            grid=(tokens // tile,),
            in_specs=weight.specs + [pl.BlockSpec((tile, width), lambda i, o: (0, 0))] * 2 + extra_specs,
            out_specs=out_specs,
        ),
        compiler_params=params(mib),
        cost_estimate=LONG,
    )(offs, *weight.args, *acts, *extra)


def x_projection(weight, chans, acts, offs):
    tile = acts[0].shape[0]
    parts = (chans, STATE, weight.rows - chans - STATE)

    def body(acc, extra, outs):
        at = 0
        for out, rows in zip(outs, parts):
            out[...] = acc[at : at + rows]
            at += rows

    return projection(
        body, weight, acts, offs, (), [],
        tuple(jax.ShapeDtypeStruct((rows, 2 * tile), F32) for rows in parts),
        tuple(pl.BlockSpec((rows, tile), lambda i, o: (0, i)) for rows in parts),
    )


def sigmoid(v):
    return 0.5 * jnp.tanh(0.5 * v) + 0.5


def gate_projection(weight, acts, offs, y):
    rows, tokens = y.shape
    tile = tokens // 2

    def body(z, extra, outs):
        outs[0][...] = z
        g = extra[0][...] * (z * sigmoid(z))
        outs[1][...] = jnp.sum(g * g, axis=0, keepdims=True)

    wide = pl.BlockSpec((rows, tile), lambda i, o: (0, i))
    line = pl.BlockSpec((1, tile), lambda i, o: (0, i))
    return projection(
        body, weight, acts, offs, (y,), [wide],
        (jax.ShapeDtypeStruct((rows, tokens), F32), jax.ShapeDtypeStruct((1, tokens), F32)),
        (wide, line), 58,
    )


def back_projection(weight, acts, offs, y, z, gain):
    rows, tokens = y.shape
    tile = tokens // 2

    def body(dyn, extra, outs):
        y, z, gain = extra
        outs[0][...] = dyn
        zv = z[...]
        g = y[...] * (zv * sigmoid(zv))
        outs[1][...] = jnp.sum(dyn * gain[...] * g, axis=0, keepdims=True)

    wide = pl.BlockSpec((rows, tile), lambda i, o: (0, i))
    line = pl.BlockSpec((1, tile), lambda i, o: (0, i))
    return projection(
        body, weight, acts, offs, (y, z, gain),
        [wide, wide, pl.BlockSpec((rows, 1), lambda i, o: (0, 0))],
        (jax.ShapeDtypeStruct((rows, tokens), F32), jax.ShapeDtypeStruct((1, tokens), F32)),
        (wide, line),
    )


def back(groups, offs, width, parts=1, part=0, hiddens=None, states=None, mib=40):
    dd = groups[0][0].dd
    size = groups[0][1].shape[1] // (2 * parts)
    args, specs = [], []
    flops = 0
    for weight, vt in groups:
        args += weight.args + [vt, vt]
        specs += weight.specs
        specs += [pl.BlockSpec((vt.shape[0], size), lambda i, o, p=p: (0, p)) for p in (part, parts + part)]
    if states is not None:
        dbc, w_own, w_other, core = states
        args += [dbc, dbc, w_own, w_other]
        specs += [pl.BlockSpec((dbc.shape[0], size), lambda i, o, p=p: (0, p)) for p in (part, parts + part)]
        specs += [pl.BlockSpec(w_own.shape, lambda i, o: (0, 0))] * 2
        offs = jnp.concatenate([offs, core])
    out_spec = pl.BlockSpec((size, width), lambda i, o: (0, 0))
    shapes = [jax.ShapeDtypeStruct((size, width), BF16)] * 2
    out_specs = [out_spec, out_spec]
    if hiddens is not None:
        args += list(hiddens)
        specs += [pl.BlockSpec((size, width), lambda i, o: (part, 0))] * 2
        shapes.append(jax.ShapeDtypeStruct((1, width), F32))
        out_specs.append(pl.BlockSpec((1, width), lambda i, o: (0, 0)))

    def kernel(offs, *refs):
        outs = refs[len(args) :]
        at, terms = 0, []
        for weight, _ in groups:
            n = len(weight.args)
            v = jnp.concatenate([refs[at + n][...].T, refs[at + n + 1][...].T], axis=0)
            terms.append((v, weight.read(refs[at : at + n])))
            at += n + 2
        if states is not None:
            dbc = jnp.concatenate([refs[at][...], refs[at + 1][...]], axis=1)
            first = offs[offs.shape[0] - 1] == 0
            low, high = dbc[:STATE], dbc[STATE:]
            v_own, v_other = jnp.where(first, low, high).T, jnp.where(first, high, low).T
            w_own, w_other = refs[at + 2], refs[at + 3]
        scales = []
        if hiddens is not None:
            for h in refs[len(args) - 2 : len(args)]:
                v = h[...].astype(F32)
                scales.append(lax.rsqrt(jnp.mean(v * v, axis=1, keepdims=True) + EPS))
        for b in range(len(terms[0][1])):
            off = pl.multiple_of(offs[b], dd)
            along = None
            total = None
            for v, blocks in terms:
                term = dot(v, blocks[b], (((1,), (0,))))
                total = term if total is None else total + term
            if states is not None:
                total = total + dot(v_own, w_own[:, pl.ds(off, dd)], (((1,), (0,))))
                total = total + dot(v_other, w_other[:, pl.ds(off, dd)], (((1,), (0,))))
            for k in range(2):
                here = total[k * size : (k + 1) * size]
                outs[k][:, pl.ds(off, dd)] = here.astype(BF16)
                if hiddens is not None:
                    h = refs[len(args) - 2 + k][:, pl.ds(off, dd)].astype(F32)
                    line = jnp.sum(here * (h * scales[k]), axis=0, keepdims=True)
                    along = line if along is None else along + line
            if hiddens is not None:
                outs[2][:, pl.ds(off, dd)] = along

    return pl.pallas_call(
        kernel,
        out_shape=tuple(shapes),
        grid_spec=pltpu.PrefetchScalarGridSpec(
            num_scalar_prefetch=1, grid=(1,), in_specs=specs, out_specs=tuple(out_specs)
        ),
        compiler_params=params(mib),
        cost_estimate=LONG,
    )(offs, *args)


def whole_rows(weight, offs, width):
    def kernel(offs, *refs):
        for b, w in enumerate(weight.read(refs[:-1])):
            refs[-1][:, pl.ds(pl.multiple_of(offs[b], weight.dd), weight.dd)] = w

    return pl.pallas_call(
        kernel,
        out_shape=jax.ShapeDtypeStruct((weight.rows, width), BF16),
        grid_spec=pltpu.PrefetchScalarGridSpec(
            num_scalar_prefetch=1,
            grid=(1,),
            in_specs=weight.specs,
            out_specs=pl.BlockSpec((weight.rows, width), lambda i, o: (0, 0)),
        ),
        compiler_params=params(20),
        cost_estimate=BRIEF,
    )(offs, *weight.args)


def gathered_sums_kernel(cg_a, cg_b, dgain, hg_a, hg_b, spots, pre_a, pre_b, out):
    wide = out.shape[1]
    padded = hg_a.shape[1]
    out[...] = jnp.zeros_like(out)
    row = lax.broadcasted_iota(jnp.int32, (8, 8), 0)
    lane = lax.broadcasted_iota(jnp.int32, (8, 8), 1)
    cg = dot((row == lane).astype(F32), cg_a[...] + cg_b[...], (((1,), (1,))), HIGH)
    out[0:5, :] = cg[0:5]
    out[5:6, : dgain.shape[1]] = dgain[0:1, :]
    for k in range(3):
        sums = dot(lane_sums(hg_a[k] + hg_b[k]), spots[k * padded : (k + 1) * padded, :], (((1,), (0,))), HIGH)
        out[6:7, k * 128 : (k + 1) * 128] = sums[0:1]
    pre = pre_a[...] + pre_b[...]
    width = pre.shape[1]
    for k in range(-(-width // wide)):
        size = min(wide, width - k * wide)
        out[7 + k : 8 + k, :size] = pre[:, k * wide : k * wide + size]


def gathered_sums(cg_a, cg_b, dgain, hg_a, hg_b, spots, *pre):
    wide = cg_a.shape[0]
    rows = -(-(7 + -(-pre[0].shape[1] // wide)) // 8) * 8
    args = (cg_a, cg_b, dgain, hg_a, hg_b, spots, *pre)
    whole = lambda shape: pl.BlockSpec(shape, lambda i: (0,) * len(shape))
    return pl.pallas_call(
        gathered_sums_kernel,
        out_shape=jax.ShapeDtypeStruct((rows, wide), F32),
        grid=(1,),
        in_specs=[whole(v.shape) for v in args],
        out_specs=whole((rows, wide)),
        compiler_params=params(16),
        cost_estimate=BRIEF,
    )(*args)


def finals_kernel(heads, padded, n_everyone, place, keep_z, other_z, keep_x, other_x, small, own, other, *refs):
    everyone = refs[0][...]
    for r in refs[1:n_everyone]:
        everyone = everyone + r[...]
    if n_everyone > 1:
        everyone = everyone + own[...] + other[...]
    zx, dt, bc, taps, bias, taps_bc, bias_bc, g_dt, g_a, g_d, pre, gate = refs[n_everyone:]
    first = place[0] == 0
    chans = keep_z.shape[0]
    for k, (a, b) in enumerate(((keep_z, other_z), (keep_x, other_x))):
        zx[k, :, :chans] = jnp.where(first, a[...], b[...]).T
        zx[k, :, chans:] = jnp.where(first, b[...], a[...]).T
    rows = bc.shape[1]
    turned = small[...].T
    bc[...] = turned[:, :rows]
    dt[:, :heads] = turned[:, rows : rows + heads]
    dt[:, heads:] = turned[:, rows + padded : rows + padded + heads]
    a, b = own[...], other[...]
    low, high = jnp.where(first, a, b)[:, :chans], jnp.where(first, b, a)[:, :chans]
    for out, at, size in ((taps, 0, 4), (bias, 4, 1), (gate, 5, 1)):
        out[:, :chans] = low[at : at + size]
        out[:, chans:] = high[at : at + size]
    taps_bc[...] = everyone[0:4, chans:]
    bias_bc[...] = everyone[4:5, chans:]
    both = a + b
    for k, out in enumerate((g_dt, g_a, g_d)):
        out[...] = both[6:7, k * 128 : k * 128 + 2 * heads]
    wide = both.shape[1]
    width = pre.shape[1]
    for k in range(-(-width // wide)):
        size = min(wide, width - k * wide)
        pre[:, k * wide : k * wide + size] = everyone[7 + k : 8 + k, :size]


def finals(place, keep_z, other_z, keep_x, other_x, small, own, other, everyone, heads, padded, width):
    chans, dd = keep_z.shape
    bc_rows = small.shape[0] - 2 * padded
    args = (keep_z, other_z, keep_x, other_x, small, own, other, *everyone)
    shapes = (
        (2, dd, 2 * chans), (dd, 2 * heads), (dd, bc_rows), (4, 2 * chans), (1, 2 * chans), (4, 2 * STATE),
        (1, 2 * STATE), (1, 2 * heads), (1, 2 * heads), (1, 2 * heads), (1, width), (1, 2 * chans),
    )
    whole = lambda shape: pl.BlockSpec(shape, lambda i, p: (0,) * len(shape))
    return pl.pallas_call(
        functools.partial(finals_kernel, heads, padded, len(everyone)),
        out_shape=tuple(jax.ShapeDtypeStruct(shape, F32) for shape in shapes),
        grid_spec=pltpu.PrefetchScalarGridSpec(
            num_scalar_prefetch=1,
            grid=(1,),
            in_specs=[
                pl.BlockSpec((chans, dd), lambda i, p: (1, 0)) if k == 1 else whole(v.shape)
                for k, v in enumerate(args)
            ],
            out_specs=tuple(whole(shape) for shape in shapes),
        ),
        compiler_params=params(24),
        cost_estimate=BRIEF,
    )(place, *args)


def reversed_bits(index, bits):
    return sum(((index >> k) & 1) << (bits - 1 - k) for k in range(bits))


def small_terms_kernel(shards, core_place, states, steps, own, other, keep, give):
    first = core_place[0] == 0
    both = both_parts(steps, own, other)
    total = jnp.concatenate(
        [dot(states[...], own[...], (((1,), (0,)))), jnp.where(first, both, 0.0), jnp.where(first, 0.0, both)]
    )
    chips = shards // 2
    lanes = own.shape[1] // shards
    bits = chips.bit_length() - 1
    for chip in range(chips):
        at = reversed_bits(chip, bits) * lanes
        low = total[:, 2 * chip * lanes : (2 * chip + 1) * lanes]
        high = total[:, (2 * chip + 1) * lanes : (2 * chip + 2) * lanes]
        keep[:, at : at + lanes] = jnp.where(first, low, high)
        give[:, at : at + lanes] = jnp.where(first, high, low).astype(BF16)


def small_terms(place, states, steps, acts, shards):
    m, k = states.shape[0], steps.shape[0]
    width = acts[0].shape[1]
    whole = lambda i, p: (0, 0)
    shape = (m + 2 * k, width // 2)
    return pl.pallas_call(
        functools.partial(small_terms_kernel, shards),
        out_shape=(jax.ShapeDtypeStruct(shape, F32), jax.ShapeDtypeStruct(shape, BF16)),
        grid_spec=pltpu.PrefetchScalarGridSpec(
            num_scalar_prefetch=1,
            grid=(1,),
            in_specs=[pl.BlockSpec(v.shape, whole) for v in (states, steps, *acts)],
            out_specs=(pl.BlockSpec(shape, whole),) * 2,
        ),
        compiler_params=params(20),
        cost_estimate=BRIEF,
    )(place, states, steps, *acts)


def output_kernel(late_own, late_came, own, came, hidden, out):
    late = pl.program_id(0) >= pl.num_programs(0) // 2
    rest = jnp.where(late, late_own[...].astype(F32), own[...].astype(F32))
    rest = rest + jnp.where(late, late_came[...].astype(F32), came[...].astype(F32))
    out[...] = (hidden[...].astype(F32) + rest).astype(BF16)


def residual(late, early, hidden):
    rows, width = hidden.shape
    tile = 128
    half = rows // tile // 2
    block = pl.BlockSpec((tile, width), lambda i: (i, 0))
    first = pl.BlockSpec((tile, width), lambda i: (jnp.minimum(i, half - 1), 0))
    second = pl.BlockSpec((tile, width), lambda i: (jnp.maximum(i - half, 0), 0))
    return pl.pallas_call(
        output_kernel,
        out_shape=jax.ShapeDtypeStruct(hidden.shape, BF16),
        grid=(rows // tile,),
        in_specs=[second, second, first, first, block],
        out_specs=block,
        compiler_params=params(20),
        cost_estimate=LONG,
    )(*late, *early, hidden)


def norm_back_kernel(late_own, late_came, own, came, hidden, cot, gain, out):
    h = hidden[...].astype(F32)
    width = h.shape[1]
    r = lax.rsqrt(jnp.mean(h * h, axis=1, keepdims=True) + EPS)
    late = pl.program_id(0) >= pl.num_programs(0) // 2
    dn = jnp.where(late, late_own[...].astype(F32), own[...].astype(F32))
    dn = dn + jnp.where(late, late_came[...].astype(F32), came[...].astype(F32))
    weighted = dn * gain[...]
    along = jnp.sum(weighted * h, axis=1, keepdims=True) * (1.0 / width)
    out[...] = (weighted * r - h * (r * r * r * along) + cot[...].astype(F32)).astype(BF16)


def norm_back(late, early, hidden, cot, gain):
    rows, width = hidden.shape
    tile = 128
    half = rows // tile // 2
    block = pl.BlockSpec((tile, width), lambda i: (i, 0))
    first = pl.BlockSpec((tile, width), lambda i: (jnp.minimum(i, half - 1), 0))
    second = pl.BlockSpec((tile, width), lambda i: (jnp.maximum(i - half, 0), 0))
    return pl.pallas_call(
        norm_back_kernel,
        out_shape=jax.ShapeDtypeStruct(hidden.shape, BF16),
        grid=(rows // tile,),
        in_specs=[second, second, first, first, block, block, pl.BlockSpec((1, width), lambda i: (0, 0))],
        out_specs=block,
        compiler_params=params(30),
        cost_estimate=LONG,
    )(*late, *early, hidden, cot, gain)


def gate_back_kernel(total, dyn, y, z, s, q, gain, dz, dy, dgain):
    zv, yv, sv = z[...], y[...], s[...]
    sig = sigmoid(zv)
    silu = zv * sig
    g = yv * silu
    scaled = dyn[...] * sv
    t = scaled * g
    lanes = t[:, :128]
    for k in range(128, t.shape[1], 128):
        lanes = lanes + t[:, k : k + 128]
    dgain[...] = lane_sums(lanes)
    dg = scaled * gain[...] - g * (sv * sv * sv * q[...] * (1.0 / total))
    dz[...] = (dg * yv * (sig * (1.0 + zv * (1.0 - sig)))).astype(BF16)
    dy[...] = (dg * silu).astype(BF16)


def gate_back(total, dyn, y, z, s, q, gain):
    rows, tokens = dyn.shape
    tile = max(rows // 4, 128)
    wide = pl.BlockSpec((tile, tokens), lambda i: (i, 0))
    line = pl.BlockSpec((1, tokens), lambda i: (0, 0))
    return pl.pallas_call(
        functools.partial(gate_back_kernel, float(total)),
        grid=(rows // tile,),
        out_shape=(jax.ShapeDtypeStruct((rows, tokens), BF16),) * 2
        + (jax.ShapeDtypeStruct((8, rows), F32),),
        in_specs=[wide, wide, wide, line, line, pl.BlockSpec((tile, 1), lambda i: (i, 0))],
        out_specs=(wide, wide, pl.BlockSpec((8, tile), lambda i: (0, i))),
        compiler_params=params(40),
        cost_estimate=BRIEF,
    )(dyn, y, z, s, q, gain)


def head_terms(raw, hp_ref):
    pre = raw + hp_ref[:, 0:1]
    small = jnp.exp(-jnp.abs(pre))
    one = 1.0 + small
    away = one - 1.0
    log1p = jnp.where(away == 0.0, small, jnp.log(one) * (small / jnp.where(away == 0.0, 1.0, away)))
    dt = jnp.maximum(pre, 0.0) + log1p
    logistic = jnp.where(pre >= 0.0, 1.0, small) / one
    rows = lax.broadcasted_iota(jnp.int32, (Q, Q), 0)
    lanes = lax.broadcasted_iota(jnp.int32, (Q, Q), 1)
    upto = (rows <= lanes).astype(F32)
    logs = dt * hp_ref[:, 1:2]
    cums = dot(logs, upto, (((1,), (0,))), HIGH)
    return dt, logistic, cums


def to_columns(cums):
    n = cums.shape[0]
    square = jnp.concatenate([cums, jnp.zeros((Q - n, Q), F32)], axis=0)
    return square.T


def pair_bias(segr_ref, segc_ref):
    rows = lax.broadcasted_iota(jnp.int32, (Q, Q), 0)
    lanes = lax.broadcasted_iota(jnp.int32, (Q, Q), 1)
    keep = (segc_ref[...] == segr_ref[...]) & (rows <= lanes)
    return jnp.where(keep, 0.0, NEG)


def state_rows(place, own, other, r0):
    at = r0 % STATE
    rows = slice(at, at + HEAD)
    return jnp.where(place[0] == r0 // STATE, own[rows, :], other[rows, :])


def fwd_kernel(
    heads, given, place, xr_ref, bco_ref, bcs_ref, dt_ref, mask_ref, segr_ref, segc_ref, par_ref, hp_ref, *rest
):
    y_ref, xa_ref, u_ref, s_ref, prev, state, parb, xt = rest[given:]
    chans = heads * HEAD
    wide = chans + 2 * STATE

    @pl.when(pl.program_id(0) == 0)
    def _():
        for k in range(6):
            parb[k] = jnp.broadcast_to(par_ref[:, k : k + 1], (wide, Q))
        prev[...] = jnp.zeros_like(prev)
        state[...] = jnp.zeros_like(state)

    lane = lax.broadcasted_iota(jnp.int32, (HEAD, Q), 1)
    m1, m2, m3 = mask_ref[0:1, :], mask_ref[1:2, :], mask_ref[2:3, :]

    def conv(r0):
        rows = slice(r0, r0 + HEAD)
        cur = xr_ref[rows, :] if r0 < chans else state_rows(place, bco_ref, bcs_ref, r0 - chans)
        old = prev[rows, :]
        u = parb[4, rows, :] + parb[3, rows, :] * cur
        u = u + parb[2, rows, :] * (m1 * pltpu.roll(jnp.where(lane >= Q - 1, old, cur), 1, 1))
        u = u + parb[1, rows, :] * (m2 * pltpu.roll(jnp.where(lane >= Q - 2, old, cur), 2, 1))
        u = u + parb[0, rows, :] * (m3 * pltpu.roll(jnp.where(lane >= Q - 3, old, cur), 3, 1))
        prev[rows, :] = cur
        u_ref[rows, :] = u
        xa = (u * (0.5 * jnp.tanh(0.5 * u) + 0.5)).astype(BF16)
        xa_ref[rows, :] = xa
        return xa

    for r0 in range(chans, wide, HEAD):
        conv(r0)
    bt = xa_ref[chans : chans + STATE, :]
    ct = xa_ref[chans + STATE : wide, :]
    mix = dot(bt.T, ct, (((1,), (0,))))
    dt, _, cums = head_terms(dt_ref[...], hp_ref)
    cols = to_columns(cums)
    bias = pair_bias(segr_ref, segc_ref)
    enter = jnp.exp(cums) * mask_ref[3:4, :]
    last = jnp.broadcast_to(cums[:, Q - 1 : Q], cums.shape)
    tail = jnp.exp(last - cums) * mask_ref[4:5, :]
    passing = jnp.exp(last) * mask_ref[5:6, :]
    s_in = state[...].astype(BF16)
    s_ref[...] = s_in
    carried = dot(s_in, ct, (((1,), (0,))))
    for h in range(heads):
        rows = slice(h * HEAD, (h + 1) * HEAD)
        xa = conv(h * HEAD).astype(F32)
        decay = jnp.exp(cums[h : h + 1, :] - cols[:, h : h + 1] + bias)
        mixing = (mix * decay).astype(BF16)
        xd = xa * dt[h : h + 1, :]
        xt[rows, :] = (xd * tail[h : h + 1, :]).astype(BF16)
        y = dot(xd.astype(BF16), mixing, (((1,), (0,))))
        y = y + enter[h : h + 1, :] * carried[rows, :] + parb[5, rows, :] * xa
        y_ref[rows, :] = y
    fresh = dot(xt[...], bt, (((1,), (1,))))
    for h in range(heads):
        rows = slice(h * HEAD, (h + 1) * HEAD)
        state[rows, :] = state[rows, :] * passing[h : h + 1, :] + fresh[rows, :]


def scan_forward(place, xr, bco, bcs, dtr, masks, segr, segc, par, hp, heads, seqs, seq, given=()):
    chans, tokens = xr.shape
    padded = dtr.shape[0]
    wide = chans + 2 * STATE
    count = tokens // seqs // Q
    at = lambda k, p: (0, seq * count + k)
    swapped = lambda k, p: (0, (seqs - 1 - seq) * count + k)
    whole = lambda k, p: (0, 0)
    args = (xr, bco, bcs, dtr, masks, segr, segc, par, hp)
    return pl.pallas_call(
        functools.partial(fwd_kernel, heads, len(given)),
        out_shape=(
            jax.ShapeDtypeStruct((chans, tokens), F32),
            jax.ShapeDtypeStruct((wide, tokens), BF16),
            jax.ShapeDtypeStruct((wide, tokens), F32),
            jax.ShapeDtypeStruct((chans, tokens), BF16),
        ),
        grid_spec=pltpu.PrefetchScalarGridSpec(
            num_scalar_prefetch=1,
            grid=(count,),
            in_specs=[
                pl.BlockSpec((chans, Q), at),
                pl.BlockSpec((STATE, Q), at),
                pl.BlockSpec((STATE, Q), swapped),
                pl.BlockSpec((padded, Q), at),
                pl.BlockSpec((8, Q), at),
                pl.BlockSpec((1, Q), at),
                pl.BlockSpec((Q, 1), lambda k, p: (seq * count + k, 0)),
                pl.BlockSpec(par.shape, whole),
                pl.BlockSpec(hp.shape, whole),
            ]
            + [pl.BlockSpec(memory_space=pl.ANY)] * len(given),
            out_specs=(
                pl.BlockSpec((chans, Q), at),
                pl.BlockSpec((wide, Q), at),
                pl.BlockSpec((wide, Q), at),
                pl.BlockSpec((chans, STATE), at),
            ),
            scratch_shapes=[
                pltpu.VMEM((wide, Q), F32),
                pltpu.VMEM((chans, STATE), F32),
                pltpu.VMEM((6, wide, Q), F32),
                pltpu.VMEM((chans, Q), BF16),
            ],
        ),
        input_output_aliases={1 + len(args) + k: k for k in range(len(given))},
        compiler_params=params(54),
        cost_estimate=LONG,
    )(place, *args, *given)


def bwd_kernel(
    heads, late, place, xr_ref, bco_ref, bcs_ref, dt_ref, mask_ref, segr_ref, segc_ref, par_ref, hp_ref, xa_ref,
    u_ref, s_ref, dy_ref, y_ref, *rest,
):
    if late:
        dx_ref, dbc_ref, ddt_ref, cgo_ref, hg_ref, dstate_out, after_out = rest[:7]
    else:
        dstate_in, after_in, next_ref = rest[:3]
        dx_ref, dbc_ref, ddt_ref, cgo_ref, hg_ref = rest[6:11]
    dstate, parb, after, nmask, xt, dye, cg_ref = rest[-7:]
    chans = heads * HEAD
    wide = chans + 2 * STATE
    seq, block = pl.program_id(0), pl.program_id(1)
    final = block == pl.num_programs(1) - 1

    @pl.when((seq == 0) & (block == 0))
    def _():
        for k in range(6):
            parb[k] = jnp.broadcast_to(par_ref[:, k : k + 1], (wide, Q))
        cg_ref[...] = jnp.zeros_like(cg_ref)
        hg_ref[...] = jnp.zeros_like(hg_ref)

    @pl.when(block == 0)
    def _():
        if late:
            dstate[...] = jnp.zeros_like(dstate)
            after[...] = jnp.zeros_like(after)
            nmask[...] = jnp.zeros_like(nmask)
        else:
            dstate[...] = dstate_in[...]
            after[...] = after_in[...]
            nmask[...] = next_ref[...]

    lane = lax.broadcasted_iota(jnp.int32, (HEAD, Q), 1)
    lane8 = lax.broadcasted_iota(jnp.int32, (8, Q), 1)
    sub8 = lax.broadcasted_iota(jnp.int32, (8, Q), 0)
    masks = mask_ref[...]
    shifted_masks = jnp.where(lane8 <= sub8, nmask[...], masks)
    nmask[...] = masks

    def conv_back(r0, dxa, out, out0):
        rows = slice(r0, r0 + HEAD)
        u = u_ref[rows, :]
        sig = 0.5 * jnp.tanh(0.5 * u) + 0.5
        dc = dxa * (sig * (1.0 + u * (1.0 - sig)))
        xr = xr_ref[rows, :] if r0 < chans else state_rows(place, bco_ref, bcs_ref, r0 - chans)
        old = after[rows, :]
        after[rows, :] = dc
        dx = parb[3, rows, :] * dc
        cg_ref[4, rows, :] += dc
        cg_ref[3, rows, :] += xr * dc
        for k in (1, 2, 3):
            e = jnp.where(lane < k, old, dc) * shifted_masks[k - 1 : k, :]
            e = pltpu.roll(e, Q - k, 1)
            dx = dx + parb[3 - k, rows, :] * e
            cg_ref[3 - k, rows, :] += xr * e
        out[out0 : out0 + HEAD, :] = dx.astype(out.dtype)

    bt = xa_ref[chans : chans + STATE, :]
    ct = xa_ref[chans + STATE : wide, :]
    mix = dot(bt.T, ct, (((1,), (0,))))
    dt, logistic, cums = head_terms(dt_ref[...], hp_ref)
    cols = to_columns(cums)
    bias = pair_bias(segr_ref, segc_ref)
    enter = jnp.exp(cums) * masks[3:4, :]
    last = jnp.broadcast_to(cums[:, Q - 1 : Q], cums.shape)
    tail = jnp.exp(last - cums) * masks[4:5, :]
    passing = jnp.exp(last) * masks[5:6, :]
    ds = dstate[...].astype(BF16)
    spread = dot(ds, bt, (((1,), (0,))))
    dmix = jnp.zeros((Q, Q), F32)
    s_in = s_ref[...]
    direct, cross, skip, outward, through, inward = [], [], [], [], [], []
    for h in range(heads):
        rows = slice(h * HEAD, (h + 1) * HEAD)
        xa = xa_ref[rows, :].astype(F32)
        dyb = dy_ref[rows, :]
        dy = dyb.astype(F32)
        decay = jnp.exp(cums[h : h + 1, :] - cols[:, h : h + 1] + bias)
        mixing = (mix * decay).astype(BF16)
        xd = xa * dt[h : h + 1, :]
        xdb = xd.astype(BF16)
        xt[rows, :] = (xd * tail[h : h + 1, :]).astype(BF16)
        dye[rows, :] = (dy * enter[h : h + 1, :]).astype(BF16)
        dmix = dmix + dot(xdb, dyb, (((0,), (0,)))) * decay
        near = dot(dyb, mixing, (((1,), (1,))))
        far = tail[h : h + 1, :] * spread[rows, :]
        pull = near + far
        direct.append(jnp.sum(xa * pull, axis=0, keepdims=True))
        cross.append(jnp.sum(xdb.astype(F32) * near, axis=0, keepdims=True))
        outward.append(jnp.sum(xd * far, axis=0, keepdims=True))
        through.append(jnp.sum(dstate[rows, :] * s_in[rows, :].astype(F32), axis=0, keepdims=True))
        skip.append(jnp.sum(xa * dy, axis=0, keepdims=True))
        inward.append(jnp.sum(y_ref[rows, :] * dy, axis=0, keepdims=True))
        dxa = dt[h : h + 1, :] * pull + parb[5, rows, :] * dy
        conv_back(h * HEAD, dxa, dx_ref, h * HEAD)
    pad = ddt_ref.shape[0] - heads
    if pad:
        zero = [jnp.zeros((pad, Q), F32)]
        direct, cross, skip = direct + zero, cross + zero, skip + zero
        outward, through, inward = outward + zero, through + zero, inward + zero
    direct, cross, skip, outward, through, inward = (
        jnp.concatenate(v, axis=0) for v in (direct, cross, skip, outward, through, inward)
    )
    dlog = inward - hp_ref[:, 2:3] * skip - cross
    rows = lax.broadcasted_iota(jnp.int32, (Q, Q), 0)
    lanes = lax.broadcasted_iota(jnp.int32, (Q, Q), 1)
    dl = dot(dlog, (rows >= lanes).astype(F32), (((1,), (0,))), HIGH)
    dl = dl + dot(outward, (rows < lanes).astype(F32), (((1,), (0,))), HIGH)
    dl = dl + passing * jnp.sum(through, axis=1, keepdims=True)
    ddt = (direct + hp_ref[:, 1:2] * dl) * logistic
    ddt_ref[...] = ddt.astype(BF16)
    hg_ref[0] += ddt
    hg_ref[1] += dt * dl
    hg_ref[2] += skip
    dmixb = dmix.astype(BF16)
    xtv, dyev = xt[...], dye[...]
    dbt = dot(ct, dmixb, (((1,), (1,)))) + dot(ds, xtv, (((0,), (0,))))
    dct = dot(bt, dmixb, (((1,), (0,)))) + dot(s_ref[...], dyev, (((0,), (0,))))
    dbca = jnp.concatenate([dbt, dct], axis=0)
    for r0 in range(0, 2 * STATE, HEAD):
        conv_back(chans + r0, dbca[r0 : r0 + HEAD, :], dbc_ref, r0)
    fresh = dot(dyev, ct, (((1,), (1,))))
    for h in range(heads):
        rows = slice(h * HEAD, (h + 1) * HEAD)
        dstate[rows, :] = dstate[rows, :] * passing[h : h + 1, :] + fresh[rows, :]

    if late:

        @pl.when(final)
        def _():
            dstate_out[...] = dstate[...]
            after_out[...] = after[...]

    @pl.when((seq == pl.num_programs(0) - 1) & final)
    def _():
        for r0 in range(0, wide, HEAD):
            rows = slice(r0, r0 + HEAD)
            for k in range(5):
                cgo_ref[rows, k : k + 1] = jnp.sum(cg_ref[k, rows, :], axis=1, keepdims=True)


def scan_backward(
    place, xr, bco, bcs, dtr, masks, segr, segc, par, hp, xa, u, s_in, dy, y, heads, seqs, carry=(), given=()
):
    chans, tokens = xr.shape
    padded = dtr.shape[0]
    wide = chans + 2 * STATE
    count = tokens // seqs // Q
    late = not carry
    last = count - 1 if late else count // 2 - 1
    at = lambda s, k, p: (0, s * count + last - k)
    swapped = lambda s, k, p: (0, (seqs - 1 - s) * count + last - k)
    whole = lambda s, k, p: (0, 0)
    by_seq = lambda s, k, p: (s, 0)
    args = (xr, bco, bcs, dtr, masks, segr, segc, par, hp, xa, u, s_in, dy, y)
    if not late:
        args = (*args, *carry, masks)
    carried = [pl.BlockSpec((chans, STATE), by_seq), pl.BlockSpec((wide, Q), by_seq)]
    extra = [] if late else carried + [pl.BlockSpec((8, Q), lambda s, k, p: (0, s * count + count // 2))]
    shapes = (
        jax.ShapeDtypeStruct((chans, tokens), BF16),
        jax.ShapeDtypeStruct((2 * STATE, tokens), BF16),
        jax.ShapeDtypeStruct((padded, tokens), BF16),
        jax.ShapeDtypeStruct((wide, 8), F32),
        jax.ShapeDtypeStruct((3, padded, Q), F32),
    )
    if late:
        shapes += (
            jax.ShapeDtypeStruct((seqs * chans, STATE), F32),
            jax.ShapeDtypeStruct((seqs * wide, Q), F32),
        )
    return pl.pallas_call(
        functools.partial(bwd_kernel, heads, late),
        out_shape=shapes,
        grid_spec=pltpu.PrefetchScalarGridSpec(
            num_scalar_prefetch=1,
            grid=(seqs, count // 2),
            in_specs=[
                pl.BlockSpec((chans, Q), at),
                pl.BlockSpec((STATE, Q), at),
                pl.BlockSpec((STATE, Q), swapped),
                pl.BlockSpec((padded, Q), at),
                pl.BlockSpec((8, Q), at),
                pl.BlockSpec((1, Q), at),
                pl.BlockSpec((Q, 1), lambda s, k, p: (s * count + last - k, 0)),
                pl.BlockSpec(par.shape, whole),
                pl.BlockSpec(hp.shape, whole),
                pl.BlockSpec((wide, Q), at),
                pl.BlockSpec((wide, Q), at),
                pl.BlockSpec((chans, STATE), at),
                pl.BlockSpec((chans, Q), at),
                pl.BlockSpec((chans, Q), at),
            ]
            + extra
            + [pl.BlockSpec(memory_space=pl.ANY)] * len(given),
            out_specs=[
                pl.BlockSpec((chans, Q), at),
                pl.BlockSpec((2 * STATE, Q), at),
                pl.BlockSpec((padded, Q), at),
                pl.BlockSpec((wide, 8), whole),
                pl.BlockSpec((3, padded, Q), lambda s, k, p: (0, 0, 0)),
            ]
            + (carried if late else []),
            scratch_shapes=[
                pltpu.VMEM((chans, STATE), F32),
                pltpu.VMEM((6, wide, Q), F32),
                pltpu.VMEM((wide, Q), F32),
                pltpu.VMEM((8, Q), F32),
                pltpu.VMEM((chans, Q), BF16),
                pltpu.VMEM((chans, Q), BF16),
                pltpu.VMEM((5, wide, Q), F32),
            ],
        ),
        input_output_aliases={1 + len(args) + k: k for k in range(len(given))},
        compiler_params=params(54),
        cost_estimate=LONG,
    )(place, *args, *given)


def block_masks(segs, seqs):
    s = segs.reshape(seqs, -1)
    length = s.shape[1]
    rows = []
    for k in (1, 2, 3):
        old = jnp.pad(s, ((0, 0), (k, 0)), constant_values=-1)[:, :length]
        rows.append(old == s)
    b = s.reshape(seqs, length // Q, Q)
    ends = b[:, :, -1:]
    before = jnp.concatenate([jnp.full((seqs, 1, 1), -1, s.dtype), ends[:, :-1]], axis=1)
    rows += [b == before, b == ends, jnp.broadcast_to(ends == before, b.shape)]
    rows = [r.reshape(1, -1).astype(F32) for r in rows]
    return jnp.concatenate(rows + [jnp.zeros((2, segs.shape[0]), F32)], axis=0)


def local(
    hidden, segment_ids, cotangent, w_zx, w_dt, w_bc, w_out, conv_x, conv_bias_x, conv_bc, conv_bias_bc,
    dt_bias, a_log, d_skip, pre_gain, gate_gain,
):
    n_dp, n_t = lax.axis_size("dp"), lax.axis_size("tensor")
    t_index = lax.axis_index("tensor")
    ring = Ring(n_dp)
    core = ring.core
    mine, width = hidden.shape
    inner_here = w_zx.shape[2]
    chans = inner_here // 2
    heads = w_dt.shape[1] // 2
    padded = max(16, heads)
    wide = chans + 2 * STATE
    inner_all = inner_here * n_t
    dd = 2 * w_zx.shape[1]

    def tensor_sum(v):
        if n_t == 2:
            return v + lax.ppermute(v, "tensor", [(0, 1), (1, 0)])
        return lax.psum(v, "tensor")

    def over_tensor(v):
        if n_t == 2:
            return v.astype(F32) + lax.ppermute(v, "tensor", [(0, 1), (1, 0)]).astype(F32)
        return lax.psum(v.astype(F32), "tensor")

    def pick(v, which, axis=0):
        size = v.shape[axis] // 2
        return lax.dynamic_slice_in_dim(v, which * size, size, axis)

    def in_order(own, other, axis):
        return jnp.where(
            core == 0, jnp.concatenate([own, other], axis), jnp.concatenate([other, own], axis)
        )

    pad_dt = lambda v: jnp.pad(v, ((0, 0), (0, STATE - heads)))
    small = jnp.concatenate([w_bc, pad_dt(w_dt[:, :heads]), pad_dt(w_dt[:, heads:])], axis=1)
    zx_other = ring.swap(w_zx)
    small_other = ring.swap(small)
    place = core.reshape(1).astype(jnp.int32)
    ux = prep_x(place, w_zx, zx_other, small, small_other, padded)
    cut = chans // 2
    gx = Gather(ring, ux, "both", cut)
    gx.step()

    hiddens = [hidden, ring.swap(after(hidden, ux))]

    def norm(h):
        h = h.astype(F32)
        return (h * lax.rsqrt(jnp.mean(h * h, -1, keepdims=True) + EPS) * pre_gain).astype(BF16)

    normed = [norm(h) for h in hiddens]
    segs = jnp.concatenate([segment_ids, ring.swap(after(segment_ids, ux))])
    masks = block_masks(segs, 2)
    segr, segc = segs[None, :], segs[:, None]
    offs = ring.offsets(dd)
    table = ring.table()

    def own_chans(v):
        return pick(v, core, v.ndim - 1)

    taps = jnp.concatenate([own_chans(conv_x), conv_bc], axis=1)
    biases = jnp.concatenate([own_chans(conv_bias_x), conv_bias_bc])
    skips = jnp.repeat(own_chans(d_skip), HEAD)
    par = jnp.concatenate(
        [taps, biases[None], jnp.pad(skips, (0, 2 * STATE))[None], jnp.zeros((2, wide), F32)], axis=0
    ).T
    a_own = -jnp.exp(own_chans(a_log))
    spot = lax.broadcasted_iota(jnp.int32, (padded, 128), 1) - core * heads
    spot = (spot == lax.broadcasted_iota(jnp.int32, (padded, 128), 0)).astype(F32)
    spots = jnp.concatenate([spot, spot * jnp.pad(a_own, (0, padded - heads))[:, None], spot])
    hp = jnp.stack([own_chans(dt_bias), a_own, own_chans(d_skip)], axis=1)
    hp = jnp.pad(hp, ((0, padded - heads), (0, 5)))
    gain = own_chans(gate_gain)[:, None]

    out_other = ring.swap(after(w_out, ux))
    uz, uo = prep_zo(place, w_zx, zx_other, w_out, out_other)
    cots = [cotangent, ring.swap(after(cotangent, uz))]

    gx.step()
    gx.step()
    third = gx.newest()
    gx.finish()
    gz = Gather(ring, after(uz, *third), "right")
    came = gz.step()

    across = [(2 * i + t, 2 * (i ^ 1) + 1 - t) for i in range(n_dp) for t in range(2)]

    def wave(v):
        turned = jnp.concatenate([v[:, mine:], v[:, :mine]], axis=1)
        if n_t != 2:
            return tensor_sum(v + ring.swap(turned))
        return (
            v
            + ring.swap(turned)
            + lax.ppermute(v, "tensor", [(0, 1), (1, 0)])
            + lax.ppermute(turned, ("dp", "tensor"), across)
        )

    def tensor_other(v):
        if n_t == 2:
            return lax.ppermute(v, "tensor", [(0, 1), (1, 0)])
        return (lax.psum(v.astype(F32), "tensor") - v.astype(F32)).astype(BF16)

    def joined(own, came):
        return (own.astype(F32) + came.astype(F32)).astype(BF16)

    blocks = gx.blocks()
    gz.step(*gx.last)
    w_states = Weight(blocks, chans, STATE, cut)
    xr, bc_own, dtr = after(
        x_projection(
            Weight(blocks, 0, chans + STATE + padded, cut), chans, normed, after(offs, *came, *gx.last)
        ),
        *gz.newest(),
    )
    bc_other = ring.swap(bc_own)
    gz.step()
    scan_args = (bc_own, bc_other, dtr, masks, segr, segc, par, hp)
    half = after(scan_forward(place, xr, *scan_args, heads, 2, 0), *gz.newest())
    gz.finish(half[0])
    wb_own = whole_rows(w_states, after(offs, half[0]), width)
    wb_other = ring.swap(wb_own)
    go = Gather(ring, after(uo, half[0]), "left")
    go.left()
    y, xa, u, s_in = after(
        scan_forward(place, after(xr, wb_own), *scan_args, heads, 2, 1, half), *gz.last, go.l[-1], wb_other
    )
    go.step(y)
    z, squares = after(
        gate_projection(Weight(gz.blocks(), 0, chans), normed, after(offs, y), y), *go.newest()
    )
    go.step(squares)
    total_sq = wave(squares)
    s = lax.rsqrt(total_sq / inner_all + EPS)
    ynt = (y * (z * sigmoid(z)) * s * gain).astype(BF16)
    ynt = after(ynt, *go.newest())
    go.right()
    go.finish()
    ro = Scatter(ring, terms(ring, table, ynt, cots, dd))

    weight_o = Weight(go.blocks(), 0, chans)
    dyn, q = after(
        back_projection(weight_o, cots, after(offs, *ro.out), y, z, gain), *ro.got
    )
    sent_o = ro.step(q)
    q_total = wave(after(q, *sent_o))
    out_own, out_rest = after(back([(weight_o, ynt)], after(offs, *sent_o), width), *ro.got, q_total)
    sent_o = ro.step(out_own)
    out_came = ring.swap(out_rest)
    dzt, dyt, dgain = gate_back(inner_all, after(dyn, *sent_o), y, z, s, q_total, gain)
    parts_z = after(terms(ring, table, dzt, normed, dd), *ro.got, out_came)
    half = mine // 2
    sent_o = ro.step(parts_z[1])
    rz = Scatter(ring, after(parts_z, *sent_o))
    out_own, out_came = after((out_own, out_came), *sent_o)
    out_late = joined(out_own[half:], out_came[half:])
    out_early = joined(out_own[:half], out_came[:half])

    def dn_part(part, *others):
        return back(
            [
                (Weight(gz.blocks(), 0, chans), dzt),
                (Weight(blocks, 0, chans, cut), dxt),
                (Weight(blocks, chans + STATE, padded, cut), ddt_low),
            ],
            after(offs, *others), width, 2, part, hiddens,
            (dbc_low, wb_own, wb_other, place), 58,
        )

    scan_args = (*scan_args, xa, u, s_in)
    out_late_other = tensor_other(out_late)
    first = after(
        scan_backward(place, xr, *scan_args, after(dyt, *rz.out, out_late, out_early), y, heads, 2),
        *ro.got, *rz.got,
    )
    sent_z = rz.step(first[3])
    dxt, dbc_low, ddt_low = first[:3]
    out_early_other = tensor_other(after(out_early, *sent_z))
    late_own, late_rest, late_pre = after(dn_part(1, *sent_z), *rz.got, out_late_other)
    sent_z = rz.step(late_own)
    late_came = ring.swap(late_rest)
    second = after(
        scan_backward(place, xr, *scan_args, after(dyt, *sent_z), y, heads, 2, first[5:], first[:3]),
        *rz.got, out_early_other, late_came,
    )
    dxt, dbc_low, ddt_low = second[:3]
    sent_z = rz.step(ddt_low)
    dbc_came = ring.swap(after(dbc_low, *sent_z)[:, mine:])
    late_own = joined(late_own, after(late_came, *sent_z))
    late_other = tensor_other(late_own)
    parts_x = after(terms(ring, table, after(dxt, *sent_z, late_own), normed, dd), *rz.got, dbc_came)
    rx = Scatter(ring, parts_x)
    dbc_own = joined(dbc_low[:, :mine], after(dbc_came, *parts_x))
    dbc_other = tensor_other(dbc_own)
    early_own, early_rest, early_pre = after(
        dn_part(0, *rx.out, dbc_own), *rx.got, late_other, dbc_other
    )

    sent_x = rx.step(early_own)
    early_came = ring.swap(early_rest)
    early_own = joined(after(early_own, *sent_x), early_came)
    early_other = tensor_other(early_own)
    dbc_own = joined(dbc_own, after(dbc_other, early_own))
    bc_cols = 2 * STATE // n_t
    states = lax.dynamic_slice_in_dim(dbc_own, t_index * bc_cols, bc_cols, 0)
    products, give = small_terms(place, states, ddt_low, normed, n_dp)
    products_came = ring.swap(give)
    common = gathered_sums(
        first[3], second[3], dgain, first[4], after(second[4], products), spots, early_pre, late_pre
    )
    common_came = ring.doubling(common, 1)
    keep_o, give_o = ro.finish(place, common)
    keep_z, give_z = rz.finish(place, keep_o)
    give_both = jnp.concatenate([give_o, give_z])
    products, give_both = after((products, give_both), *rx.got, products_came, common_came)
    common, products = common + common_came, products + products_came.astype(F32)

    sent_x = rx.step(give_both)
    common_came = ring.doubling(after(common, *sent_x), 2)
    products, products_came = ring.halving(after(products, *sent_x), 1)
    output = residual(
        (out_late, out_late_other), (out_early, out_early_other), after(hidden, *sent_x)
    )
    output, common, products = after(
        (output, common, products), *rx.got, common_came, products_came, early_other
    )
    common, products = common + common_came, products + products_came.astype(F32)

    sent_x = rx.step(output)
    common_came = ring.doubling(after(common, *sent_x), 4)
    products, products_came = ring.halving(after(products, *sent_x), 2)
    other_both = ring.swap(after(give_both, *sent_x))
    grad_hidden = norm_back(
        (after(late_own, *sent_x), late_other), (early_own, early_other), hidden, cotangent, pre_gain[None]
    )
    grad_hidden, common, products, other_both = after(
        (grad_hidden, common, products, other_both), *rx.got, common_came, products_came, other_both
    )
    common, products = common + common_came, products + products_came.astype(F32)
    dist = 8
    while dist < ring.n:
        common = common + ring.doubling(common, dist)
        dist *= 2
    dist = 4
    while dist < ring.n // 2:
        products, products_came = ring.halving(products, dist)
        products = products + products_came.astype(F32)
        dist *= 2

    keep_x, give_x = rx.finish(place, grad_hidden)
    other_x = ring.swap(give_x)
    products, products_came = ring.halving(after(products, keep_x), ring.n // 2)
    sum_small = products + products_came.astype(F32)
    common = after(common, keep_x)
    other = ring.swap(common)
    if n_t == 2:
        everyone = (
            lax.ppermute(common, "tensor", [(0, 1), (1, 0)]), lax.ppermute(common, ("dp", "tensor"), across)
        )
    else:
        everyone = (tensor_sum(common + other),)
    grad_zx, grad_dt, grad_bc, *sums = finals(
        place, keep_z, other_both, keep_x, other_x, sum_small, common, other, everyone, heads, padded, width
    )
    grad_out = in_order(keep_o, other_both[:chans], 0)
    taps, bias, taps_bc, bias_bc, grad_dt_bias, grad_a_log, grad_d_skip, grad_pre, grad_gate = sums
    return (
        output, grad_hidden, grad_zx, grad_dt, grad_bc, grad_out, taps, bias[0], taps_bc, bias_bc[0],
        grad_dt_bias[0], grad_a_log[0], grad_d_skip[0], grad_pre[0], grad_gate[0],
    )


def solution(mesh):
    in_specs = (
        P("dp", None), P("dp"), P("dp", None), P(None, "dp", "tensor"), P("dp", "tensor"), P("dp", None),
        P("tensor", "dp"), P(None, "tensor"), P("tensor"), P(), P(), P("tensor"), P("tensor"), P("tensor"),
        P(), P("tensor"),
    )
    out_specs = (
        P("dp", None), P("dp", None), P(None, "dp", "tensor"), P("dp", "tensor"), P("dp", "tensor"),
        P("tensor", "dp"), P(None, "tensor"), P("tensor"), P(), P(), P("tensor"), P("tensor"), P("tensor"),
        P(), P("tensor"),
    )
    return jax.shard_map(local, mesh=mesh, in_specs=in_specs, out_specs=out_specs, check_vma=False)
```

```python
import functools

import jax
import jax.numpy as jnp
from jax import lax
from jax.experimental import pallas as pl
from jax.experimental.pallas import tpu as pltpu
from jax.sharding import PartitionSpec as P

EPS = 1e-05
Q = 128
NEG = -1e30
F32 = jnp.float32
BF16 = jnp.bfloat16
HIGH = lax.Precision.HIGHEST
MIB = 1024 * 1024
HEAD = 64
STATE = 128


LONG = pl.CostEstimate(flops=30_000_000_000, bytes_accessed=1, transcendentals=0)
BRIEF = pl.CostEstimate(flops=1, bytes_accessed=1, transcendentals=0)


def dot(a, b, dims, precision=None):
    return lax.dot_general(a, b, (dims, ((), ())), precision=precision, preferred_element_type=F32)


def lane_sums(v):
    return dot(jnp.ones((8, v.shape[1]), F32), v, (((1,), (1,))), HIGH)


def params(mib):
    return pltpu.CompilerParams(vmem_limit_bytes=mib * MIB)


def after(value, *others):
    return lax.optimization_barrier((value, others))[0]


def ring_order(chips):
    if chips == 8:
        return [0, 2, 4, 6, 7, 5, 3, 1]
    half = chips // 2
    return list(range(half)) + list(range(chips - 1, half - 1, -1))


class Ring:
    def __init__(self, n_dp):
        self.n = n_dp // 2
        self.order = ring_order(self.n)
        place = [0] * self.n
        for position, chip in enumerate(self.order):
            place[chip] = position
        me = lax.axis_index("dp")
        self.core = me % 2
        self.mine = me // 2
        self.pos = jnp.asarray(place, jnp.int32)[self.mine]
        self.right = self.perm(1)
        self.left = self.perm(-1)
        self.full = self.n // 2 - 1

    def perm(self, step):
        pairs = []
        for p in range(self.n):
            for c in range(2):
                pairs.append((self.order[p] * 2 + c, self.order[(p + step) % self.n] * 2 + c))
        return pairs

    def table(self):
        table = [[self.order[(p + s) % self.n] for s in range(self.n)] for p in range(self.n)]
        row = lax.dynamic_index_in_dim(jnp.asarray(table, jnp.int32), self.pos, 0, keepdims=False)
        return jnp.concatenate([row, self.core.reshape(1).astype(jnp.int32)])

    def offsets(self, dd):
        steps = [0] + [-k for k in range(1, self.full + 1)] + list(range(1, self.full + 1)) + [self.n // 2]
        table = [[self.order[(p + s) % self.n] * dd for s in steps] for p in range(self.n)]
        return lax.dynamic_index_in_dim(jnp.asarray(table, jnp.int32), self.pos, 0, keepdims=False)

    def go_right(self, v):
        return lax.ppermute(v, "dp", self.right)

    def go_left(self, v):
        return lax.ppermute(v, "dp", self.left)

    def swap(self, v):
        return lax.ppermute(v, "dp", [(i, i ^ 1) for i in range(2 * self.n)])

    def halving(self, v, dist):
        pairs = [(i, i ^ (2 * dist)) for i in range(2 * self.n)]
        keep, give = self.halves(v, (self.mine // dist) % 2)
        return keep, lax.ppermute(give.astype(BF16), "dp", pairs)

    def doubling(self, v, dist):
        return lax.ppermute(v, "dp", [(i, i ^ (2 * dist)) for i in range(2 * self.n)])

    def halves(self, v, bit):
        size = v.shape[1] // 2
        return (
            lax.dynamic_slice_in_dim(v, bit * size, size, 1),
            lax.dynamic_slice_in_dim(v, (1 - bit) * size, size, 1),
        )


class Gather:
    def __init__(self, ring, unit, far, cut=None):
        self.ring, self.far, self.cut = ring, far, cut
        self.r, self.l = [unit], [unit]
        self.last = []

    def right(self, *others):
        if len(self.r) <= self.ring.full:
            v = after(self.r[-1], *others) if others else self.r[-1]
            self.r.append(self.ring.go_right(v))
        return self.r[-1]

    def left(self, *others):
        if len(self.l) <= self.ring.full:
            v = after(self.l[-1], *others) if others else self.l[-1]
            self.l.append(self.ring.go_left(v))
        return self.l[-1]

    def step(self, *others):
        return self.right(*others), self.left(*others)

    def newest(self):
        return self.r[-1], self.l[-1]

    def finish(self, *others):
        while len(self.r) <= self.ring.full:
            self.right()
        while len(self.l) <= self.ring.full:
            self.left()
        r, l, cut = self.r[-1], self.l[-1], self.cut
        if others:
            r, l = after(r, *others), after(l, *others)
        if self.far == "both":
            self.last = [self.ring.go_right(r[:cut]), self.ring.go_left(l[cut:])]
        elif self.far == "right":
            self.last = [self.ring.go_right(r)]
        else:
            self.last = [self.ring.go_left(l)]
        return self.last

    def blocks(self):
        return self.r + self.l[1:] + self.last


def both_parts(vt, own, other):
    half = own.shape[0]
    return dot(vt[:, :half], own[...], (((1,), (0,)))) + dot(vt[:, half:], other[...], (((1,), (0,))))


def terms_kernel(table, vt, own, other, *outs):
    total = both_parts(vt, own, other).astype(BF16)
    top, bottom = outs[:2]
    half = top.shape[0]
    s = pl.program_id(0)

    @pl.when(s == 0)
    def _():
        top[...] = total[:half]
        bottom[...] = total[half:]

    for k, out in enumerate(outs[2:]):

        @pl.when((s == 1 + 2 * k) | (s == 2 + 2 * k))
        def _():
            out[0] = total


def terms(ring, table, vt, acts, dd):
    rows, tokens = vt.shape
    n, full = ring.n, ring.full
    half = n // 2

    def step(s):
        j = full - (s - 1) // 2
        at = jnp.where(s == 0, half, jnp.where(s % 2 == 1, j, n - j))
        return jnp.where(s == n - 1, 0, at)

    column = pl.BlockSpec((tokens // 2, dd), lambda s, t: (0, t[step(s)]))
    part = pl.BlockSpec((rows // 2, dd), lambda s, t: (0, 0))
    pair = lambda k: pl.BlockSpec((1, rows, dd), lambda s, t: (jnp.clip(s - 1 - 2 * k, 0, 1), 0, 0))
    single = pl.BlockSpec((1, rows, dd), lambda s, t: (0, 0, 0))
    return pl.pallas_call(
        terms_kernel,
        out_shape=tuple([jax.ShapeDtypeStruct((rows // 2, dd), BF16)] * 2)
        + tuple([jax.ShapeDtypeStruct((2, rows, dd), BF16)] * full)
        + (jax.ShapeDtypeStruct((1, rows, dd), BF16),),
        grid_spec=pltpu.PrefetchScalarGridSpec(
            num_scalar_prefetch=1,
            grid=(n,),
            in_specs=[pl.BlockSpec((rows, tokens), lambda s, t: (0, 0)), column, column],
            out_specs=tuple([part, part] + [pair(k) for k in range(full)] + [single]),
        ),
        compiler_params=params(24),
        cost_estimate=LONG,
    )(table, vt, *acts)


def first_add_kernel(own, r, l, out_r, out_l):
    half = r.shape[0]
    out_r[:half] = (own[0, :half].astype(F32) + r[...].astype(F32)).astype(BF16)
    out_r[half:] = own[0, half:]
    out_l[:half] = own[1, :half]
    out_l[half:] = (own[1, half:].astype(F32) + l[...].astype(F32)).astype(BF16)


def add_kernel(own, r, l, out_r, out_l):
    out_r[...] = (own[0].astype(F32) + r[...].astype(F32)).astype(BF16)
    out_l[...] = (own[1].astype(F32) + l[...].astype(F32)).astype(BF16)


def last_add_kernel(place, own, r, l, keep, give):
    total = own[0].astype(F32) + r[...].astype(F32) + l[...].astype(F32)
    dd = keep.shape[1]
    low, high = total[:, :dd], total[:, dd:]
    keep[...] = jnp.where(place[0] == 0, low, high)
    give[...] = jnp.where(place[0] == 0, high, low)


class Scatter:
    def __init__(self, ring, parts):
        self.ring = ring
        top, bottom, *self.own = parts
        self.left_to_do = ring.full
        self.send(top, bottom)

    def send(self, r, l):
        self.out = (r, l)
        self.got = (self.ring.go_right(r), self.ring.go_left(l))

    def step(self, *others):
        if not self.left_to_do:
            return self.out
        j = self.left_to_do
        self.left_to_do -= 1
        own = self.own[self.ring.full - j]
        rows, dd = own.shape[1:]
        got = after(self.got, *others) if others else self.got
        whole = lambda shape: pl.BlockSpec(shape, lambda i: (0,) * len(shape))
        out = pl.pallas_call(
            first_add_kernel if j == self.ring.full else add_kernel,
            grid=(1,),
            out_shape=(jax.ShapeDtypeStruct((rows, dd), BF16),) * 2,
            in_specs=[whole(v.shape) for v in (own, *got)],
            out_specs=(whole((rows, dd)),) * 2,
            compiler_params=params(16),
            cost_estimate=BRIEF,
        )(own, *got)
        self.send(*out)
        return self.out

    def finish(self, place, *others, cost=BRIEF):
        while self.left_to_do:
            self.step()
        own = self.own[-1]
        rows, dd = own.shape[1:]
        got = after(self.got, *others) if others else self.got
        whole = lambda shape: pl.BlockSpec(shape, lambda i, p: (0,) * len(shape))
        return pl.pallas_call(
            last_add_kernel,
            out_shape=(jax.ShapeDtypeStruct((rows, dd // 2), F32),) * 2,
            grid_spec=pltpu.PrefetchScalarGridSpec(
                num_scalar_prefetch=1,
                grid=(1,),
                in_specs=[whole(v.shape) for v in (own, *got)],
                out_specs=(whole((rows, dd // 2)),) * 2,
            ),
            compiler_params=params(16),
            cost_estimate=cost,
        )(place, own, *got)


def prep_x_kernel(place, own, other, small_own, small_other, out):
    core = place[0]
    dd = own.shape[1]
    chans = own.shape[2] // 2
    padded = out.shape[0] - chans - STATE
    for b in range(2):
        lanes = slice(b * dd, (b + 1) * dd)
        near = core == b
        src = jnp.where(near, own[0], other[0])
        src = jnp.where(core == 0, src[:, :chans], src[:, chans:])
        out[:chans, lanes] = src.T
        small = jnp.where(near, small_own[...], small_other[...])
        states = jnp.where(core == 0, small[:, :STATE], small[:, STATE : 2 * STATE])
        out[chans : chans + STATE, lanes] = states.T
        steps = jnp.where(core == 0, small[:, 2 * STATE : 3 * STATE], small[:, 3 * STATE :])
        out[chans + STATE :, lanes] = steps.T[:padded]


def prep_x(place, own, other, small_own, small_other, padded):
    _, dd, inner = own.shape
    rows = inner // 2 + STATE + padded
    return pl.pallas_call(
        prep_x_kernel,
        out_shape=jax.ShapeDtypeStruct((rows, 2 * dd), BF16),
        grid_spec=pltpu.PrefetchScalarGridSpec(
            num_scalar_prefetch=1,
            grid=(1,),
            in_specs=[pl.BlockSpec((1, dd, inner), lambda i, p: (1, 0, 0))] * 2
            + [pl.BlockSpec((dd, 4 * STATE), lambda i, p: (0, 0))] * 2,
            out_specs=pl.BlockSpec((rows, 2 * dd), lambda i, p: (0, 0)),
        ),
        compiler_params=params(12),
        cost_estimate=BRIEF,
    )(place, own, other, small_own, small_other)


def prep_zo_kernel(place, own, other, out_own, out_other, z, o):
    core = place[0]
    dd = own.shape[1]
    chans = own.shape[2] // 2
    for b in range(2):
        lanes = slice(b * dd, (b + 1) * dd)
        near = core == b
        src = jnp.where(near, own[0], other[0])
        src = jnp.where(core == 0, src[:, :chans], src[:, chans:])
        z[:, lanes] = src.T
        src = jnp.where(near, out_own[...], out_other[...])
        o[:, lanes] = jnp.where(core == 0, src[:chans], src[chans:])


def prep_zo(place, own, other, out_own, out_other):
    _, dd, inner = own.shape
    shape = (inner // 2, 2 * dd)
    return pl.pallas_call(
        prep_zo_kernel,
        out_shape=(jax.ShapeDtypeStruct(shape, BF16),) * 2,
        grid_spec=pltpu.PrefetchScalarGridSpec(
            num_scalar_prefetch=1,
            grid=(1,),
            in_specs=[pl.BlockSpec((1, dd, inner), lambda i, p: (0, 0, 0))] * 2
            + [pl.BlockSpec((inner, dd), lambda i, p: (0, 0))] * 2,
            out_specs=(pl.BlockSpec(shape, lambda i, p: (0, 0)),) * 2,
        ),
        compiler_params=params(12),
        cost_estimate=BRIEF,
    )(place, own, other, out_own, out_other)


class Weight:
    def __init__(self, blocks, first, rows, cut=None):
        self.args, self.specs, self.plan = [], [], []
        self.rows, self.dd = rows, blocks[0].shape[1]

        def view(array, start, size):
            index = start // size
            self.args.append(array)
            self.specs.append(pl.BlockSpec((size, self.dd), lambda i, o, index=index: (index, 0)))

        whole = blocks if cut is None else blocks[:-2]
        for block in whole:
            view(block, first, rows)
            self.plan.append(1)
        if cut is not None:
            pieces = 0
            if first < cut:
                view(blocks[-2], first, min(rows, cut - first))
                pieces += 1
            if first + rows > cut:
                start = max(first, cut)
                view(blocks[-1], start - cut, first + rows - start)
                pieces += 1
            self.plan.append(pieces)

    def read(self, refs):
        at, out = 0, []
        for pieces in self.plan:
            part = [r[...] for r in refs[at : at + pieces]]
            out.append(part[0] if pieces == 1 else jnp.concatenate(part, axis=0))
            at += pieces
        return out


def projected(weight, refs, act, offs):
    total = None
    for b, w in enumerate(weight.read(refs)):
        off = pl.multiple_of(offs[b], weight.dd)
        part = dot(w, act[:, pl.ds(off, weight.dd)], (((1,), (1,))))
        total = part if total is None else total + part
    return total


def projection(body, weight, acts, offs, extra, extra_specs, out_shape, out_specs, mib=40):
    tile, width = acts[0].shape
    tokens = 2 * tile
    n = len(weight.args)

    def kernel(offs, *refs):
        for k in range(2):

            @pl.when(pl.program_id(0) == k)
            def _():
                acc = projected(weight, refs[:n], refs[n + k], offs)
                body(acc, refs[n + 2 : n + 2 + len(extra)], refs[n + 2 + len(extra) :])

    return pl.pallas_call(
        kernel,
        out_shape=out_shape,
        grid_spec=pltpu.PrefetchScalarGridSpec(
            num_scalar_prefetch=1,
            grid=(tokens // tile,),
            in_specs=weight.specs + [pl.BlockSpec((tile, width), lambda i, o: (0, 0))] * 2 + extra_specs,
            out_specs=out_specs,
        ),
        compiler_params=params(mib),
        cost_estimate=LONG,
    )(offs, *weight.args, *acts, *extra)


def x_projection(weight, chans, acts, offs):
    tile = acts[0].shape[0]
    parts = (chans, STATE, weight.rows - chans - STATE)

    def body(acc, extra, outs):
        at = 0
        for out, rows in zip(outs, parts):
            out[...] = acc[at : at + rows]
            at += rows

    return projection(
        body, weight, acts, offs, (), [],
        tuple(jax.ShapeDtypeStruct((rows, 2 * tile), F32) for rows in parts),
        tuple(pl.BlockSpec((rows, tile), lambda i, o: (0, i)) for rows in parts),
    )


def sigmoid(v):
    return 0.5 * jnp.tanh(0.5 * v) + 0.5


def gate_projection(weight, acts, offs, y):
    rows, tokens = y.shape
    tile = tokens // 2

    def body(z, extra, outs):
        outs[0][...] = z
        g = extra[0][...] * (z * sigmoid(z))
        outs[1][...] = jnp.sum(g * g, axis=0, keepdims=True)

    wide = pl.BlockSpec((rows, tile), lambda i, o: (0, i))
    line = pl.BlockSpec((1, tile), lambda i, o: (0, i))
    return projection(
        body, weight, acts, offs, (y,), [wide],
        (jax.ShapeDtypeStruct((rows, tokens), F32), jax.ShapeDtypeStruct((1, tokens), F32)),
        (wide, line), 58,
    )


def back_projection(weight, acts, offs, y, z, gain):
    rows, tokens = y.shape
    tile = tokens // 2

    def body(dyn, extra, outs):
        y, z, gain = extra
        outs[0][...] = dyn
        zv = z[...]
        g = y[...] * (zv * sigmoid(zv))
        outs[1][...] = jnp.sum(dyn * gain[...] * g, axis=0, keepdims=True)

    wide = pl.BlockSpec((rows, tile), lambda i, o: (0, i))
    line = pl.BlockSpec((1, tile), lambda i, o: (0, i))
    return projection(
        body, weight, acts, offs, (y, z, gain),
        [wide, wide, pl.BlockSpec((rows, 1), lambda i, o: (0, 0))],
        (jax.ShapeDtypeStruct((rows, tokens), F32), jax.ShapeDtypeStruct((1, tokens), F32)),
        (wide, line),
    )


def back(groups, offs, width, parts=1, part=0, hiddens=None, states=None, mib=40):
    dd = groups[0][0].dd
    size = groups[0][1].shape[1] // (2 * parts)
    args, specs = [], []
    flops = 0
    for weight, vt in groups:
        args += weight.args + [vt, vt]
        specs += weight.specs
        specs += [pl.BlockSpec((vt.shape[0], size), lambda i, o, p=p: (0, p)) for p in (part, parts + part)]
    if states is not None:
        dbc, w_own, w_other, core = states
        args += [dbc, dbc, w_own, w_other]
        specs += [pl.BlockSpec((dbc.shape[0], size), lambda i, o, p=p: (0, p)) for p in (part, parts + part)]
        specs += [pl.BlockSpec(w_own.shape, lambda i, o: (0, 0))] * 2
        offs = jnp.concatenate([offs, core])
    out_spec = pl.BlockSpec((size, width), lambda i, o: (0, 0))
    shapes = [jax.ShapeDtypeStruct((size, width), BF16)] * 2
    out_specs = [out_spec, out_spec]
    if hiddens is not None:
        args += list(hiddens)
        specs += [pl.BlockSpec((size, width), lambda i, o: (part, 0))] * 2
        shapes.append(jax.ShapeDtypeStruct((1, width), F32))
        out_specs.append(pl.BlockSpec((1, width), lambda i, o: (0, 0)))

    def kernel(offs, *refs):
        outs = refs[len(args) :]
        at, terms = 0, []
        for weight, _ in groups:
            n = len(weight.args)
            v = jnp.concatenate([refs[at + n][...].T, refs[at + n + 1][...].T], axis=0)
            terms.append((v, weight.read(refs[at : at + n])))
            at += n + 2
        if states is not None:
            dbc = jnp.concatenate([refs[at][...], refs[at + 1][...]], axis=1)
            first = offs[offs.shape[0] - 1] == 0
            low, high = dbc[:STATE], dbc[STATE:]
            v_own, v_other = jnp.where(first, low, high).T, jnp.where(first, high, low).T
            w_own, w_other = refs[at + 2], refs[at + 3]
        scales = []
        if hiddens is not None:
            for h in refs[len(args) - 2 : len(args)]:
                v = h[...].astype(F32)
                scales.append(lax.rsqrt(jnp.mean(v * v, axis=1, keepdims=True) + EPS))
        for b in range(len(terms[0][1])):
            off = pl.multiple_of(offs[b], dd)
            along = None
            total = None
            for v, blocks in terms:
                term = dot(v, blocks[b], (((1,), (0,))))
                total = term if total is None else total + term
            if states is not None:
                total = total + dot(v_own, w_own[:, pl.ds(off, dd)], (((1,), (0,))))
                total = total + dot(v_other, w_other[:, pl.ds(off, dd)], (((1,), (0,))))
            for k in range(2):
                here = total[k * size : (k + 1) * size]
                outs[k][:, pl.ds(off, dd)] = here.astype(BF16)
                if hiddens is not None:
                    h = refs[len(args) - 2 + k][:, pl.ds(off, dd)].astype(F32)
                    line = jnp.sum(here * (h * scales[k]), axis=0, keepdims=True)
                    along = line if along is None else along + line
            if hiddens is not None:
                outs[2][:, pl.ds(off, dd)] = along

    return pl.pallas_call(
        kernel,
        out_shape=tuple(shapes),
        grid_spec=pltpu.PrefetchScalarGridSpec(
            num_scalar_prefetch=1, grid=(1,), in_specs=specs, out_specs=tuple(out_specs)
        ),
        compiler_params=params(mib),
        cost_estimate=LONG,
    )(offs, *args)


def whole_rows(weight, offs, width):
    def kernel(offs, *refs):
        for b, w in enumerate(weight.read(refs[:-1])):
            refs[-1][:, pl.ds(pl.multiple_of(offs[b], weight.dd), weight.dd)] = w

    return pl.pallas_call(
        kernel,
        out_shape=jax.ShapeDtypeStruct((weight.rows, width), BF16),
        grid_spec=pltpu.PrefetchScalarGridSpec(
            num_scalar_prefetch=1,
            grid=(1,),
            in_specs=weight.specs,
            out_specs=pl.BlockSpec((weight.rows, width), lambda i, o: (0, 0)),
        ),
        compiler_params=params(20),
        cost_estimate=BRIEF,
    )(offs, *weight.args)


def gathered_sums_kernel(cg_a, cg_b, dgain, hg_a, hg_b, spots, pre_a, pre_b, out):
    wide = out.shape[1]
    padded = hg_a.shape[1]
    out[...] = jnp.zeros_like(out)
    row = lax.broadcasted_iota(jnp.int32, (8, 8), 0)
    lane = lax.broadcasted_iota(jnp.int32, (8, 8), 1)
    cg = dot((row == lane).astype(F32), cg_a[...] + cg_b[...], (((1,), (1,))), HIGH)
    out[0:5, :] = cg[0:5]
    out[5:6, : dgain.shape[1]] = dgain[0:1, :]
    for k in range(3):
        sums = dot(lane_sums(hg_a[k] + hg_b[k]), spots[k * padded : (k + 1) * padded, :], (((1,), (0,))), HIGH)
        out[6:7, k * 128 : (k + 1) * 128] = sums[0:1]
    pre = pre_a[...] + pre_b[...]
    width = pre.shape[1]
    for k in range(-(-width // wide)):
        size = min(wide, width - k * wide)
        out[7 + k : 8 + k, :size] = pre[:, k * wide : k * wide + size]


def gathered_sums(cg_a, cg_b, dgain, hg_a, hg_b, spots, *pre):
    wide = cg_a.shape[0]
    rows = -(-(7 + -(-pre[0].shape[1] // wide)) // 8) * 8
    args = (cg_a, cg_b, dgain, hg_a, hg_b, spots, *pre)
    whole = lambda shape: pl.BlockSpec(shape, lambda i: (0,) * len(shape))
    return pl.pallas_call(
        gathered_sums_kernel,
        out_shape=jax.ShapeDtypeStruct((rows, wide), F32),
        grid=(1,),
        in_specs=[whole(v.shape) for v in args],
        out_specs=whole((rows, wide)),
        compiler_params=params(16),
        cost_estimate=BRIEF,
    )(*args)


def finals_kernel(heads, padded, n_everyone, place, keep_z, other_z, keep_x, other_x, small, own, other, *refs):
    everyone = refs[0][...]
    for r in refs[1:n_everyone]:
        everyone = everyone + r[...]
    if n_everyone > 1:
        everyone = everyone + own[...] + other[...]
    zx, dt, bc, taps, bias, taps_bc, bias_bc, g_dt, g_a, g_d, pre, gate = refs[n_everyone:]
    first = place[0] == 0
    chans = keep_z.shape[0]
    for k, (a, b) in enumerate(((keep_z, other_z), (keep_x, other_x))):
        zx[k, :, :chans] = jnp.where(first, a[...], b[...]).T
        zx[k, :, chans:] = jnp.where(first, b[...], a[...]).T
    rows = bc.shape[1]
    turned = small[...].T
    bc[...] = turned[:, :rows]
    dt[:, :heads] = turned[:, rows : rows + heads]
    dt[:, heads:] = turned[:, rows + padded : rows + padded + heads]
    a, b = own[...], other[...]
    low, high = jnp.where(first, a, b)[:, :chans], jnp.where(first, b, a)[:, :chans]
    for out, at, size in ((taps, 0, 4), (bias, 4, 1), (gate, 5, 1)):
        out[:, :chans] = low[at : at + size]
        out[:, chans:] = high[at : at + size]
    taps_bc[...] = everyone[0:4, chans:]
    bias_bc[...] = everyone[4:5, chans:]
    both = a + b
    for k, out in enumerate((g_dt, g_a, g_d)):
        out[...] = both[6:7, k * 128 : k * 128 + 2 * heads]
    wide = both.shape[1]
    width = pre.shape[1]
    for k in range(-(-width // wide)):
        size = min(wide, width - k * wide)
        pre[:, k * wide : k * wide + size] = everyone[7 + k : 8 + k, :size]


def finals(place, keep_z, other_z, keep_x, other_x, small, own, other, everyone, heads, padded, width):
    chans, dd = keep_z.shape
    bc_rows = small.shape[0] - 2 * padded
    args = (keep_z, other_z, keep_x, other_x, small, own, other, *everyone)
    shapes = (
        (2, dd, 2 * chans), (dd, 2 * heads), (dd, bc_rows), (4, 2 * chans), (1, 2 * chans), (4, 2 * STATE),
        (1, 2 * STATE), (1, 2 * heads), (1, 2 * heads), (1, 2 * heads), (1, width), (1, 2 * chans),
    )
    whole = lambda shape: pl.BlockSpec(shape, lambda i, p: (0,) * len(shape))
    return pl.pallas_call(
        functools.partial(finals_kernel, heads, padded, len(everyone)),
        out_shape=tuple(jax.ShapeDtypeStruct(shape, F32) for shape in shapes),
        grid_spec=pltpu.PrefetchScalarGridSpec(
            num_scalar_prefetch=1,
            grid=(1,),
            in_specs=[
                pl.BlockSpec((chans, dd), lambda i, p: (1, 0)) if k == 1 else whole(v.shape)
                for k, v in enumerate(args)
            ],
            out_specs=tuple(whole(shape) for shape in shapes),
        ),
        compiler_params=params(24),
        cost_estimate=BRIEF,
    )(place, *args)


def reversed_bits(index, bits):
    return sum(((index >> k) & 1) << (bits - 1 - k) for k in range(bits))


def small_terms_kernel(shards, core_place, states, steps, own, other, keep, give):
    first = core_place[0] == 0
    both = both_parts(steps, own, other)
    total = jnp.concatenate(
        [dot(states[...], own[...], (((1,), (0,)))), jnp.where(first, both, 0.0), jnp.where(first, 0.0, both)]
    )
    chips = shards // 2
    lanes = own.shape[1] // shards
    bits = chips.bit_length() - 1
    for chip in range(chips):
        at = reversed_bits(chip, bits) * lanes
        low = total[:, 2 * chip * lanes : (2 * chip + 1) * lanes]
        high = total[:, (2 * chip + 1) * lanes : (2 * chip + 2) * lanes]
        keep[:, at : at + lanes] = jnp.where(first, low, high)
        give[:, at : at + lanes] = jnp.where(first, high, low).astype(BF16)


def small_terms(place, states, steps, acts, shards):
    m, k = states.shape[0], steps.shape[0]
    width = acts[0].shape[1]
    whole = lambda i, p: (0, 0)
    shape = (m + 2 * k, width // 2)
    return pl.pallas_call(
        functools.partial(small_terms_kernel, shards),
        out_shape=(jax.ShapeDtypeStruct(shape, F32), jax.ShapeDtypeStruct(shape, BF16)),
        grid_spec=pltpu.PrefetchScalarGridSpec(
            num_scalar_prefetch=1,
            grid=(1,),
            in_specs=[pl.BlockSpec(v.shape, whole) for v in (states, steps, *acts)],
            out_specs=(pl.BlockSpec(shape, whole),) * 2,
        ),
        compiler_params=params(20),
        cost_estimate=BRIEF,
    )(place, states, steps, *acts)


def output_kernel(late_own, late_came, own, came, hidden, out):
    late = pl.program_id(0) >= pl.num_programs(0) // 2
    rest = jnp.where(late, late_own[...].astype(F32), own[...].astype(F32))
    rest = rest + jnp.where(late, late_came[...].astype(F32), came[...].astype(F32))
    out[...] = (hidden[...].astype(F32) + rest).astype(BF16)


def residual(late, early, hidden):
    rows, width = hidden.shape
    tile = 128
    half = rows // tile // 2
    block = pl.BlockSpec((tile, width), lambda i: (i, 0))
    first = pl.BlockSpec((tile, width), lambda i: (jnp.minimum(i, half - 1), 0))
    second = pl.BlockSpec((tile, width), lambda i: (jnp.maximum(i - half, 0), 0))
    return pl.pallas_call(
        output_kernel,
        out_shape=jax.ShapeDtypeStruct(hidden.shape, BF16),
        grid=(rows // tile,),
        in_specs=[second, second, first, first, block],
        out_specs=block,
        compiler_params=params(20),
        cost_estimate=LONG,
    )(*late, *early, hidden)


def norm_back_kernel(late_own, late_came, own, came, hidden, cot, gain, out):
    h = hidden[...].astype(F32)
    width = h.shape[1]
    r = lax.rsqrt(jnp.mean(h * h, axis=1, keepdims=True) + EPS)
    late = pl.program_id(0) >= pl.num_programs(0) // 2
    dn = jnp.where(late, late_own[...].astype(F32), own[...].astype(F32))
    dn = dn + jnp.where(late, late_came[...].astype(F32), came[...].astype(F32))
    weighted = dn * gain[...]
    along = jnp.sum(weighted * h, axis=1, keepdims=True) * (1.0 / width)
    out[...] = (weighted * r - h * (r * r * r * along) + cot[...].astype(F32)).astype(BF16)


def norm_back(late, early, hidden, cot, gain):
    rows, width = hidden.shape
    tile = 128
    half = rows // tile // 2
    block = pl.BlockSpec((tile, width), lambda i: (i, 0))
    first = pl.BlockSpec((tile, width), lambda i: (jnp.minimum(i, half - 1), 0))
    second = pl.BlockSpec((tile, width), lambda i: (jnp.maximum(i - half, 0), 0))
    return pl.pallas_call(
        norm_back_kernel,
        out_shape=jax.ShapeDtypeStruct(hidden.shape, BF16),
        grid=(rows // tile,),
        in_specs=[second, second, first, first, block, block, pl.BlockSpec((1, width), lambda i: (0, 0))],
        out_specs=block,
        compiler_params=params(30),
        cost_estimate=LONG,
    )(*late, *early, hidden, cot, gain)


def gate_back_kernel(total, dyn, y, z, s, q, gain, dz, dy, dgain):
    zv, yv, sv = z[...], y[...], s[...]
    sig = sigmoid(zv)
    silu = zv * sig
    g = yv * silu
    scaled = dyn[...] * sv
    t = scaled * g
    lanes = t[:, :128]
    for k in range(128, t.shape[1], 128):
        lanes = lanes + t[:, k : k + 128]
    dgain[...] = lane_sums(lanes)
    dg = scaled * gain[...] - g * (sv * sv * sv * q[...] * (1.0 / total))
    dz[...] = (dg * yv * (sig * (1.0 + zv * (1.0 - sig)))).astype(BF16)
    dy[...] = (dg * silu).astype(BF16)


def gate_back(total, dyn, y, z, s, q, gain):
    rows, tokens = dyn.shape
    tile = max(rows // 4, 128)
    wide = pl.BlockSpec((tile, tokens), lambda i: (i, 0))
    line = pl.BlockSpec((1, tokens), lambda i: (0, 0))
    return pl.pallas_call(
        functools.partial(gate_back_kernel, float(total)),
        grid=(rows // tile,),
        out_shape=(jax.ShapeDtypeStruct((rows, tokens), BF16),) * 2
        + (jax.ShapeDtypeStruct((8, rows), F32),),
        in_specs=[wide, wide, wide, line, line, pl.BlockSpec((tile, 1), lambda i: (i, 0))],
        out_specs=(wide, wide, pl.BlockSpec((8, tile), lambda i: (0, i))),
        compiler_params=params(40),
        cost_estimate=BRIEF,
    )(dyn, y, z, s, q, gain)


def head_terms(raw, hp_ref):
    pre = raw + hp_ref[:, 0:1]
    small = jnp.exp(-jnp.abs(pre))
    one = 1.0 + small
    away = one - 1.0
    log1p = jnp.where(away == 0.0, small, jnp.log(one) * (small / jnp.where(away == 0.0, 1.0, away)))
    dt = jnp.maximum(pre, 0.0) + log1p
    logistic = jnp.where(pre >= 0.0, 1.0, small) / one
    rows = lax.broadcasted_iota(jnp.int32, (Q, Q), 0)
    lanes = lax.broadcasted_iota(jnp.int32, (Q, Q), 1)
    upto = (rows <= lanes).astype(F32)
    logs = dt * hp_ref[:, 1:2]
    cums = dot(logs, upto, (((1,), (0,))), HIGH)
    return dt, logistic, cums


def to_columns(cums):
    n = cums.shape[0]
    square = jnp.concatenate([cums, jnp.zeros((Q - n, Q), F32)], axis=0)
    return square.T


def pair_bias(segr_ref, segc_ref):
    rows = lax.broadcasted_iota(jnp.int32, (Q, Q), 0)
    lanes = lax.broadcasted_iota(jnp.int32, (Q, Q), 1)
    keep = (segc_ref[...] == segr_ref[...]) & (rows <= lanes)
    return jnp.where(keep, 0.0, NEG)


def state_rows(place, own, other, r0):
    at = r0 % STATE
    rows = slice(at, at + HEAD)
    return jnp.where(place[0] == r0 // STATE, own[rows, :], other[rows, :])


def fwd_kernel(
    heads, given, place, xr_ref, bco_ref, bcs_ref, dt_ref, mask_ref, segr_ref, segc_ref, par_ref, hp_ref, *rest
):
    y_ref, xa_ref, u_ref, s_ref, prev, state, parb, xt = rest[given:]
    chans = heads * HEAD
    wide = chans + 2 * STATE

    @pl.when(pl.program_id(0) == 0)
    def _():
        for k in range(6):
            parb[k] = jnp.broadcast_to(par_ref[:, k : k + 1], (wide, Q))
        prev[...] = jnp.zeros_like(prev)
        state[...] = jnp.zeros_like(state)

    lane = lax.broadcasted_iota(jnp.int32, (HEAD, Q), 1)
    m1, m2, m3 = mask_ref[0:1, :], mask_ref[1:2, :], mask_ref[2:3, :]

    def conv(r0):
        rows = slice(r0, r0 + HEAD)
        cur = xr_ref[rows, :] if r0 < chans else state_rows(place, bco_ref, bcs_ref, r0 - chans)
        old = prev[rows, :]
        u = parb[4, rows, :] + parb[3, rows, :] * cur
        u = u + parb[2, rows, :] * (m1 * pltpu.roll(jnp.where(lane >= Q - 1, old, cur), 1, 1))
        u = u + parb[1, rows, :] * (m2 * pltpu.roll(jnp.where(lane >= Q - 2, old, cur), 2, 1))
        u = u + parb[0, rows, :] * (m3 * pltpu.roll(jnp.where(lane >= Q - 3, old, cur), 3, 1))
        prev[rows, :] = cur
        u_ref[rows, :] = u
        xa = (u * (0.5 * jnp.tanh(0.5 * u) + 0.5)).astype(BF16)
        xa_ref[rows, :] = xa
        return xa

    for r0 in range(chans, wide, HEAD):
        conv(r0)
    bt = xa_ref[chans : chans + STATE, :]
    ct = xa_ref[chans + STATE : wide, :]
    mix = dot(bt.T, ct, (((1,), (0,))))
    dt, _, cums = head_terms(dt_ref[...], hp_ref)
    cols = to_columns(cums)
    bias = pair_bias(segr_ref, segc_ref)
    enter = jnp.exp(cums) * mask_ref[3:4, :]
    last = jnp.broadcast_to(cums[:, Q - 1 : Q], cums.shape)
    tail = jnp.exp(last - cums) * mask_ref[4:5, :]
    passing = jnp.exp(last) * mask_ref[5:6, :]
    s_in = state[...].astype(BF16)
    s_ref[...] = s_in
    carried = dot(s_in, ct, (((1,), (0,))))
    for h in range(heads):
        rows = slice(h * HEAD, (h + 1) * HEAD)
        xa = conv(h * HEAD).astype(F32)
        decay = jnp.exp(cums[h : h + 1, :] - cols[:, h : h + 1] + bias)
        mixing = (mix * decay).astype(BF16)
        xd = xa * dt[h : h + 1, :]
        xt[rows, :] = (xd * tail[h : h + 1, :]).astype(BF16)
        y = dot(xd.astype(BF16), mixing, (((1,), (0,))))
        y = y + enter[h : h + 1, :] * carried[rows, :] + parb[5, rows, :] * xa
        y_ref[rows, :] = y
    fresh = dot(xt[...], bt, (((1,), (1,))))
    for h in range(heads):
        rows = slice(h * HEAD, (h + 1) * HEAD)
        state[rows, :] = state[rows, :] * passing[h : h + 1, :] + fresh[rows, :]


def scan_forward(place, xr, bco, bcs, dtr, masks, segr, segc, par, hp, heads, seqs, seq, given=()):
    chans, tokens = xr.shape
    padded = dtr.shape[0]
    wide = chans + 2 * STATE
    count = tokens // seqs // Q
    at = lambda k, p: (0, seq * count + k)
    swapped = lambda k, p: (0, (seqs - 1 - seq) * count + k)
    whole = lambda k, p: (0, 0)
    args = (xr, bco, bcs, dtr, masks, segr, segc, par, hp)
    return pl.pallas_call(
        functools.partial(fwd_kernel, heads, len(given)),
        out_shape=(
            jax.ShapeDtypeStruct((chans, tokens), F32),
            jax.ShapeDtypeStruct((wide, tokens), BF16),
            jax.ShapeDtypeStruct((wide, tokens), F32),
            jax.ShapeDtypeStruct((chans, tokens), BF16),
        ),
        grid_spec=pltpu.PrefetchScalarGridSpec(
            num_scalar_prefetch=1,
            grid=(count,),
            in_specs=[
                pl.BlockSpec((chans, Q), at),
                pl.BlockSpec((STATE, Q), at),
                pl.BlockSpec((STATE, Q), swapped),
                pl.BlockSpec((padded, Q), at),
                pl.BlockSpec((8, Q), at),
                pl.BlockSpec((1, Q), at),
                pl.BlockSpec((Q, 1), lambda k, p: (seq * count + k, 0)),
                pl.BlockSpec(par.shape, whole),
                pl.BlockSpec(hp.shape, whole),
            ]
            + [pl.BlockSpec(memory_space=pl.ANY)] * len(given),
            out_specs=(
                pl.BlockSpec((chans, Q), at),
                pl.BlockSpec((wide, Q), at),
                pl.BlockSpec((wide, Q), at),
                pl.BlockSpec((chans, STATE), at),
            ),
            scratch_shapes=[
                pltpu.VMEM((wide, Q), F32),
                pltpu.VMEM((chans, STATE), F32),
                pltpu.VMEM((6, wide, Q), F32),
                pltpu.VMEM((chans, Q), BF16),
            ],
        ),
        input_output_aliases={1 + len(args) + k: k for k in range(len(given))},
        compiler_params=params(54),
        cost_estimate=LONG,
    )(place, *args, *given)


def bwd_kernel(
    heads, late, place, xr_ref, bco_ref, bcs_ref, dt_ref, mask_ref, segr_ref, segc_ref, par_ref, hp_ref, xa_ref,
    u_ref, s_ref, dy_ref, y_ref, *rest,
):
    if late:
        dx_ref, dbc_ref, ddt_ref, cgo_ref, hg_ref, dstate_out, after_out = rest[:7]
    else:
        dstate_in, after_in, next_ref = rest[:3]
        dx_ref, dbc_ref, ddt_ref, cgo_ref, hg_ref = rest[6:11]
    dstate, parb, after, nmask, xt, dye, cg_ref = rest[-7:]
    chans = heads * HEAD
    wide = chans + 2 * STATE
    seq, block = pl.program_id(0), pl.program_id(1)
    final = block == pl.num_programs(1) - 1

    @pl.when((seq == 0) & (block == 0))
    def _():
        for k in (0, 1, 2, 3, 5):
            parb[k] = jnp.broadcast_to(par_ref[:, k : k + 1], (wide, Q))
        cg_ref[...] = jnp.zeros_like(cg_ref)
        hg_ref[...] = jnp.zeros_like(hg_ref)

    @pl.when(block == 0)
    def _():
        if late:
            dstate[...] = jnp.zeros_like(dstate)
            after[...] = jnp.zeros_like(after)
            nmask[...] = jnp.zeros_like(nmask)
        else:
            dstate[...] = dstate_in[...]
            after[...] = after_in[...]
            nmask[...] = next_ref[...]

    lane = lax.broadcasted_iota(jnp.int32, (HEAD, Q), 1)
    lane8 = lax.broadcasted_iota(jnp.int32, (8, Q), 1)
    sub8 = lax.broadcasted_iota(jnp.int32, (8, Q), 0)
    masks = mask_ref[...]
    shifted_masks = jnp.where(lane8 <= sub8, nmask[...], masks)
    nmask[...] = masks

    def conv_back(r0, dxa, out, out0):
        rows = slice(r0, r0 + HEAD)
        u = u_ref[rows, :]
        sig = 0.5 * jnp.tanh(0.5 * u) + 0.5
        dc = dxa * (sig * (1.0 + u * (1.0 - sig)))
        xr = xr_ref[rows, :] if r0 < chans else state_rows(place, bco_ref, bcs_ref, r0 - chans)
        old = after[rows, :]
        after[rows, :] = dc
        dx = parb[3, rows, :] * dc
        cg_ref[4, rows, :] += dc
        cg_ref[3, rows, :] += xr * dc
        for k in (1, 2, 3):
            e = jnp.where(lane < k, old, dc) * shifted_masks[k - 1 : k, :]
            e = pltpu.roll(e, Q - k, 1)
            dx = dx + parb[3 - k, rows, :] * e
            cg_ref[3 - k, rows, :] += xr * e
        out[out0 : out0 + HEAD, :] = dx.astype(out.dtype)

    bt = xa_ref[chans : chans + STATE, :]
    ct = xa_ref[chans + STATE : wide, :]
    mix = dot(bt.T, ct, (((1,), (0,))))
    dt, logistic, cums = head_terms(dt_ref[...], hp_ref)
    cols = to_columns(cums)
    bias = pair_bias(segr_ref, segc_ref)
    enter = jnp.exp(cums) * masks[3:4, :]
    last = jnp.broadcast_to(cums[:, Q - 1 : Q], cums.shape)
    tail = jnp.exp(last - cums) * masks[4:5, :]
    passing = jnp.exp(last) * masks[5:6, :]
    ds = dstate[...].astype(BF16)
    spread = dot(ds, bt, (((1,), (0,))))
    dmix = jnp.zeros((Q, Q), F32)
    s_in = s_ref[...]
    direct, cross, skip, outward, through, inward = [], [], [], [], [], []
    for h in range(heads):
        rows = slice(h * HEAD, (h + 1) * HEAD)
        xa = xa_ref[rows, :].astype(F32)
        dyb = dy_ref[rows, :]
        dy = dyb.astype(F32)
        decay = jnp.exp(cums[h : h + 1, :] - cols[:, h : h + 1] + bias)
        mixing = (mix * decay).astype(BF16)
        xd = xa * dt[h : h + 1, :]
        xdb = xd.astype(BF16)
        xt[rows, :] = (xd * tail[h : h + 1, :]).astype(BF16)
        dye[rows, :] = (dy * enter[h : h + 1, :]).astype(BF16)
        dmix = dmix + dot(xdb, dyb, (((0,), (0,)))) * decay
        near = dot(dyb, mixing, (((1,), (1,))))
        far = tail[h : h + 1, :] * spread[rows, :]
        pull = near + far
        direct.append(jnp.sum(xa * pull, axis=0, keepdims=True))
        cross.append(jnp.sum(xdb.astype(F32) * near, axis=0, keepdims=True))
        outward.append(jnp.sum(xd * far, axis=0, keepdims=True))
        through.append(jnp.sum(dstate[rows, :] * s_in[rows, :].astype(F32), axis=0, keepdims=True))
        skip.append(jnp.sum(xa * dy, axis=0, keepdims=True))
        inward.append(jnp.sum(y_ref[rows, :] * dy, axis=0, keepdims=True))
        dxa = dt[h : h + 1, :] * pull + parb[5, rows, :] * dy
        conv_back(h * HEAD, dxa, dx_ref, h * HEAD)
    pad = ddt_ref.shape[0] - heads
    if pad:
        zero = [jnp.zeros((pad, Q), F32)]
        direct, cross, skip = direct + zero, cross + zero, skip + zero
        outward, through, inward = outward + zero, through + zero, inward + zero
    direct, cross, skip, outward, through, inward = (
        jnp.concatenate(v, axis=0) for v in (direct, cross, skip, outward, through, inward)
    )
    dlog = inward - hp_ref[:, 2:3] * skip - cross
    rows = lax.broadcasted_iota(jnp.int32, (Q, Q), 0)
    lanes = lax.broadcasted_iota(jnp.int32, (Q, Q), 1)
    dl = dot(dlog, (rows >= lanes).astype(F32), (((1,), (0,))), HIGH)
    dl = dl + dot(outward, (rows < lanes).astype(F32), (((1,), (0,))), HIGH)
    dl = dl + passing * jnp.sum(through, axis=1, keepdims=True)
    ddt = (direct + hp_ref[:, 1:2] * dl) * logistic
    ddt_ref[...] = ddt.astype(BF16)
    hg_ref[0] += ddt
    hg_ref[1] += dt * dl
    hg_ref[2] += skip
    dmixb = dmix.astype(BF16)
    xtv, dyev = xt[...], dye[...]
    dbt = dot(ct, dmixb, (((1,), (1,)))) + dot(ds, xtv, (((0,), (0,))))
    dct = dot(bt, dmixb, (((1,), (0,)))) + dot(s_ref[...], dyev, (((0,), (0,))))
    dbca = jnp.concatenate([dbt, dct], axis=0)
    for r0 in range(0, 2 * STATE, HEAD):
        conv_back(chans + r0, dbca[r0 : r0 + HEAD, :], dbc_ref, r0)
    fresh = dot(dyev, ct, (((1,), (1,))))
    for h in range(heads):
        rows = slice(h * HEAD, (h + 1) * HEAD)
        dstate[rows, :] = dstate[rows, :] * passing[h : h + 1, :] + fresh[rows, :]

    if late:

        @pl.when(final)
        def _():
            dstate_out[...] = dstate[...]
            after_out[...] = after[...]

    @pl.when((seq == pl.num_programs(0) - 1) & final)
    def _():
        for r0 in range(0, wide, HEAD):
            rows = slice(r0, r0 + HEAD)
            for k in range(5):
                cgo_ref[rows, k : k + 1] = jnp.sum(cg_ref[k, rows, :], axis=1, keepdims=True)


def scan_backward(
    place, xr, bco, bcs, dtr, masks, segr, segc, par, hp, xa, u, s_in, dy, y, heads, seqs, carry=(), given=()
):
    chans, tokens = xr.shape
    padded = dtr.shape[0]
    wide = chans + 2 * STATE
    count = tokens // seqs // Q
    late = not carry
    last = count - 1 if late else count // 2 - 1
    at = lambda s, k, p: (0, s * count + last - k)
    swapped = lambda s, k, p: (0, (seqs - 1 - s) * count + last - k)
    whole = lambda s, k, p: (0, 0)
    by_seq = lambda s, k, p: (s, 0)
    args = (xr, bco, bcs, dtr, masks, segr, segc, par, hp, xa, u, s_in, dy, y)
    if not late:
        args = (*args, *carry, masks)
    carried = [pl.BlockSpec((chans, STATE), by_seq), pl.BlockSpec((wide, Q), by_seq)]
    extra = [] if late else carried + [pl.BlockSpec((8, Q), lambda s, k, p: (0, s * count + count // 2))]
    shapes = (
        jax.ShapeDtypeStruct((chans, tokens), BF16),
        jax.ShapeDtypeStruct((2 * STATE, tokens), BF16),
        jax.ShapeDtypeStruct((padded, tokens), BF16),
        jax.ShapeDtypeStruct((wide, 8), F32),
        jax.ShapeDtypeStruct((3, padded, Q), F32),
    )
    if late:
        shapes += (
            jax.ShapeDtypeStruct((seqs * chans, STATE), F32),
            jax.ShapeDtypeStruct((seqs * wide, Q), F32),
        )
    return pl.pallas_call(
        functools.partial(bwd_kernel, heads, late),
        out_shape=shapes,
        grid_spec=pltpu.PrefetchScalarGridSpec(
            num_scalar_prefetch=1,
            grid=(seqs, count // 2),
            in_specs=[
                pl.BlockSpec((chans, Q), at),
                pl.BlockSpec((STATE, Q), at),
                pl.BlockSpec((STATE, Q), swapped),
                pl.BlockSpec((padded, Q), at),
                pl.BlockSpec((8, Q), at),
                pl.BlockSpec((1, Q), at),
                pl.BlockSpec((Q, 1), lambda s, k, p: (s * count + last - k, 0)),
                pl.BlockSpec(par.shape, whole),
                pl.BlockSpec(hp.shape, whole),
                pl.BlockSpec((wide, Q), at),
                pl.BlockSpec((wide, Q), at),
                pl.BlockSpec((chans, STATE), at),
                pl.BlockSpec((chans, Q), at),
                pl.BlockSpec((chans, Q), at),
            ]
            + extra
            + [pl.BlockSpec(memory_space=pl.ANY)] * len(given),
            out_specs=[
                pl.BlockSpec((chans, Q), at),
                pl.BlockSpec((2 * STATE, Q), at),
                pl.BlockSpec((padded, Q), at),
                pl.BlockSpec((wide, 8), whole),
                pl.BlockSpec((3, padded, Q), lambda s, k, p: (0, 0, 0)),
            ]
            + (carried if late else []),
            scratch_shapes=[
                pltpu.VMEM((chans, STATE), F32),
                pltpu.VMEM((6, wide, Q), F32),
                pltpu.VMEM((wide, Q), F32),
                pltpu.VMEM((8, Q), F32),
                pltpu.VMEM((chans, Q), BF16),
                pltpu.VMEM((chans, Q), BF16),
                pltpu.VMEM((5, wide, Q), F32),
            ],
        ),
        input_output_aliases={1 + len(args) + k: k for k in range(len(given))},
        compiler_params=params(54),
        cost_estimate=LONG,
    )(place, *args, *given)


def block_masks(segs, seqs):
    s = segs.reshape(seqs, -1)
    length = s.shape[1]
    rows = []
    for k in (1, 2, 3):
        old = jnp.pad(s, ((0, 0), (k, 0)), constant_values=-1)[:, :length]
        rows.append(old == s)
    b = s.reshape(seqs, length // Q, Q)
    ends = b[:, :, -1:]
    before = jnp.concatenate([jnp.full((seqs, 1, 1), -1, s.dtype), ends[:, :-1]], axis=1)
    rows += [b == before, b == ends, jnp.broadcast_to(ends == before, b.shape)]
    rows = [r.reshape(1, -1).astype(F32) for r in rows]
    return jnp.concatenate(rows + [jnp.zeros((2, segs.shape[0]), F32)], axis=0)


def local(
    hidden, segment_ids, cotangent, w_zx, w_dt, w_bc, w_out, conv_x, conv_bias_x, conv_bc, conv_bias_bc,
    dt_bias, a_log, d_skip, pre_gain, gate_gain,
):
    n_dp, n_t = lax.axis_size("dp"), lax.axis_size("tensor")
    t_index = lax.axis_index("tensor")
    ring = Ring(n_dp)
    core = ring.core
    mine, width = hidden.shape
    inner_here = w_zx.shape[2]
    chans = inner_here // 2
    heads = w_dt.shape[1] // 2
    padded = max(16, heads)
    wide = chans + 2 * STATE
    inner_all = inner_here * n_t
    dd = 2 * w_zx.shape[1]

    def tensor_sum(v):
        if n_t == 2:
            return v + lax.ppermute(v, "tensor", [(0, 1), (1, 0)])
        return lax.psum(v, "tensor")

    def over_tensor(v):
        if n_t == 2:
            return v.astype(F32) + lax.ppermute(v, "tensor", [(0, 1), (1, 0)]).astype(F32)
        return lax.psum(v.astype(F32), "tensor")

    def pick(v, which, axis=0):
        size = v.shape[axis] // 2
        return lax.dynamic_slice_in_dim(v, which * size, size, axis)

    def in_order(own, other, axis):
        return jnp.where(
            core == 0, jnp.concatenate([own, other], axis), jnp.concatenate([other, own], axis)
        )

    pad_dt = lambda v: jnp.pad(v, ((0, 0), (0, STATE - heads)))
    small = jnp.concatenate([w_bc, pad_dt(w_dt[:, :heads]), pad_dt(w_dt[:, heads:])], axis=1)
    zx_other = ring.swap(w_zx)
    small_other = ring.swap(small)
    place = core.reshape(1).astype(jnp.int32)
    ux = prep_x(place, w_zx, zx_other, small, small_other, padded)
    cut = chans // 2
    gx = Gather(ring, ux, "both", cut)
    gx.step()

    hiddens = [hidden, ring.swap(after(hidden, ux))]

    def norm(h):
        h = h.astype(F32)
        return (h * lax.rsqrt(jnp.mean(h * h, -1, keepdims=True) + EPS) * pre_gain).astype(BF16)

    normed = [norm(h) for h in hiddens]
    segs = jnp.concatenate([segment_ids, ring.swap(after(segment_ids, ux))])
    masks = block_masks(segs, 2)
    segr, segc = segs[None, :], segs[:, None]
    offs = ring.offsets(dd)
    table = ring.table()

    def own_chans(v):
        return pick(v, core, v.ndim - 1)

    taps = jnp.concatenate([own_chans(conv_x), conv_bc], axis=1)
    biases = jnp.concatenate([own_chans(conv_bias_x), conv_bias_bc])
    skips = jnp.repeat(own_chans(d_skip), HEAD)
    par = jnp.concatenate(
        [taps, biases[None], jnp.pad(skips, (0, 2 * STATE))[None], jnp.zeros((2, wide), F32)], axis=0
    ).T
    a_own = -jnp.exp(own_chans(a_log))
    spot = lax.broadcasted_iota(jnp.int32, (padded, 128), 1) - core * heads
    spot = (spot == lax.broadcasted_iota(jnp.int32, (padded, 128), 0)).astype(F32)
    spots = jnp.concatenate([spot, spot * jnp.pad(a_own, (0, padded - heads))[:, None], spot])
    hp = jnp.stack([own_chans(dt_bias), a_own, own_chans(d_skip)], axis=1)
    hp = jnp.pad(hp, ((0, padded - heads), (0, 5)))
    gain = own_chans(gate_gain)[:, None]

    out_other = ring.swap(after(w_out, ux))
    uz, uo = prep_zo(place, w_zx, zx_other, w_out, out_other)
    cots = [cotangent, ring.swap(after(cotangent, uz))]

    gx.step()
    gx.step()
    third = gx.newest()
    gx.finish()
    gz = Gather(ring, after(uz, *third), "right")
    came = gz.step()

    across = [(2 * i + t, 2 * (i ^ 1) + 1 - t) for i in range(n_dp) for t in range(2)]

    def wave(v):
        turned = jnp.concatenate([v[:, mine:], v[:, :mine]], axis=1)
        if n_t != 2:
            return tensor_sum(v + ring.swap(turned))
        return (
            v
            + ring.swap(turned)
            + lax.ppermute(v, "tensor", [(0, 1), (1, 0)])
            + lax.ppermute(turned, ("dp", "tensor"), across)
        )

    def tensor_other(v):
        if n_t == 2:
            return lax.ppermute(v, "tensor", [(0, 1), (1, 0)])
        return (lax.psum(v.astype(F32), "tensor") - v.astype(F32)).astype(BF16)

    def joined(own, came):
        return (own.astype(F32) + came.astype(F32)).astype(BF16)

    blocks = gx.blocks()
    gz.step(*gx.last)
    w_states = Weight(blocks, chans, STATE, cut)
    xr, bc_own, dtr = after(
        x_projection(
            Weight(blocks, 0, chans + STATE + padded, cut), chans, normed, after(offs, *came, *gx.last)
        ),
        *gz.newest(),
    )
    bc_other = ring.swap(bc_own)
    gz.step()
    scan_args = (bc_own, bc_other, dtr, masks, segr, segc, par, hp)
    half = after(scan_forward(place, xr, *scan_args, heads, 2, 0), *gz.newest())
    gz.finish(half[0])
    wb_own = whole_rows(w_states, after(offs, half[0]), width)
    wb_other = ring.swap(wb_own)
    go = Gather(ring, after(uo, half[0]), "left")
    go.left()
    y, xa, u, s_in = after(
        scan_forward(place, after(xr, wb_own), *scan_args, heads, 2, 1, half), *gz.last, go.l[-1], wb_other
    )
    go.step(y)
    z, squares = after(
        gate_projection(Weight(gz.blocks(), 0, chans), normed, after(offs, y), y), *go.newest()
    )
    go.step(squares)
    total_sq = wave(squares)
    s = lax.rsqrt(total_sq / inner_all + EPS)
    ynt = (y * (z * sigmoid(z)) * s * gain).astype(BF16)
    ynt = after(ynt, *go.newest())
    go.right()
    go.finish()
    ro = Scatter(ring, terms(ring, table, ynt, cots, dd))

    weight_o = Weight(go.blocks(), 0, chans)
    dyn, q = after(
        back_projection(weight_o, cots, after(offs, *ro.out), y, z, gain), *ro.got
    )
    sent_o = ro.step(q)
    q_total = wave(after(q, *sent_o))
    out_own, out_rest = after(back([(weight_o, ynt)], after(offs, *sent_o), width), *ro.got, q_total)
    sent_o = ro.step(out_own)
    out_came = ring.swap(out_rest)
    dzt, dyt, dgain = gate_back(inner_all, after(dyn, *sent_o), y, z, s, q_total, gain)
    parts_z = after(terms(ring, table, dzt, normed, dd), *ro.got, out_came)
    half = mine // 2
    sent_o = ro.step(parts_z[1])
    rz = Scatter(ring, after(parts_z, *sent_o))
    out_own, out_came = after((out_own, out_came), *sent_o)
    out_late = joined(out_own[half:], out_came[half:])
    out_early = joined(out_own[:half], out_came[:half])

    def dn_part(part, *others):
        return back(
            [
                (Weight(gz.blocks(), 0, chans), dzt),
                (Weight(blocks, 0, chans, cut), dxt),
                (Weight(blocks, chans + STATE, padded, cut), ddt_low),
            ],
            after(offs, *others), width, 2, part, hiddens,
            (dbc_low, wb_own, wb_other, place), 58,
        )

    scan_args = (*scan_args, xa, u, s_in)
    out_late_other = tensor_other(out_late)
    first = after(
        scan_backward(place, xr, *scan_args, after(dyt, *rz.out, out_late, out_early), y, heads, 2),
        *ro.got, *rz.got,
    )
    sent_z = rz.step(first[3])
    dxt, dbc_low, ddt_low = first[:3]
    out_early_other = tensor_other(after(out_early, *sent_z))
    late_own, late_rest, late_pre = after(dn_part(1, *sent_z), *rz.got, out_late_other)
    sent_z = rz.step(late_own)
    late_came = ring.swap(late_rest)
    second = after(
        scan_backward(place, xr, *scan_args, after(dyt, *sent_z), y, heads, 2, first[5:], first[:3]),
        *rz.got, out_early_other, late_came,
    )
    dxt, dbc_low, ddt_low = second[:3]
    sent_z = rz.step(ddt_low)
    dbc_came = ring.swap(after(dbc_low, *sent_z)[:, mine:])
    late_own = joined(late_own, after(late_came, *sent_z))
    late_other = tensor_other(late_own)
    parts_x = after(terms(ring, table, after(dxt, *sent_z, late_own), normed, dd), *rz.got, dbc_came)
    rx = Scatter(ring, parts_x)
    dbc_own = joined(dbc_low[:, :mine], after(dbc_came, *parts_x))
    dbc_other = tensor_other(dbc_own)
    early_own, early_rest, early_pre = after(
        dn_part(0, *rx.out, dbc_own), *rx.got, late_other, dbc_other
    )

    sent_x = rx.step(early_own)
    early_came = ring.swap(early_rest)
    early_own = joined(after(early_own, *sent_x), early_came)
    early_other = tensor_other(early_own)
    dbc_own = joined(dbc_own, after(dbc_other, early_own))
    bc_cols = 2 * STATE // n_t
    states = lax.dynamic_slice_in_dim(dbc_own, t_index * bc_cols, bc_cols, 0)
    products, give = small_terms(place, states, ddt_low, normed, n_dp)
    products_came = ring.swap(give)
    common = gathered_sums(
        first[3], second[3], dgain, first[4], after(second[4], products), spots, early_pre, late_pre
    )
    common_came = ring.doubling(common, 1)
    keep_o, give_o = ro.finish(place, common)
    keep_z, give_z = rz.finish(place, keep_o)
    give_both = jnp.concatenate([give_o, give_z])
    products, give_both = after((products, give_both), *rx.got, products_came, common_came)
    common, products = common + common_came, products + products_came.astype(F32)

    sent_x = rx.step(give_both)
    common_came = ring.doubling(after(common, *sent_x), 2)
    products, products_came = ring.halving(after(products, *sent_x), 1)
    output = residual(
        (out_late, out_late_other), (out_early, out_early_other), after(hidden, *sent_x)
    )
    output, common, products = after(
        (output, common, products), *rx.got, common_came, products_came, early_other
    )
    common, products = common + common_came, products + products_came.astype(F32)

    sent_x = rx.step(output)
    common_came = ring.doubling(after(common, *sent_x), 4)
    products, products_came = ring.halving(after(products, *sent_x), 2)
    other_both = ring.swap(after(give_both, *sent_x))
    grad_hidden = norm_back(
        (after(late_own, *sent_x), late_other), (early_own, early_other), hidden, cotangent, pre_gain[None]
    )
    grad_hidden, common, products, other_both = after(
        (grad_hidden, common, products, other_both), *rx.got, common_came, products_came, other_both
    )
    common, products = common + common_came, products + products_came.astype(F32)
    dist = 8
    while dist < ring.n:
        common = common + ring.doubling(common, dist)
        dist *= 2
    dist = 4
    while dist < ring.n // 2:
        products, products_came = ring.halving(products, dist)
        products = products + products_came.astype(F32)
        dist *= 2

    keep_x, give_x = rx.finish(place, grad_hidden)
    other_x = ring.swap(give_x)
    products, products_came = ring.halving(after(products, keep_x), ring.n // 2)
    sum_small = products + products_came.astype(F32)
    common = after(common, keep_x)
    other = ring.swap(common)
    if n_t == 2:
        everyone = (
            lax.ppermute(common, "tensor", [(0, 1), (1, 0)]), lax.ppermute(common, ("dp", "tensor"), across)
        )
    else:
        everyone = (tensor_sum(common + other),)
    grad_zx, grad_dt, grad_bc, *sums = finals(
        place, keep_z, other_both, keep_x, other_x, sum_small, common, other, everyone, heads, padded, width
    )
    grad_out = in_order(keep_o, other_both[:chans], 0)
    taps, bias, taps_bc, bias_bc, grad_dt_bias, grad_a_log, grad_d_skip, grad_pre, grad_gate = sums
    return (
        output, grad_hidden, grad_zx, grad_dt, grad_bc, grad_out, taps, bias[0], taps_bc, bias_bc[0],
        grad_dt_bias[0], grad_a_log[0], grad_d_skip[0], grad_pre[0], grad_gate[0],
    )


def solution(mesh):
    in_specs = (
        P("dp", None), P("dp"), P("dp", None), P(None, "dp", "tensor"), P("dp", "tensor"), P("dp", None),
        P("tensor", "dp"), P(None, "tensor"), P("tensor"), P(), P(), P("tensor"), P("tensor"), P("tensor"),
        P(), P("tensor"),
    )
    out_specs = (
        P("dp", None), P("dp", None), P(None, "dp", "tensor"), P("dp", "tensor"), P("dp", "tensor"),
        P("tensor", "dp"), P(None, "tensor"), P("tensor"), P(), P(), P("tensor"), P("tensor"), P("tensor"),
        P(), P("tensor"),
    )
    return jax.shard_map(local, mesh=mesh, in_specs=in_specs, out_specs=out_specs, check_vma=False)
```
